512 devices in a mesh: dp: 16 (over z, core), sketch: 32 (over x, y).
Axes of the slice: x: 4, y: 8, z: 8, core: 2. Of those that a mesh axis runs over, the one named last changes fastest.
Arguments:
- samples: bfloat16 [16384, 512], P('dp'), may hold values from -6 to 6
- projections: bfloat16 [4, 512, 16384], P(None, 'dp', 'sketch'), may hold values from -0.25 to 0.25
- targets: bfloat16 [16384, 64], P('dp'), may hold values from -6 to 6
- feature_scale: float32 [16384], P('sketch'), may hold values from 0.1 to 1.5
- coarse_factor: bfloat16 [1024, 1024], replicated, may hold values from -1 to 3, as said below
Outputs:
- solution: float32 [16384, 64], P('sketch')
- residual: float32 [16384, 64], P('sketch')
The draws below stay inside these ranges and needn't reach their ends.
Inputs may be any that keep to these rules, and one draw needn't show every extreme that they name: `coarse_factor`: lower triangular; its diagonal entries lie between 2 and 3.
All inputs are finite; a program needn't handle non-finite values.
Results may differ from the reference program's by a relative error of at most 0.0075.
The reference program's roundings to bfloat16 on the way (of `features`) count: a program that leaves them out, or rounds other values in their place, can miss the bound.
Values may be sent and summed in bfloat16 or wider, within the bound.
No kernel may reach another device: no remote copies, remote signals or barrier semaphores. Data moves between devices by JAX's collectives and lax.ppermute only.
A program may use at most 64 MiB of HBM per device.

```python
import math
import jax
import jax.numpy as jnp
from jax import lax

D = 512
F = 16384
K = 1024
R = 64
N_DEV = 1024
ITERS = 2
SAMPLES = 16384
N_DP = 16


def draw_coarse_factor(key, part):
    key = jax.random.fold_in(key, 7)
    key_off, key_diag = jax.random.split(key)
    off = jax.random.normal(key_off, (K, K), jnp.float32) * (0.5 / K ** 0.5)
    diag = jax.random.uniform(key_diag, (K,), jnp.float32, 2.0, 3.0)
    rows = jnp.arange(K, dtype=jnp.int32)[:, None]
    cols = jnp.arange(K, dtype=jnp.int32)[None, :]
    lower = jnp.where(rows > cols, off, 0.0) + jnp.where(rows == cols, diag[:, None], 0.0)
    return lower.astype(jnp.bfloat16)


def block_scale(rng, shape, cuts, low, largest):
    level, own = 1.0, jax.random.fold_in(rng, 6)
    for axis_at, blocks in cuts:
        steps = jnp.exp(jax.random.uniform(jax.random.fold_in(own, axis_at), (blocks,), jnp.float32, low / len(cuts), largest / len(cuts)))
        level = level * jnp.repeat(steps, shape[axis_at] // blocks).reshape([-1 if axis == axis_at else 1 for axis in range(len(shape))])
    return level


def noise(own_key, dims, scale, most, cuts=(), kind=jnp.bfloat16):
    entries = jax.random.normal(own_key, dims, jnp.float32) * scale
    if len(cuts) > 0:
        entries = block_scale(own_key, dims, cuts, -0.22, 0.18) * entries
    return jnp.clip(entries, min=-most, max=most).astype(kind)


def setup_inputs(seed: int = 0) -> dict:
    splits = jax.random.split(jax.random.key(seed), 6)
    return {
        "samples": noise(splits[0], (SAMPLES, D), 1.0, 6.0, ((0, 16),)),
        "projections": noise(splits[1], (4, D, F), D ** -0.5, 0.25, ((1, 16), (2, 32))),
        "targets": noise(splits[2], (SAMPLES, R), 1.0, 6.0, ((0, 16),)),
        "feature_scale": jnp.clip(jnp.exp(math.log(1.5) - 2.7080502 * jax.random.uniform(splits[3], (F,), jnp.float32) ** block_scale(splits[3], (F,), ((0, 32),), -0.2, 0.2)), 0.1, 1.5),
        "coarse_factor": draw_coarse_factor(jax.random.fold_in(splits[5], 71), 0),
    }


RIDGE = 0.5

def solve_coarse(lower, restricted):
    forward = lax.linalg.triangular_solve(lower, restricted, left_side=True, lower=True)
    return lax.linalg.triangular_solve(lower, forward, left_side=True, lower=True, transpose_a=True)

def reference(samples, projections, targets, feature_scale, coarse_factor):

    def panel(block):
        outs = [jnp.dot(block.astype(jnp.float32), projections[j].astype(jnp.float32), preferred_element_type=jnp.float32) for j in range(4)]
        return (outs[0] * outs[1] * outs[2] * outs[3] * (1.0 / math.sqrt(F))).astype(jnp.bfloat16)
    features = lax.map(panel, samples.reshape(N_DP, N_DEV, D)).reshape(SAMPLES, F)
    lower = coarse_factor.astype(jnp.float32)
    group = jnp.arange(F, dtype=jnp.int32) % K
    onehot = (jnp.arange(K, dtype=jnp.int32)[:, None] == group[None, :]).astype(jnp.float32) * (1.0 / math.sqrt(F // K))
    contract = (((0,), (0,)), ((), ()))

    def backward(values):
        return lax.dot_general(features.astype(jnp.float32), values.astype(jnp.float32), contract, preferred_element_type=jnp.float32)

    def operate(direction):
        sums = jnp.dot(features.astype(jnp.float32), direction.astype(jnp.bfloat16).astype(jnp.float32), preferred_element_type=jnp.float32).astype(jnp.bfloat16)
        return backward(sums) + RIDGE * direction

    def precondition(resid):
        restricted = jnp.dot(onehot, resid, precision=lax.Precision.HIGHEST)
        solved = solve_coarse(lower, restricted)
        fine = feature_scale[:, None] * resid + lax.dot_general(onehot, solved, contract, precision=lax.Precision.HIGHEST)
        return (fine, lax.optimization_barrier(jnp.sum(resid * fine, 0)))
    rhs = backward(targets)
    solution = jnp.zeros_like(rhs)
    resid = rhs
    fine, product = precondition(resid)
    direction = fine
    for step in range(ITERS):
        image = operate(direction)
        alpha = product / lax.optimization_barrier(jnp.sum(direction * image, 0))
        solution = solution + alpha * direction
        resid = resid - alpha * image
        if step + 1 < ITERS:
            fine, fresh = precondition(resid)
            direction = fine + fresh / product * direction
            product = fresh
    return (solution, resid)
```

```python
import functools
import math

import jax
import jax.numpy as jnp
from jax import lax
from jax.experimental import pallas as pl
from jax.experimental.pallas import tpu as pltpu
from jax.sharding import PartitionSpec as P

F = 16384
K = 1024
ITERS = 2
RIDGE = 0.5

f32 = jnp.float32
bf16 = jnp.bfloat16


def split(value):
    high = value.astype(bf16)
    return high, (value - high.astype(f32)).astype(bf16)


def dot(a, b):
    return lax.dot_general(a, b, (((1,), (0,)), ((), ())), preferred_element_type=f32)


def dot3(a, b):
    ah, al = split(a)
    bh, bl = split(b)
    return dot(ah, bh) + (dot(ah, bl) + dot(al, bh))


def dot2_left(a, exact):
    ah, al = split(a)
    return dot(ah, exact) + dot(al, exact)


def dot2_right(exact, b):
    bh, bl = split(b)
    return dot(exact, bh) + dot(exact, bl)


BLOCK = 256


def inverse_kernel(lower_ref, high_ref, low_ref, inv):
    n = lower_ref.shape[0]
    blocks = n // BLOCK
    rows = lax.broadcasted_iota(jnp.int32, (BLOCK, BLOCK), 0)
    cols = lax.broadcasted_iota(jnp.int32, (BLOCK, BLOCK), 1)
    spans = [pl.ds(b * BLOCK, BLOCK) for b in range(blocks)]
    inv[...] = jnp.zeros_like(inv)
    for span in spans:
        block = lower_ref[span, span].astype(f32)
        diag = jnp.sum(jnp.where(rows == cols, block, 0.0), axis=1, keepdims=True)
        inv[span, span] = jnp.where(rows == cols, 1.0 / diag, 0.0)

    def level(k, carry):
        below = ((rows >> k) == (cols >> k) + 1) & ((rows >> (k + 1)) == (cols >> (k + 1)))
        for span in spans:
            x = inv[span, span]
            off = jnp.where(below, lower_ref[span, span].astype(f32), 0.0).astype(bf16)
            inv[span, span] = x - dot3(dot2_left(x, off), x)
        return carry

    lax.fori_loop(0, int(math.log2(BLOCK)), level, 0)
    size = BLOCK
    while size < n:
        for at in range(0, n, 2 * size):
            top, bottom = pl.ds(at, size), pl.ds(at + size, size)
            a, b = inv[top, top], inv[bottom, bottom]
            inv[bottom, top] = -dot3(b, dot2_right(lower_ref[bottom, top], a))
        size *= 2
    xh, xl = split(inv[...])
    xht, xlt = split(inv[...].T)
    for span in spans:
        m = dot(xht, xh[:, span.start : span.start + BLOCK]) + (
            dot(xht, xl[:, span.start : span.start + BLOCK])
            + dot(xlt, xh[:, span.start : span.start + BLOCK])
        )
        high_ref[:, span], low_ref[:, span] = split(m)


def coarse_inverse(lower):
    n = lower.shape[0]
    return pl.pallas_call(
        inverse_kernel,
        out_shape=[jax.ShapeDtypeStruct((n, n), bf16)] * 2,
        in_specs=[pl.BlockSpec(memory_space=pltpu.VMEM)],
        out_specs=[pl.BlockSpec(memory_space=pltpu.VMEM)] * 2,
        scratch_shapes=[pltpu.VMEM((n, n), f32)],
        compiler_params=pltpu.CompilerParams(vmem_limit_bytes=48 * 1024 * 1024),
        cost_estimate=pl.CostEstimate(flops=20 * 10**9, bytes_accessed=6 * 2**20, transcendentals=0),
    )(lower)


ROWS = 256


def feature_kernel(samples_ref, proj_ref, targets_ref, feat_ref, part_ref):
    n, parts = samples_ref.shape[0], part_ref.shape[0]
    total = None
    for at in range(0, n, ROWS):
        block = samples_ref[at : at + ROWS, :]
        acc = dot(block, proj_ref[0])
        for j in range(1, proj_ref.shape[0]):
            acc = acc * dot(block, proj_ref[j])
        feat = (acc * (1.0 / math.sqrt(F))).astype(bf16)
        feat_ref[at : at + ROWS, :] = feat
        term = dot(targets_ref[:, at : at + ROWS], feat)
        total = term if total is None else total + term
    step = total.shape[0] // parts
    for p in range(parts):
        part_ref[p] = total[p * step : (p + 1) * step, :]


def make_features(samples, proj, targets_t, parts):
    n, width = samples.shape[0], proj.shape[2]
    vmem = pl.BlockSpec(memory_space=pltpu.VMEM)
    return pl.pallas_call(
        feature_kernel,
        out_shape=[
            jax.ShapeDtypeStruct((n, width), bf16),
            jax.ShapeDtypeStruct((parts, targets_t.shape[0] // parts, width), f32),
        ],
        in_specs=[vmem] * 3,
        out_specs=[vmem] * 2,
        compiler_params=pltpu.CompilerParams(vmem_limit_bytes=48 * 1024 * 1024),
        cost_estimate=pl.CostEstimate(flops=2 * 10**9, bytes_accessed=5 * 2**20, transcendentals=0),
    )(samples, proj, targets_t)


def triple(value):
    high = value.astype(bf16)
    rest = value - high.astype(f32)
    mid = rest.astype(bf16)
    return jnp.stack([high, mid, (rest - mid.astype(f32)).astype(bf16)], -1)


def body(samples, projections, targets, feature_scale, coarse_factor):
    n_dp, n_sk = lax.axis_size("dp"), lax.axis_size("sketch")
    count = projections.shape[2]
    width = targets.shape[1]
    mine = width // n_dp
    cols = width // n_sk
    groups = F // K
    factor = 1.0 / math.sqrt(groups)
    halves = K // count
    parity = lax.axis_index("sketch") % halves
    n = samples.shape[0]
    scale = feature_scale[None, :]

    proj = lax.all_gather(projections, "dp", axis=1, tiled=True)
    inv_high, inv_low = coarse_inverse(coarse_factor)
    feat, part = make_features(samples, proj, targets.T, n_dp)

    def scatter_dp(value):
        got = lax.all_to_all(value, "dp", 0, 0)
        return jnp.sum(got, 0)

    def gather_dp(value):
        return lax.all_to_all(jnp.broadcast_to(value[None], (n_dp,) + value.shape), "dp", 0, 0)

    def gather_sk(value):
        return lax.all_to_all(jnp.broadcast_to(value[None], (n_sk,) + value.shape), "sketch", 0, 0)

    def everywhere(value, dots):
        k = dots.shape[1]
        extra = jnp.pad(triple(dots).reshape(mine, 3 * k), ((0, 0), (0, 128 - 3 * k)))
        got = gather_sk(jnp.concatenate([value.astype(bf16), extra], 1)).astype(f32)
        sums = jnp.sum(jnp.sum(got[:, :, count : count + 3 * k], 0).reshape(mine, k, 3), -1)
        rho = jnp.sum(got[:, :, :count].reshape(n_sk // halves, halves, mine, count), 0) * factor
        return jnp.concatenate([rho[h] for h in range(halves)], 1), sums

    def coarse(rho):
        high, low = split(rho)
        both = dot(jnp.concatenate([high, low], 0), inv_high)
        return both[:mine] + (both[mine:] + dot(high, inv_low))

    def own(solved):
        return lax.dynamic_slice_in_dim(solved, parity * count, count, 1) * factor

    def forward(direction):
        got = gather_dp(direction.astype(bf16)).reshape(width, count)
        sums = lax.dot_general(got, feat, (((1,), (1,)), ((), ())), preferred_element_type=f32)
        return sums.reshape(n_sk, cols, n)

    def backward(sums):
        u = jnp.sum(lax.all_to_all(sums, "sketch", 0, 0), 0).astype(bf16)
        whole = gather_sk(u).reshape(width, n)
        return dot(whole, feat).reshape(n_dp, mine, count)

    def row_sum(value):
        return jnp.sum(value, 1, keepdims=True)

    resid = scatter_dp(part)
    rho, dots = everywhere(resid, row_sum(scale * resid * resid))
    energy = dots
    solved = coarse(rho)
    product = energy + row_sum(rho * solved)
    direction = scale * resid + own(solved)
    answer = jnp.zeros_like(resid)
    for step in range(ITERS):
        image = scatter_dp(backward(forward(direction))) + RIDGE * direction
        if step + 1 < ITERS:
            weighted = scale * image
            rho_image, dots = everywhere(
                image,
                jnp.concatenate(
                    [row_sum(direction * image), row_sum(weighted * resid), row_sum(weighted * image)], 1
                ),
            )
            alpha = product / dots[:, 0:1]
        else:
            extra = jnp.pad(row_sum(direction * image), ((0, 0), (0, 127)))
            alpha = product / jnp.sum(gather_sk(extra), 0)[:, 0:1]
        answer = answer + alpha * direction
        resid = resid - alpha * image
        if step + 1 < ITERS:
            rho = rho - alpha * rho_image
            energy = energy - alpha * (2.0 * dots[:, 1:2] - alpha * dots[:, 2:3])
            solved = coarse(rho)
            fresh = energy + row_sum(rho * solved)
            direction = scale * resid + own(solved) + fresh / product * direction
            product = fresh
    got = gather_dp(jnp.stack([answer, resid]))
    out = jnp.swapaxes(got, 0, 1).reshape(2, width, count)
    return out[0].T, out[1].T


def solution(mesh):
    placed = (P("dp", None), P(None, "dp", "sketch"), P("dp", None), P("sketch"), P())
    return jax.shard_map(
        body,
        mesh=mesh,
        in_specs=placed,
        out_specs=(P("sketch", None), P("sketch", None)),
        check_vma=False,
    )
```

```python
import functools
import math

import jax
import jax.numpy as jnp
from jax import lax
from jax.experimental import pallas as pl
from jax.experimental.pallas import tpu as pltpu
from jax.sharding import PartitionSpec as P

F = 16384
K = 1024
ITERS = 2
RIDGE = 0.5

f32 = jnp.float32
bf16 = jnp.bfloat16


def split(value):
    high = value.astype(bf16)
    return high, (value - high.astype(f32)).astype(bf16)


def dot(a, b):
    return lax.dot_general(a, b, (((1,), (0,)), ((), ())), preferred_element_type=f32)


def dot3(a, b):
    ah, al = split(a)
    bh, bl = split(b)
    return dot(ah, bh) + (dot(ah, bl) + dot(al, bh))


def dot2_left(a, exact):
    ah, al = split(a)
    return dot(ah, exact) + dot(al, exact)


def dot2_right(exact, b):
    bh, bl = split(b)
    return dot(exact, bh) + dot(exact, bl)


BLOCK = 256


def inverse_kernel(lower_ref, high_ref, low_ref, made_ref, inv):
    made_ref[...] = jnp.zeros_like(made_ref)
    n = lower_ref.shape[0]
    blocks = n // BLOCK
    rows = lax.broadcasted_iota(jnp.int32, (BLOCK, BLOCK), 0)
    cols = lax.broadcasted_iota(jnp.int32, (BLOCK, BLOCK), 1)
    spans = [pl.ds(b * BLOCK, BLOCK) for b in range(blocks)]
    inv[...] = jnp.zeros_like(inv)
    for span in spans:
        block = lower_ref[span, span].astype(f32)
        diag = jnp.sum(jnp.where(rows == cols, block, 0.0), axis=1, keepdims=True)
        inv[span, span] = jnp.where(rows == cols, 1.0 / diag, 0.0)

    def level(k, carry):
        below = ((rows >> k) == (cols >> k) + 1) & ((rows >> (k + 1)) == (cols >> (k + 1)))
        for span in spans:
            x = inv[span, span]
            off = jnp.where(below, lower_ref[span, span].astype(f32), 0.0).astype(bf16)
            inv[span, span] = x - dot3(dot2_left(x, off), x)
        return carry

    lax.fori_loop(0, int(math.log2(BLOCK)), level, 0)
    size = BLOCK
    while size < n:
        for at in range(0, n, 2 * size):
            top, bottom = pl.ds(at, size), pl.ds(at + size, size)
            a, b = inv[top, top], inv[bottom, bottom]
            inv[bottom, top] = -dot3(b, dot2_right(lower_ref[bottom, top], a))
        size *= 2
    xh, xl = split(inv[...])
    xht, xlt = split(inv[...].T)
    for span in spans:
        at, cols = slice(span.start, n), slice(span.start, span.start + BLOCK)
        m = dot(xht[:, at], xh[at, cols]) + (dot(xht[:, at], xl[at, cols]) + dot(xlt[:, at], xh[at, cols]))
        high_ref[:, span], low_ref[:, span] = split(m)


def coarse_inverse(lower):
    n = lower.shape[0]
    return pl.pallas_call(
        inverse_kernel,
        out_shape=[jax.ShapeDtypeStruct((n, n), bf16)] * 2 + [jax.ShapeDtypeStruct((8, 128), f32)],
        in_specs=[pl.BlockSpec(memory_space=pltpu.VMEM)],
        out_specs=[pl.BlockSpec(memory_space=pltpu.VMEM)] * 3,
        scratch_shapes=[pltpu.VMEM((n, n), f32)],
        compiler_params=pltpu.CompilerParams(vmem_limit_bytes=30 * 1024 * 1024),
        cost_estimate=pl.CostEstimate(flops=20 * 10**9, bytes_accessed=6 * 2**20, transcendentals=0),
    )(lower)


ROWS = 256


def feature_kernel(
    core_ref, samples_hbm, mine_hbm, other_hbm, targets_hbm, after_hbm, feat_ref, part_ref, samples, proj, targets, acc, sems
):
    del after_hbm
    n, parts, panels = samples.shape[0], part_ref.shape[0], proj.shape[0]
    core = core_ref[0]
    get_samples = pltpu.make_async_copy(samples_hbm, samples, sems.at[0])
    get_targets = pltpu.make_async_copy(targets_hbm, targets, sems.at[1])
    get_proj = [
        [
            pltpu.make_async_copy(half.at[:, j], proj.at[j, :, at], sems.at[2 + 2 * j + k])
            for k, (half, at) in enumerate(((mine_hbm, core), (other_hbm, 1 - core)))
        ]
        for j in range(panels)
    ]
    for copy in [get_samples] + sum(get_proj, []) + [get_targets]:
        copy.start()
    get_samples.wait()
    total = None
    for j in range(panels):
        for copy in get_proj[j]:
            copy.wait()
        panel = proj[j].reshape(samples.shape[1], proj.shape[-1])
        if j == panels - 1:
            get_targets.wait()
        for at in range(0, n, ROWS):
            value = dot(samples[at : at + ROWS, :], panel)
            if j:
                value = acc[at : at + ROWS, :] * value
            if j < panels - 1:
                acc[at : at + ROWS, :] = value
            else:
                feat = (value * (1.0 / math.sqrt(F))).astype(bf16)
                feat_ref[at : at + ROWS, :] = feat
                term = dot(targets[:, at : at + ROWS], feat)
                total = term if total is None else total + term
    step = total.shape[0] // parts
    for p in range(parts):
        part_ref[p] = total[p * step : (p + 1) * step, :]


def make_features(core, samples, mine, other, targets_t, parts, after):
    n = samples.shape[0]
    chips, panels, rows, width = mine.shape
    return pl.pallas_call(
        feature_kernel,
        out_shape=[
            jax.ShapeDtypeStruct((n, width), bf16),
            jax.ShapeDtypeStruct((parts, targets_t.shape[0] // parts, width), f32),
        ],
        in_specs=[pl.BlockSpec(memory_space=pltpu.SMEM)] + [pl.BlockSpec(memory_space=pl.ANY)] * 5,
        out_specs=[pl.BlockSpec(memory_space=pltpu.VMEM)] * 2,
        scratch_shapes=[
            pltpu.VMEM(samples.shape, bf16),
            pltpu.VMEM((panels, chips, 2, rows, width), bf16),
            pltpu.VMEM(targets_t.shape, bf16),
            pltpu.VMEM((n, width), f32),
            pltpu.SemaphoreType.DMA((2 + 2 * panels,)),
        ],
        compiler_params=pltpu.CompilerParams(vmem_limit_bytes=58 * 1024 * 1024),
        cost_estimate=pl.CostEstimate(flops=2 * 10**9, bytes_accessed=5 * 2**20, transcendentals=0),
    )(core, samples, mine, other, targets_t, after)


SLOTS = 128


def row_sum(value):
    return jnp.sum(value, axis=1, keepdims=True)


def lane(value, k):
    at = lax.broadcasted_iota(jnp.int32, value.shape, 1)
    return row_sum(jnp.where(at == k, value, 0.0))


def gathered(got_ref, halves, count):
    parts = []
    for h in range(halves):
        acc = got_ref[h, :, :count].astype(f32)
        for p in range(h + halves, got_ref.shape[0], halves):
            acc = acc + got_ref[p, :, :count].astype(f32)
        parts.append(acc)
    dots = got_ref[0, :, count:].astype(f32)
    for p in range(1, got_ref.shape[0]):
        dots = dots + got_ref[p, :, count:].astype(f32)
    at = lax.broadcasted_iota(jnp.int32, dots.shape, 1)
    sums = [row_sum(jnp.where((at >= 3 * k) & (at < 3 * k + 3), dots, 0.0)) for k in range(3)]
    return parts, sums


def coarse(parts, high_ref, low_ref):
    rows, total = parts[0].shape[0], None
    for h, part in enumerate(parts):
        span = slice(h * part.shape[1], (h + 1) * part.shape[1])
        high = part.astype(bf16).astype(f32)
        both = jnp.concatenate([high, part - high], 0).astype(bf16)
        one = dot(both, high_ref[span, :])
        term = one[:rows] + one[rows:] + dot(both, low_ref[span, :])[:rows]
        total = term if total is None else total + term
    return total


def next_direction(parity_ref, parts, high_ref, low_ref, resid, scale, energy, factor):
    count = resid.shape[1]
    solved = coarse(parts, high_ref, low_ref)
    product = energy
    mine = solved[:, :count]
    for h, part in enumerate(parts):
        here = solved[:, h * count : (h + 1) * count]
        product = product + row_sum(part * here)
        if h:
            mine = jnp.where(parity_ref[0] == h, here, mine)
    return product, scale * resid + factor * mine


def first_kernel(factor, parity_ref, got_ref, high_ref, low_ref, resid_ref, scale_ref, dir_ref, send_ref, rho_ref, dots_ref):
    count = resid_ref.shape[1]
    parts, sums = gathered(got_ref, rho_ref.shape[1] // count, count)
    parts = [part * factor for part in parts]
    product, direction = next_direction(
        parity_ref, parts, high_ref, low_ref, resid_ref[...], scale_ref[...], sums[0], factor
    )
    dir_ref[...] = direction
    for p in range(send_ref.shape[0]):
        send_ref[p] = direction.astype(bf16)
    for h, part in enumerate(parts):
        rho_ref[:, h * count : (h + 1) * count] = part
    at = lax.broadcasted_iota(jnp.int32, dots_ref.shape, 1)
    dots_ref[...] = jnp.where(at == 0, sums[0], jnp.where(at == 1, product, 0.0))


def step_kernel(
    factor, parity_ref, got_ref, high_ref, low_ref, resid_ref, scale_ref, image_ref, old_ref, rho_ref, dots_ref, answer_ref,
    dir_ref, send_ref, new_rho_ref, new_dots_ref, new_resid_ref, new_answer_ref,
):
    count = resid_ref.shape[1]
    parts, sums = gathered(got_ref, rho_ref.shape[1] // count, count)
    energy, product = lane(dots_ref[...], 0), lane(dots_ref[...], 1)
    alpha = product / sums[0]
    old = old_ref[...]
    new_answer_ref[...] = answer_ref[...] + alpha * old
    resid = resid_ref[...] - alpha * image_ref[...]
    new_resid_ref[...] = resid
    energy = energy - alpha * (2.0 * sums[1] - alpha * sums[2])
    parts = [
        rho_ref[:, h * count : (h + 1) * count] - alpha * (part * factor) for h, part in enumerate(parts)
    ]
    fresh, fine = next_direction(parity_ref, parts, high_ref, low_ref, resid, scale_ref[...], energy, factor)
    direction = fine + fresh / product * old
    dir_ref[...] = direction
    for p in range(send_ref.shape[0]):
        send_ref[p] = direction.astype(bf16)
    for h, part in enumerate(parts):
        new_rho_ref[:, h * count : (h + 1) * count] = part
    at = lax.broadcasted_iota(jnp.int32, dots_ref.shape, 1)
    new_dots_ref[...] = jnp.where(at == 0, energy, jnp.where(at == 1, fresh, 0.0))


def run_coarse(kernel, factor, n_dp, parity, *operands, more=0):
    rows, count = operands[3].shape
    n = operands[1].shape[0]
    vmem = pl.BlockSpec(memory_space=pltpu.VMEM)
    wide = jax.ShapeDtypeStruct((rows, count), f32)
    outs = [
        wide,
        jax.ShapeDtypeStruct((n_dp, rows, count), bf16),
        jax.ShapeDtypeStruct((rows, n), f32),
        jax.ShapeDtypeStruct((rows, SLOTS), f32),
    ] + [wide] * more
    return pl.pallas_call(
        functools.partial(kernel, factor),
        out_shape=outs,
        in_specs=[pl.BlockSpec(memory_space=pltpu.SMEM)] + [vmem] * len(operands),
        out_specs=[vmem] * len(outs),
        compiler_params=pltpu.CompilerParams(vmem_limit_bytes=12 * 1024 * 1024),
        cost_estimate=pl.CostEstimate(flops=10**8, bytes_accessed=5 * 2**20, transcendentals=0),
    )(parity, *operands)


def triple(value):
    high = lax.reduce_precision(value, 8, 7)
    mid = lax.reduce_precision(value - high, 8, 7)
    return jnp.stack([high, mid, value - high - mid], -1).astype(bf16)


def rounded(value):
    return lax.reduce_precision(value, 8, 7).astype(bf16)


def slots(values):
    parts = triple(values)
    flat = parts.reshape(parts.shape[:-2] + (-1,))
    return jnp.pad(flat, ((0, 0),) * (flat.ndim - 1) + ((0, SLOTS - flat.shape[-1]),))


def body(samples, projections, targets, feature_scale, coarse_factor):
    n_dp, n_sk = lax.axis_size("dp"), lax.axis_size("sketch")
    count = projections.shape[2]
    width = targets.shape[1]
    mine = width // n_dp
    cols = width // n_sk
    factor = 1.0 / math.sqrt(F // K)
    halves = K // count
    parity = (lax.axis_index("sketch") % halves).astype(jnp.int32).reshape(1)
    n = samples.shape[0]
    scale = feature_scale[None, :]

    chips = n_dp // 2
    core = (lax.axis_index("dp") % 2).astype(jnp.int32).reshape(1)
    mine_proj = lax.all_to_all(
        jnp.broadcast_to(projections[None], (chips,) + projections.shape),
        "dp",
        0,
        0,
        axis_index_groups=[[2 * z + c for z in range(chips)] for c in range(2)],
    )
    inv_high, inv_low, made = coarse_inverse(coarse_factor)
    mine_proj, made = lax.optimization_barrier((mine_proj, made))
    other_proj = lax.ppermute(mine_proj, "dp", [(i, i ^ 1) for i in range(n_dp)])
    feat, part = make_features(core, samples, mine_proj, other_proj, targets.T, n_dp, made)

    def scatter_dp(value):
        return jnp.sum(lax.all_to_all(value, "dp", 0, 0), 0)

    def gather_sk(value):
        return lax.all_to_all(jnp.broadcast_to(value[None], (n_sk,) + value.shape), "sketch", 0, 0)

    def everywhere(value, dots):
        return gather_sk(jnp.concatenate([value.astype(bf16), slots(dots)], 1))

    def forward(send):
        whole = lax.all_to_all(send, "dp", 0, 0).reshape(width, count)
        sums = lax.dot_general(whole, feat, (((1,), (1,)), ((), ())), preferred_element_type=f32)
        return whole, sums.astype(bf16).reshape(n_sk, cols, n)

    resid = scatter_dp(part)
    got = everywhere(resid, row_sum(scale * resid * resid))
    direction, send, rho, dots = run_coarse(
        first_kernel, factor, n_dp, parity, got, inv_high, inv_low, resid, scale
    )
    answer = jnp.zeros_like(resid)
    for step in range(ITERS - 1):
        _, sums = forward(send)
        u = rounded(jnp.sum(lax.all_to_all(sums, "sketch", 0, 0).astype(f32), 0))
        whole = gather_sk(u).reshape(width, n)
        image = scatter_dp(dot(whole, feat).reshape(n_dp, mine, count)) + RIDGE * direction
        weighted = scale * image
        got = everywhere(
            image,
            jnp.concatenate(
                [row_sum(direction * image), row_sum(weighted * resid), row_sum(weighted * image)], 1
            ),
        )
        direction, send, rho, dots, resid, answer = run_coarse(
            step_kernel, factor, n_dp, parity, got, inv_high, inv_low, resid, scale, image, direction, rho, dots, answer,
            more=2,
        )
    whole, sums = forward(send)
    squares = jnp.sum(jnp.square(whole.astype(f32)), 1).reshape(n_sk, cols, 1)
    got = lax.all_to_all(jnp.concatenate([sums, slots(squares)], 2), "sketch", 0, 0).astype(f32)
    total = jnp.sum(got, 0)
    u = rounded(total[:, :n])
    curve = row_sum(total[:, :n] * u.astype(f32)) + (RIDGE / n_dp) * row_sum(total[:, n:])
    got = gather_sk(jnp.concatenate([u, slots(curve)], 1)).reshape(width, n + SLOTS)
    image = dot(got[:, :n], feat)
    curve = row_sum(got[:, n : n + 3].astype(f32))
    sent = jnp.concatenate([image, jnp.broadcast_to(curve, (width, SLOTS))], 1)
    total = scatter_dp(sent.reshape(n_dp, mine, count + SLOTS))
    image = total[:, :count] + RIDGE * direction
    alpha = dots[:, 1:2] / total[:, count : count + 1]
    out = jnp.stack([answer + alpha * direction, resid - alpha * image])
    got = lax.all_to_all(jnp.broadcast_to(out[None], (n_dp,) + out.shape), "dp", 0, 0)
    return got[:, 0].reshape(width, count).T, got[:, 1].reshape(width, count).T


def solution(mesh):
    placed = (P("dp", None), P(None, "dp", "sketch"), P("dp", None), P("sketch"), P())
    return jax.shard_map(
        body,
        mesh=mesh,
        in_specs=placed,
        out_specs=(P("sketch", None), P("sketch", None)),
        check_vma=False,
    )
```

```python
import functools
import math

import jax
import jax.numpy as jnp
from jax import lax
from jax.experimental import pallas as pl
from jax.experimental.pallas import tpu as pltpu
from jax.sharding import PartitionSpec as P

F = 16384
K = 1024
ITERS = 2
RIDGE = 0.5

f32 = jnp.float32
bf16 = jnp.bfloat16


def split(value):
    high = value.astype(bf16)
    return high, (value - high.astype(f32)).astype(bf16)


def dot(a, b):
    return lax.dot_general(a, b, (((1,), (0,)), ((), ())), preferred_element_type=f32)


def dot3(a, b):
    ah, al = split(a)
    bh, bl = split(b)
    return dot(ah, bh) + (dot(ah, bl) + dot(al, bh))


def dot2_left(a, exact):
    ah, al = split(a)
    return dot(ah, exact) + dot(al, exact)


def dot2_right(exact, b):
    bh, bl = split(b)
    return dot(exact, bh) + dot(exact, bl)


BLOCK = 256


def inverse_kernel(core_ref, lower_hbm, high_ref, low_ref, made_ref, lower, inv, sems):
    n = lower.shape[0]
    blocks = n // BLOCK
    spans = [pl.ds(b * BLOCK, BLOCK) for b in range(blocks)]
    parts = [(span, span) for span in spans]
    size = BLOCK
    while size < n:
        parts += [(pl.ds(at + size, size), pl.ds(at, size)) for at in range(0, n, 2 * size)]
        size *= 2
    copies = [
        pltpu.make_async_copy(lower_hbm.at[part], lower.at[part], sems.at[k]) for k, part in enumerate(parts)
    ]
    for copy in copies:
        copy.start()
    made_ref[0] = core_ref[0]
    inv[...] = jnp.zeros_like(inv)
    rows = lax.broadcasted_iota(jnp.int32, (BLOCK, BLOCK), 0)
    cols = lax.broadcasted_iota(jnp.int32, (BLOCK, BLOCK), 1)

    def below(k):
        return ((rows >> k) == (cols >> k) + 1) & ((rows >> (k + 1)) == (cols >> (k + 1)))

    for copy, span in zip(copies, spans):
        copy.wait()
        block = lower[span, span].astype(f32)
        diag = jnp.where(rows == cols, block, 0.0)
        down = 1.0 / jnp.sum(diag, axis=1, keepdims=True)
        across = 1.0 / jnp.sum(diag, axis=0, keepdims=True)
        inv[span, span] = jnp.where(rows == cols, down, jnp.where(below(0), -(block * down) * across, 0.0))

    def level(k, carry):
        mask = below(k)
        for span in spans:
            x = inv[span, span]
            off = jnp.where(mask, lower[span, span].astype(f32), 0.0).astype(bf16)
            inv[span, span] = x - dot3(dot2_left(x, off), x)
        return carry

    lax.fori_loop(1, int(math.log2(BLOCK)), level, 0)
    for copy, (bottom, top) in list(zip(copies, parts))[blocks:]:
        copy.wait()
        a, b = inv[top, top], inv[bottom, bottom]
        inv[bottom, top] = -dot3(b, dot2_right(lower[bottom, top], a))
    for span in spans:
        high_ref[span, :], low_ref[span, :] = split(inv[span, :])


def coarse_factor_inverse(core, lower):
    n = lower.shape[0]
    vmem = pl.BlockSpec(memory_space=pltpu.VMEM)
    return pl.pallas_call(
        inverse_kernel,
        out_shape=[jax.ShapeDtypeStruct((n, n), bf16)] * 2 + [jax.ShapeDtypeStruct((1,), jnp.int32)],
        in_specs=[pl.BlockSpec(memory_space=pltpu.SMEM), pl.BlockSpec(memory_space=pl.ANY)],
        out_specs=[vmem] * 2 + [pl.BlockSpec(memory_space=pltpu.SMEM)],
        scratch_shapes=[
            pltpu.VMEM((n, n), bf16),
            pltpu.VMEM((n, n), f32),
            pltpu.SemaphoreType.DMA((2 * (n // BLOCK) - 1,)),
        ],
        compiler_params=pltpu.CompilerParams(vmem_limit_bytes=56 * 1024 * 1024),
        cost_estimate=pl.CostEstimate(flops=10**10, bytes_accessed=6 * 2**20, transcendentals=0),
    )(core, lower)


def product_kernel(xh_ref, xl_ref, high_ref, low_ref):
    n = xh_ref.shape[0]
    xht = xh_ref[...].astype(f32).T.astype(bf16)
    xlt = xl_ref[...].astype(f32).T.astype(bf16)
    for start in range(0, n, BLOCK):
        at, cols = slice(start, n), slice(start, start + BLOCK)
        xh, xl = xh_ref[at, cols], xl_ref[at, cols]
        m = dot(xht[:, at], xh) + (dot(xht[:, at], xl) + dot(xlt[:, at], xh))
        high_ref[:, cols], low_ref[:, cols] = split(m)


def coarse_inverse(xh, xl):
    n = xh.shape[0]
    vmem = pl.BlockSpec(memory_space=pltpu.VMEM)
    return pl.pallas_call(
        product_kernel,
        out_shape=[jax.ShapeDtypeStruct((n, n), bf16)] * 2,
        in_specs=[vmem] * 2,
        out_specs=[vmem] * 2,
        compiler_params=pltpu.CompilerParams(vmem_limit_bytes=56 * 1024 * 1024),
        cost_estimate=pl.CostEstimate(flops=4 * 10**9, bytes_accessed=8 * 2**20, transcendentals=0),
    )(xh, xl)


def copies_kernel(value_hbm, out_hbm, sems):
    copies = [pltpu.make_async_copy(value_hbm, out_hbm.at[p], sems.at[p]) for p in range(out_hbm.shape[0])]
    for copy in copies:
        copy.start()
    for copy in copies:
        copy.wait()


def repeat(value, count):
    return pl.pallas_call(
        copies_kernel,
        out_shape=jax.ShapeDtypeStruct((count,) + value.shape, value.dtype),
        in_specs=[pl.BlockSpec(memory_space=pl.ANY)],
        out_specs=pl.BlockSpec(memory_space=pl.ANY),
        scratch_shapes=[pltpu.SemaphoreType.DMA((count,))],
    )(value)


def output_kernel(got_ref, answer_ref, resid_ref):
    rows = got_ref.shape[2]
    for p in range(got_ref.shape[0]):
        answer_ref[p * rows : (p + 1) * rows, :] = got_ref[p, 0].astype(f32)
        resid_ref[p * rows : (p + 1) * rows, :] = got_ref[p, 1].astype(f32)


def outputs(got):
    parts, _, rows, count = got.shape
    vmem = pl.BlockSpec(memory_space=pltpu.VMEM)
    return pl.pallas_call(
        output_kernel,
        out_shape=[jax.ShapeDtypeStruct((parts * rows, count), f32)] * 2,
        in_specs=[vmem],
        out_specs=[vmem] * 2,
    )(got)


ROWS = 256


def feature_kernel(
    core_ref, samples_hbm, mine_hbm, other_hbm, targets_hbm, feat_ref, part_ref, samples, proj, targets, acc, sems
):
    n, parts, panels = samples.shape[0], part_ref.shape[0], proj.shape[0]
    core = core_ref[0]
    get_samples = pltpu.make_async_copy(samples_hbm, samples, sems.at[0])
    get_targets = pltpu.make_async_copy(targets_hbm, targets, sems.at[1])
    get_proj = [
        [
            pltpu.make_async_copy(half.at[:, j], proj.at[j, :, at], sems.at[2 + 2 * j + k])
            for k, (half, at) in enumerate(((mine_hbm, core), (other_hbm, 1 - core)))
        ]
        for j in range(panels)
    ]
    for copy in [get_samples] + sum(get_proj, []) + [get_targets]:
        copy.start()
    get_samples.wait()
    total = None
    for j in range(panels):
        for copy in get_proj[j]:
            copy.wait()
        panel = proj[j].reshape(samples.shape[1], proj.shape[-1])
        if j == panels - 1:
            get_targets.wait()
        for at in range(0, n, ROWS):
            value = dot(samples[at : at + ROWS, :], panel)
            if j:
                value = acc[at : at + ROWS, :] * value
            if j < panels - 1:
                acc[at : at + ROWS, :] = value
            else:
                feat = (value * (1.0 / math.sqrt(F))).astype(bf16)
                feat_ref[at : at + ROWS, :] = feat
                term = dot(targets[:, at : at + ROWS], feat)
                total = term if total is None else total + term
    step = total.shape[0] // parts
    for p in range(parts):
        part_ref[p] = total[p * step : (p + 1) * step, :]


def make_features(core, samples, mine, other, targets_t, parts):
    n = samples.shape[0]
    chips, panels, rows, width = mine.shape
    return pl.pallas_call(
        feature_kernel,
        out_shape=[
            jax.ShapeDtypeStruct((n, width), bf16),
            jax.ShapeDtypeStruct((parts, targets_t.shape[0] // parts, width), f32),
        ],
        in_specs=[pl.BlockSpec(memory_space=pltpu.SMEM)] + [pl.BlockSpec(memory_space=pl.ANY)] * 4,
        out_specs=[pl.BlockSpec(memory_space=pltpu.VMEM)] * 2,
        scratch_shapes=[
            pltpu.VMEM(samples.shape, bf16),
            pltpu.VMEM((panels, chips, 2, rows, width), bf16),
            pltpu.VMEM(targets_t.shape, bf16),
            pltpu.VMEM((n, width), f32),
            pltpu.SemaphoreType.DMA((2 + 2 * panels,)),
        ],
        compiler_params=pltpu.CompilerParams(vmem_limit_bytes=48 * 1024 * 1024),
        cost_estimate=pl.CostEstimate(flops=2 * 10**9, bytes_accessed=5 * 2**20, transcendentals=0),
    )(core, samples, mine, other, targets_t)


SLOTS = 128


def row_sum(value):
    return jnp.sum(value, axis=1, keepdims=True)


def lane(value, k):
    at = lax.broadcasted_iota(jnp.int32, value.shape, 1)
    return row_sum(jnp.where(at == k, value, 0.0))


def gathered(got_ref, halves, count):
    parts = []
    for h in range(halves):
        acc = got_ref[h, :, :count].astype(f32)
        for p in range(h + halves, got_ref.shape[0], halves):
            acc = acc + got_ref[p, :, :count].astype(f32)
        parts.append(acc)
    dots = got_ref[0, :, count:].astype(f32)
    for p in range(1, got_ref.shape[0]):
        dots = dots + got_ref[p, :, count:].astype(f32)
    at = lax.broadcasted_iota(jnp.int32, dots.shape, 1)
    sums = [row_sum(jnp.where((at >= 3 * k) & (at < 3 * k + 3), dots, 0.0)) for k in range(3)]
    return parts, sums


def fetch(high_hbm, low_hbm, high, low, sems, halves):
    span = high.shape[0] // halves
    copies = [
        [
            pltpu.make_async_copy(src.at[pl.ds(h * span, span)], dst.at[pl.ds(h * span, span)], sems.at[2 * h + k])
            for k, (src, dst) in enumerate(((high_hbm, high), (low_hbm, low)))
        ]
        for h in range(halves)
    ]
    for copy in sum(copies, []):
        copy.start()
    return high, low, copies


def coarse(parts, inverse):
    high_ref, low_ref, copies = inverse
    rows, total = parts[0].shape[0], None
    for h, part in enumerate(parts):
        span = slice(h * part.shape[1], (h + 1) * part.shape[1])
        high = part.astype(bf16).astype(f32)
        both = jnp.concatenate([high, part - high], 0).astype(bf16)
        copies[h][0].wait()
        one = dot(both, high_ref[span, :])
        copies[h][1].wait()
        term = one[:rows] + one[rows:] + dot(both, low_ref[span, :])[:rows]
        total = term if total is None else total + term
    return total


def next_direction(parity_ref, parts, inverse, resid, scale, energy, factor):
    count = resid.shape[1]
    solved = coarse(parts, inverse)
    product = energy
    mine = solved[:, :count]
    for h, part in enumerate(parts):
        here = solved[:, h * count : (h + 1) * count]
        product = product + row_sum(part * here)
        if h:
            mine = jnp.where(parity_ref[0] == h, here, mine)
    return product, scale * resid + factor * mine


def first_kernel(
    factor, parity_ref, got_ref, high_hbm, low_hbm, resid_ref, scale_ref, dir_ref, send_ref, rho_ref, dots_ref, high, low, sems
):
    count = resid_ref.shape[1]
    inverse = fetch(high_hbm, low_hbm, high, low, sems, rho_ref.shape[1] // count)
    parts, sums = gathered(got_ref, rho_ref.shape[1] // count, count)
    parts = [part * factor for part in parts]
    product, direction = next_direction(
        parity_ref, parts, inverse, resid_ref[...], scale_ref[...], sums[0], factor
    )
    dir_ref[...] = direction
    for p in range(send_ref.shape[0]):
        send_ref[p] = direction.astype(bf16)
    for h, part in enumerate(parts):
        rho_ref[:, h * count : (h + 1) * count] = part
    at = lax.broadcasted_iota(jnp.int32, dots_ref.shape, 1)
    dots_ref[...] = jnp.where(at == 0, sums[0], jnp.where(at == 1, product, 0.0))


def step_kernel(
    factor, parity_ref, got_ref, high_hbm, low_hbm, resid_ref, scale_ref, image_ref, old_ref, rho_ref, dots_ref, answer_ref,
    dir_ref, send_ref, new_rho_ref, new_dots_ref, new_resid_ref, new_answer_ref, high, low, sems,
):
    count = resid_ref.shape[1]
    inverse = fetch(high_hbm, low_hbm, high, low, sems, rho_ref.shape[1] // count)
    parts, sums = gathered(got_ref, rho_ref.shape[1] // count, count)
    energy, product = lane(dots_ref[...], 0), lane(dots_ref[...], 1)
    alpha = product / sums[0]
    old = old_ref[...]
    new_answer_ref[...] = answer_ref[...] + alpha * old
    resid = resid_ref[...] - alpha * image_ref[...]
    new_resid_ref[...] = resid
    energy = energy - alpha * (2.0 * sums[1] - alpha * sums[2])
    parts = [
        rho_ref[:, h * count : (h + 1) * count] - alpha * (part * factor) for h, part in enumerate(parts)
    ]
    fresh, fine = next_direction(parity_ref, parts, inverse, resid, scale_ref[...], energy, factor)
    direction = fine + fresh / product * old
    dir_ref[...] = direction
    for p in range(send_ref.shape[0]):
        send_ref[p] = direction.astype(bf16)
    for h, part in enumerate(parts):
        new_rho_ref[:, h * count : (h + 1) * count] = part
    at = lax.broadcasted_iota(jnp.int32, dots_ref.shape, 1)
    new_dots_ref[...] = jnp.where(at == 0, energy, jnp.where(at == 1, fresh, 0.0))


def run_coarse(kernel, factor, n_dp, parity, *operands, more=0):
    rows, count = operands[3].shape
    n = operands[1].shape[0]
    vmem = pl.BlockSpec(memory_space=pltpu.VMEM)
    wide = jax.ShapeDtypeStruct((rows, count), f32)
    outs = [
        wide,
        jax.ShapeDtypeStruct((n_dp, rows, count), bf16),
        jax.ShapeDtypeStruct((rows, n), f32),
        jax.ShapeDtypeStruct((rows, SLOTS), f32),
    ] + [wide] * more
    return pl.pallas_call(
        functools.partial(kernel, factor),
        out_shape=outs,
        in_specs=[pl.BlockSpec(memory_space=pltpu.SMEM), vmem]
        + [pl.BlockSpec(memory_space=pl.ANY)] * 2
        + [vmem] * (len(operands) - 3),
        out_specs=[vmem] * len(outs),
        scratch_shapes=[pltpu.VMEM((n, n), bf16)] * 2 + [pltpu.SemaphoreType.DMA((2 * (n // count),))],
        compiler_params=pltpu.CompilerParams(vmem_limit_bytes=52 * 1024 * 1024),
        cost_estimate=pl.CostEstimate(flops=10**8, bytes_accessed=5 * 2**20, transcendentals=0),
    )(parity, *operands)


def triple(value):
    high = lax.reduce_precision(value, 8, 7)
    mid = lax.reduce_precision(value - high, 8, 7)
    return jnp.stack([high, mid, value - high - mid], -1).astype(bf16)


def rounded(value):
    return lax.reduce_precision(value, 8, 7).astype(bf16)


def slots(values):
    parts = triple(values)
    flat = parts.reshape(parts.shape[:-2] + (-1,))
    return jnp.pad(flat, ((0, 0),) * (flat.ndim - 1) + ((0, SLOTS - flat.shape[-1]),))


def body(samples, projections, targets, feature_scale, coarse_factor):
    n_dp, n_sk = lax.axis_size("dp"), lax.axis_size("sketch")
    count = projections.shape[2]
    width = targets.shape[1]
    mine = width // n_dp
    cols = width // n_sk
    factor = 1.0 / math.sqrt(F // K)
    halves = K // count
    parity = (lax.axis_index("sketch") % halves).astype(jnp.int32).reshape(1)
    n = samples.shape[0]
    scale = feature_scale[None, :]

    chips = n_dp // 2
    core = (lax.axis_index("dp") % 2).astype(jnp.int32).reshape(1)
    mine_proj = lax.all_to_all(
        repeat(projections, chips),
        "dp",
        0,
        0,
        axis_index_groups=[[2 * z + c for z in range(chips)] for c in range(2)],
    )
    factor_high, factor_low, core = coarse_factor_inverse(core, coarse_factor)
    mine_proj, core = lax.optimization_barrier((mine_proj, core))
    other_proj = lax.ppermute(mine_proj, "dp", [(i, i ^ 1) for i in range(n_dp)])
    feat, part = make_features(core, samples, mine_proj, other_proj, targets.T, n_dp)
    inv_high, inv_low = coarse_inverse(factor_high, factor_low)

    def scatter_dp(value):
        return jnp.sum(lax.all_to_all(value, "dp", 0, 0), 0)

    def gather_sk(value):
        return lax.all_to_all(jnp.broadcast_to(value[None], (n_sk,) + value.shape), "sketch", 0, 0)

    def everywhere(value, dots):
        return gather_sk(jnp.concatenate([value.astype(bf16), slots(dots)], 1))

    def forward(send):
        whole = lax.all_to_all(send, "dp", 0, 0).reshape(width, count)
        sums = lax.dot_general(whole, feat, (((1,), (1,)), ((), ())), preferred_element_type=f32)
        return whole, sums.astype(bf16).reshape(n_sk, cols, n)

    resid = scatter_dp(part)
    got = everywhere(resid, row_sum(scale * resid * resid))
    direction, send, rho, dots = run_coarse(
        first_kernel, factor, n_dp, parity, got, inv_high, inv_low, resid, scale
    )
    answer = jnp.zeros_like(resid)
    for step in range(ITERS - 1):
        _, sums = forward(send)
        u = rounded(jnp.sum(lax.all_to_all(sums, "sketch", 0, 0).astype(f32), 0))
        whole = gather_sk(u).reshape(width, n)
        image = scatter_dp(dot(whole, feat).reshape(n_dp, mine, count)) + RIDGE * direction
        weighted = scale * image
        got = everywhere(
            image,
            jnp.concatenate(
                [row_sum(direction * image), row_sum(weighted * resid), row_sum(weighted * image)], 1
            ),
        )
        direction, send, rho, dots, resid, answer = run_coarse(
            step_kernel, factor, n_dp, parity, got, inv_high, inv_low, resid, scale, image, direction, rho, dots, answer,
            more=2,
        )
    whole, sums = forward(send)
    squares = jnp.sum(jnp.square(whole.astype(f32)), 1).reshape(n_sk, cols, 1)
    got = lax.all_to_all(jnp.concatenate([sums, slots(squares)], 2), "sketch", 0, 0).astype(f32)
    total = jnp.sum(got, 0)
    u = rounded(total[:, :n])
    curve = row_sum(total[:, :n] * u.astype(f32)) + (RIDGE / n_dp) * row_sum(total[:, n:])
    got = gather_sk(jnp.concatenate([u, slots(curve)], 1)).reshape(width, n + SLOTS)
    image = dot(got[:, :n], feat)
    sent = jnp.concatenate([image.astype(bf16), got[:, n:]], 1)
    got = lax.all_to_all(sent.reshape(n_dp, mine, count + SLOTS), "dp", 0, 0).astype(f32)
    total = jnp.sum(got, 0)
    image = total[:, :count] + RIDGE * direction
    alpha = dots[:, 1:2] / row_sum(total[:, count:])
    out = jnp.stack([answer + alpha * direction, resid - alpha * image]).astype(bf16)
    got = lax.all_to_all(jnp.broadcast_to(out[None], (n_dp,) + out.shape), "dp", 0, 0)
    answer, resid = outputs(got)
    return answer.T, resid.T


def solution(mesh):
    placed = (P("dp", None), P(None, "dp", "sketch"), P("dp", None), P("sketch"), P())
    return jax.shard_map(
        body,
        mesh=mesh,
        in_specs=placed,
        out_specs=(P("sketch", None), P("sketch", None)),
        check_vma=False,
    )
```

```python
import functools
import math

import jax
import jax.numpy as jnp
from jax import lax
from jax.experimental import pallas as pl
from jax.experimental.pallas import tpu as pltpu
from jax.sharding import PartitionSpec as P

F = 16384
K = 1024
ITERS = 2
RIDGE = 0.5

f32 = jnp.float32
bf16 = jnp.bfloat16


def split(value):
    high = value.astype(bf16)
    return high, (value - high.astype(f32)).astype(bf16)


def dot(a, b):
    return lax.dot_general(a, b, (((1,), (0,)), ((), ())), preferred_element_type=f32)


def dot3(a, b):
    ah, al = split(a)
    bh, bl = split(b)
    return dot(ah, bh) + (dot(ah, bl) + dot(al, bh))


def dot2_left(a, exact):
    ah, al = split(a)
    return dot(ah, exact) + dot(al, exact)


def dot2_right(exact, b):
    bh, bl = split(b)
    return dot(exact, bh) + dot(exact, bl)


BLOCK = 256


def blocks_kernel(order_ref, lower_hbm, inv_ref, lower, sems):
    del order_ref
    n = lower_hbm.shape[0]
    spans = [pl.ds(b * BLOCK, BLOCK) for b in range(n // BLOCK)]
    copies = [
        pltpu.make_async_copy(lower_hbm.at[span, span], lower.at[span], sems.at[b]) for b, span in enumerate(spans)
    ]
    for copy in copies:
        copy.start()
    rows = lax.broadcasted_iota(jnp.int32, (BLOCK, BLOCK), 0)
    cols = lax.broadcasted_iota(jnp.int32, (BLOCK, BLOCK), 1)

    def below(k):
        return ((rows >> k) == (cols >> k) + 1) & ((rows >> (k + 1)) == (cols >> (k + 1)))

    for copy, span in zip(copies, spans):
        copy.wait()
        block = lower[span, :].astype(f32)
        diag = jnp.where(rows == cols, block, 0.0)
        down = 1.0 / jnp.sum(diag, axis=1, keepdims=True)
        across = 1.0 / jnp.sum(diag, axis=0, keepdims=True)
        inv_ref[span, :] = jnp.where(rows == cols, down, jnp.where(below(0), -(block * down) * across, 0.0))

    def level(k, carry):
        mask = below(k)
        for span in spans:
            x = inv_ref[span, :]
            off = jnp.where(mask, lower[span, :].astype(f32), 0.0).astype(bf16)
            inv_ref[span, :] = x - dot3(dot2_left(x, off), x)
        return carry

    lax.fori_loop(1, int(math.log2(BLOCK)), level, 0)


def block_inverses(order, lower):
    n = lower.shape[0]
    return pl.pallas_call(
        blocks_kernel,
        out_shape=jax.ShapeDtypeStruct((n, BLOCK), f32),
        in_specs=[pl.BlockSpec(memory_space=pltpu.SMEM), pl.BlockSpec(memory_space=pl.ANY)],
        out_specs=pl.BlockSpec(memory_space=pltpu.VMEM),
        scratch_shapes=[pltpu.VMEM((n, BLOCK), bf16), pltpu.SemaphoreType.DMA((n // BLOCK,))],
        compiler_params=pltpu.CompilerParams(vmem_limit_bytes=52 * 1024 * 1024),
        cost_estimate=pl.CostEstimate(flops=10**10, bytes_accessed=2 * 2**20, transcendentals=0),
    )(order, lower)


def product_kernel(blocks_ref, lower_hbm, order_hbm, high_ref, low_ref, lower, inv, sems):
    del order_hbm
    n = lower.shape[0]
    size, joins = BLOCK, []
    while size < n:
        joins += [(pl.ds(at + size, size), pl.ds(at, size)) for at in range(0, n, 2 * size)]
        size *= 2
    copies = [
        pltpu.make_async_copy(lower_hbm.at[part], lower.at[part], sems.at[k]) for k, part in enumerate(joins)
    ]
    for copy in copies:
        copy.start()
    spans = [slice(b, b + BLOCK) for b in range(0, n, BLOCK)]
    inv[...] = jnp.zeros_like(inv)
    for span in spans:
        inv[span, span] = blocks_ref[span, :]
    for copy, (bottom, top) in zip(copies, joins):
        copy.wait()
        a, b = inv[top, top], inv[bottom, bottom]
        inv[bottom, top] = -dot3(b, dot2_right(lower[bottom, top], a))
    parts = [[split(inv[row, col]) for col in spans[: r + 1]] for r, row in enumerate(spans)]
    turned = [[tuple(half.astype(f32).T.astype(bf16) for half in part) for part in row] for row in parts]
    for a, row in enumerate(spans):
        for b, col in enumerate(spans):
            total = None
            for k in range(max(a, b), len(spans)):
                (ah, al), (bh, bl) = turned[k][a], parts[k][b]
                term = dot(ah, bh) + (dot(ah, bl) + dot(al, bh))
                total = term if total is None else total + term
            high_ref[row, col], low_ref[row, col] = split(total)


def coarse_inverse(blocks, lower, order):
    n = lower.shape[0]
    vmem, anywhere = pl.BlockSpec(memory_space=pltpu.VMEM), pl.BlockSpec(memory_space=pl.ANY)
    return pl.pallas_call(
        product_kernel,
        out_shape=[jax.ShapeDtypeStruct((n, n), bf16)] * 2,
        in_specs=[vmem, anywhere, anywhere],
        out_specs=[vmem] * 2,
        scratch_shapes=[
            pltpu.VMEM((n, n), bf16),
            pltpu.VMEM((n, n), f32),
            pltpu.SemaphoreType.DMA((n // BLOCK - 1,)),
        ],
        compiler_params=pltpu.CompilerParams(vmem_limit_bytes=50 * 1024 * 1024),
        cost_estimate=pl.CostEstimate(flops=10**10, bytes_accessed=8 * 2**20, transcendentals=0),
    )(blocks, lower, order)


def repeat_kernel(value_ref, out_ref):
    for p in range(out_ref.shape[0]):
        out_ref[p] = value_ref[...]


def repeat(value, count):
    vmem = pl.BlockSpec(memory_space=pltpu.VMEM)
    return pl.pallas_call(
        repeat_kernel,
        out_shape=jax.ShapeDtypeStruct((count,) + value.shape, value.dtype),
        in_specs=[vmem],
        out_specs=vmem,
        compiler_params=pltpu.CompilerParams(vmem_limit_bytes=8 * 1024 * 1024),
    )(value)


def output_kernel(got_ref, answer_ref, resid_ref):
    rows = got_ref.shape[2]
    for p in range(got_ref.shape[0]):
        answer_ref[p * rows : (p + 1) * rows, :] = got_ref[p, 0].astype(f32)
        resid_ref[p * rows : (p + 1) * rows, :] = got_ref[p, 1].astype(f32)


def outputs(got):
    parts, _, rows, count = got.shape
    vmem = pl.BlockSpec(memory_space=pltpu.VMEM)
    return pl.pallas_call(
        output_kernel,
        out_shape=[jax.ShapeDtypeStruct((parts * rows, count), f32)] * 2,
        in_specs=[vmem],
        out_specs=[vmem] * 2,
    )(got)


ROWS = 256


def feature_kernel(
    core_ref, samples_hbm, mine_hbm, other_hbm, targets_hbm, feat_ref, part_ref, order_ref, samples, proj, targets, acc, sems
):
    n, parts, panels = samples.shape[0], part_ref.shape[0], proj.shape[0]
    core = core_ref[0]
    order_ref[0] = core
    get_samples = pltpu.make_async_copy(samples_hbm, samples, sems.at[0])
    get_targets = pltpu.make_async_copy(targets_hbm, targets, sems.at[1])
    get_proj = [
        [
            pltpu.make_async_copy(half.at[:, j], proj.at[j, :, at], sems.at[2 + 2 * j + k])
            for k, (half, at) in enumerate(((mine_hbm, core), (other_hbm, 1 - core)))
        ]
        for j in range(panels)
    ]
    for copy in [get_samples] + sum(get_proj, []) + [get_targets]:
        copy.start()
    get_samples.wait()
    total = None
    for j in range(panels):
        for copy in get_proj[j]:
            copy.wait()
        panel = proj[j].reshape(samples.shape[1], proj.shape[-1])
        if j == panels - 1:
            get_targets.wait()
        for at in range(0, n, ROWS):
            value = dot(samples[at : at + ROWS, :], panel)
            if j:
                value = acc[at : at + ROWS, :] * value
            if j < panels - 1:
                acc[at : at + ROWS, :] = value
            else:
                feat = (value * (1.0 / math.sqrt(F))).astype(bf16)
                feat_ref[at : at + ROWS, :] = feat
                term = dot(targets[:, at : at + ROWS], feat)
                total = term if total is None else total + term
    step = total.shape[0] // parts
    for p in range(parts):
        part_ref[p] = total[p * step : (p + 1) * step, :]


def make_features(core, samples, mine, other, targets_t, parts):
    n = samples.shape[0]
    chips, panels, rows, width = mine.shape
    return pl.pallas_call(
        feature_kernel,
        out_shape=[
            jax.ShapeDtypeStruct((n, width), bf16),
            jax.ShapeDtypeStruct((parts, targets_t.shape[0] // parts, width), f32),
            jax.ShapeDtypeStruct((1,), jnp.int32),
        ],
        in_specs=[pl.BlockSpec(memory_space=pltpu.SMEM)] + [pl.BlockSpec(memory_space=pl.ANY)] * 4,
        out_specs=[pl.BlockSpec(memory_space=pltpu.VMEM)] * 2 + [pl.BlockSpec(memory_space=pltpu.SMEM)],
        scratch_shapes=[
            pltpu.VMEM(samples.shape, bf16),
            pltpu.VMEM((panels, chips, 2, rows, width), bf16),
            pltpu.VMEM(targets_t.shape, bf16),
            pltpu.VMEM((n, width), f32),
            pltpu.SemaphoreType.DMA((2 + 2 * panels,)),
        ],
        compiler_params=pltpu.CompilerParams(vmem_limit_bytes=50 * 1024 * 1024),
        cost_estimate=pl.CostEstimate(flops=2 * 10**9, bytes_accessed=5 * 2**20, transcendentals=0),
    )(core, samples, mine, other, targets_t)


SLOTS = 128


def row_sum(value):
    return jnp.sum(value, axis=1, keepdims=True)


def lane(value, k):
    at = lax.broadcasted_iota(jnp.int32, value.shape, 1)
    return row_sum(jnp.where(at == k, value, 0.0))


def gathered(got_ref, halves, count):
    parts = []
    for h in range(halves):
        acc = got_ref[h, :, :count].astype(f32)
        for p in range(h + halves, got_ref.shape[0], halves):
            acc = acc + got_ref[p, :, :count].astype(f32)
        parts.append(acc)
    dots = got_ref[0, :, count:].astype(f32)
    for p in range(1, got_ref.shape[0]):
        dots = dots + got_ref[p, :, count:].astype(f32)
    at = lax.broadcasted_iota(jnp.int32, dots.shape, 1)
    sums = [row_sum(jnp.where((at >= 3 * k) & (at < 3 * k + 3), dots, 0.0)) for k in range(3)]
    return parts, sums


def coarse(parts, inverse):
    high_ref, low_ref, copy = inverse
    rows, total, left = parts[0].shape[0], None, []
    for h, part in enumerate(parts):
        span = slice(h * part.shape[1], (h + 1) * part.shape[1])
        high = part.astype(bf16).astype(f32)
        both = jnp.concatenate([high, part - high], 0).astype(bf16)
        one = dot(both, high_ref[span, :])
        term = one[:rows] + one[rows:]
        total = term if total is None else total + term
        left.append((span, both))
    copy.wait()
    for span, both in left:
        total = total + dot(both, low_ref[span, :])[:rows]
    return total


def next_direction(parity_ref, parts, inverse, resid, scale, energy, factor):
    count = resid.shape[1]
    solved = coarse(parts, inverse)
    product = energy
    mine = solved[:, :count]
    for h, part in enumerate(parts):
        here = solved[:, h * count : (h + 1) * count]
        product = product + row_sum(part * here)
        if h:
            mine = jnp.where(parity_ref[0] == h, here, mine)
    return product, scale * resid + factor * mine


def first_kernel(
    factor, parity_ref, got_ref, high_ref, low_hbm, resid_ref, scale_ref, dir_ref, send_ref, rho_ref, dots_ref, low, sem
):
    count = resid_ref.shape[1]
    fetch = pltpu.make_async_copy(low_hbm, low, sem)
    fetch.start()
    inverse = high_ref, low, fetch
    parts, sums = gathered(got_ref, rho_ref.shape[1] // count, count)
    parts = [part * factor for part in parts]
    product, direction = next_direction(
        parity_ref, parts, inverse, resid_ref[...], scale_ref[...], sums[0], factor
    )
    dir_ref[...] = direction
    for p in range(send_ref.shape[0]):
        send_ref[p] = direction.astype(bf16)
    for h, part in enumerate(parts):
        rho_ref[:, h * count : (h + 1) * count] = part
    at = lax.broadcasted_iota(jnp.int32, dots_ref.shape, 1)
    dots_ref[...] = jnp.where(at == 0, sums[0], jnp.where(at == 1, product, 0.0))


def step_kernel(
    factor, parity_ref, got_ref, high_ref, low_hbm, resid_ref, scale_ref, image_ref, old_ref, rho_ref, dots_ref, answer_ref,
    dir_ref, send_ref, new_rho_ref, new_dots_ref, new_resid_ref, new_answer_ref, low, sem,
):
    count = resid_ref.shape[1]
    fetch = pltpu.make_async_copy(low_hbm, low, sem)
    fetch.start()
    inverse = high_ref, low, fetch
    parts, sums = gathered(got_ref, rho_ref.shape[1] // count, count)
    energy, product = lane(dots_ref[...], 0), lane(dots_ref[...], 1)
    alpha = product / sums[0]
    old = old_ref[...]
    new_answer_ref[...] = answer_ref[...] + alpha * old
    resid = resid_ref[...] - alpha * image_ref[...]
    new_resid_ref[...] = resid
    energy = energy - alpha * (2.0 * sums[1] - alpha * sums[2])
    parts = [
        rho_ref[:, h * count : (h + 1) * count] - alpha * (part * factor) for h, part in enumerate(parts)
    ]
    fresh, fine = next_direction(parity_ref, parts, inverse, resid, scale_ref[...], energy, factor)
    direction = fine + fresh / product * old
    dir_ref[...] = direction
    for p in range(send_ref.shape[0]):
        send_ref[p] = direction.astype(bf16)
    for h, part in enumerate(parts):
        new_rho_ref[:, h * count : (h + 1) * count] = part
    at = lax.broadcasted_iota(jnp.int32, dots_ref.shape, 1)
    new_dots_ref[...] = jnp.where(at == 0, energy, jnp.where(at == 1, fresh, 0.0))


def run_coarse(kernel, factor, n_dp, parity, *operands, more=0):
    rows, count = operands[3].shape
    n = operands[1].shape[0]
    vmem = pl.BlockSpec(memory_space=pltpu.VMEM)
    wide = jax.ShapeDtypeStruct((rows, count), f32)
    outs = [
        wide,
        jax.ShapeDtypeStruct((n_dp, rows, count), bf16),
        jax.ShapeDtypeStruct((rows, n), f32),
        jax.ShapeDtypeStruct((rows, SLOTS), f32),
    ] + [wide] * more
    return pl.pallas_call(
        functools.partial(kernel, factor),
        out_shape=outs,
        in_specs=[pl.BlockSpec(memory_space=pltpu.SMEM), vmem, vmem, pl.BlockSpec(memory_space=pl.ANY)]
        + [vmem] * (len(operands) - 3),
        out_specs=[vmem] * len(outs),
        scratch_shapes=[pltpu.VMEM((n, n), bf16), pltpu.SemaphoreType.DMA],
        compiler_params=pltpu.CompilerParams(vmem_limit_bytes=50 * 1024 * 1024),
        cost_estimate=pl.CostEstimate(flops=10**8, bytes_accessed=5 * 2**20, transcendentals=0),
    )(parity, *operands)


def triple(value):
    high = lax.reduce_precision(value, 8, 7)
    mid = lax.reduce_precision(value - high, 8, 7)
    return jnp.stack([high, mid, value - high - mid], -1).astype(bf16)


def rounded(value):
    return lax.reduce_precision(value, 8, 7).astype(bf16)


def slots(values):
    parts = triple(values)
    flat = parts.reshape(parts.shape[:-2] + (-1,))
    return jnp.pad(flat, ((0, 0),) * (flat.ndim - 1) + ((0, SLOTS - flat.shape[-1]),))


def body(samples, projections, targets, feature_scale, coarse_factor):
    n_dp, n_sk = lax.axis_size("dp"), lax.axis_size("sketch")
    count = projections.shape[2]
    width = targets.shape[1]
    mine = width // n_dp
    cols = width // n_sk
    factor = 1.0 / math.sqrt(F // K)
    halves = K // count
    parity = (lax.axis_index("sketch") % halves).astype(jnp.int32).reshape(1)
    n = samples.shape[0]
    scale = feature_scale[None, :]

    chips = n_dp // 2
    core = (lax.axis_index("dp") % 2).astype(jnp.int32).reshape(1)
    mine_proj = lax.all_to_all(
        repeat(projections, chips),
        "dp",
        0,
        0,
        axis_index_groups=[[2 * z + c for z in range(chips)] for c in range(2)],
    )
    other_proj = lax.ppermute(mine_proj, "dp", [(i, i ^ 1) for i in range(n_dp)])
    feat, part, order = make_features(core, samples, mine_proj, other_proj, targets.T, n_dp)

    def scatter_dp(value):
        return jnp.sum(lax.all_to_all(value, "dp", 0, 0), 0)

    def gather_sk(value):
        return lax.all_to_all(jnp.broadcast_to(value[None], (n_sk,) + value.shape), "sketch", 0, 0)

    def everywhere(value, dots):
        return gather_sk(jnp.concatenate([value.astype(bf16), slots(dots)], 1))

    def forward(send):
        whole = lax.all_to_all(send, "dp", 0, 0).reshape(width, count)
        sums = lax.dot_general(whole, feat, (((1,), (1,)), ((), ())), preferred_element_type=f32)
        return whole, sums.astype(bf16).reshape(n_sk, cols, n)

    blocks = block_inverses(order, coarse_factor)
    resid = scatter_dp(part)
    inv_high, inv_low = coarse_inverse(blocks, coarse_factor, resid)
    got = everywhere(resid, row_sum(scale * resid * resid))
    direction, send, rho, dots = run_coarse(
        first_kernel, factor, n_dp, parity, got, inv_high, inv_low, resid, scale
    )
    answer = jnp.zeros_like(resid)
    for step in range(ITERS - 1):
        _, sums = forward(send)
        u = rounded(jnp.sum(lax.all_to_all(sums, "sketch", 0, 0).astype(f32), 0))
        whole = gather_sk(u).reshape(width, n)
        image = scatter_dp(dot(whole, feat).reshape(n_dp, mine, count)) + RIDGE * direction
        weighted = scale * image
        got = everywhere(
            image,
            jnp.concatenate(
                [row_sum(direction * image), row_sum(weighted * resid), row_sum(weighted * image)], 1
            ),
        )
        direction, send, rho, dots, resid, answer = run_coarse(
            step_kernel, factor, n_dp, parity, got, inv_high, inv_low, resid, scale, image, direction, rho, dots, answer,
            more=2,
        )
    whole, sums = forward(send)
    squares = jnp.sum(jnp.square(whole.astype(f32)), 1).reshape(n_sk, cols, 1)
    got = lax.all_to_all(jnp.concatenate([sums, slots(squares)], 2), "sketch", 0, 0).astype(f32)
    total = jnp.sum(got, 0)
    u = rounded(total[:, :n])
    curve = row_sum(total[:, :n] * u.astype(f32)) + (RIDGE / n_dp) * row_sum(total[:, n:])
    got = gather_sk(jnp.concatenate([u, slots(curve)], 1)).reshape(width, n + SLOTS)
    image = dot(got[:, :n], feat)
    sent = jnp.concatenate([image.astype(bf16), got[:, n:]], 1)
    got = lax.all_to_all(sent.reshape(n_dp, mine, count + SLOTS), "dp", 0, 0).astype(f32)
    total = jnp.sum(got, 0)
    image = total[:, :count] + RIDGE * direction
    alpha = dots[:, 1:2] / row_sum(total[:, count:])
    out = jnp.stack([answer + alpha * direction, resid - alpha * image]).astype(bf16)
    got = lax.all_to_all(jnp.broadcast_to(out[None], (n_dp,) + out.shape), "dp", 0, 0)
    answer, resid = outputs(got)
    return answer.T, resid.T


def solution(mesh):
    placed = (P("dp", None), P(None, "dp", "sketch"), P("dp", None), P("sketch"), P())
    return jax.shard_map(
        body,
        mesh=mesh,
        in_specs=placed,
        out_specs=(P("sketch", None), P("sketch", None)),
        check_vma=False,
    )
```

```python
import functools
import math

import jax
import jax.numpy as jnp
from jax import lax
from jax.experimental import pallas as pl
from jax.experimental.pallas import tpu as pltpu
from jax.sharding import PartitionSpec as P

F = 16384
K = 1024
ITERS = 2
RIDGE = 0.5

f32 = jnp.float32
bf16 = jnp.bfloat16


def split(value):
    high = value.astype(bf16)
    return high, (value - high.astype(f32)).astype(bf16)


def dot(a, b):
    return lax.dot_general(a, b, (((1,), (0,)), ((), ())), preferred_element_type=f32)


def dot3(a, b):
    ah, al = split(a)
    bh, bl = split(b)
    return dot(ah, bh) + (dot(ah, bl) + dot(al, bh))


def dot2_left(a, exact):
    ah, al = split(a)
    return dot(ah, exact) + dot(al, exact)


def dot2_right(exact, b):
    bh, bl = split(b)
    return dot(exact, bh) + dot(exact, bl)


BLOCK = 256
DP = ("z", "core")


def inverse_kernel(core_ref, lower_hbm, high_ref, low_ref, made_ref, lower, inv, sems):
    n = lower.shape[0]
    blocks = n // BLOCK
    spans = [pl.ds(b * BLOCK, BLOCK) for b in range(blocks)]
    parts = [(span, span) for span in spans]
    size = BLOCK
    while size < n:
        parts += [(pl.ds(at + size, size), pl.ds(at, size)) for at in range(0, n, 2 * size)]
        size *= 2
    copies = [
        pltpu.make_async_copy(lower_hbm.at[part], lower.at[part], sems.at[k]) for k, part in enumerate(parts)
    ]
    for copy in copies:
        copy.start()
    made_ref[0] = core_ref[0]
    inv[...] = jnp.zeros_like(inv)
    rows = lax.broadcasted_iota(jnp.int32, (BLOCK, BLOCK), 0)
    cols = lax.broadcasted_iota(jnp.int32, (BLOCK, BLOCK), 1)

    def below(k):
        return ((rows >> k) == (cols >> k) + 1) & ((rows >> (k + 1)) == (cols >> (k + 1)))

    for copy, span in zip(copies, spans):
        copy.wait()
        block = lower[span, span].astype(f32)
        diag = jnp.where(rows == cols, block, 0.0)
        down = 1.0 / jnp.sum(diag, axis=1, keepdims=True)
        across = 1.0 / jnp.sum(diag, axis=0, keepdims=True)
        inv[span, span] = jnp.where(rows == cols, down, jnp.where(below(0), -(block * down) * across, 0.0))

    def level(k, carry):
        mask = below(k)
        for span in spans:
            x = inv[span, span]
            off = jnp.where(mask, lower[span, span].astype(f32), 0.0).astype(bf16)
            inv[span, span] = x - dot3(dot2_left(x, off), x)
        return carry

    lax.fori_loop(1, int(math.log2(BLOCK)), level, 0)
    for copy, (bottom, top) in list(zip(copies, parts))[blocks:]:
        copy.wait()
        a, b = inv[top, top], inv[bottom, bottom]
        inv[bottom, top] = -dot3(b, dot2_right(lower[bottom, top], a))
    for span in spans:
        high_ref[span, :], low_ref[span, :] = split(inv[span, :])


def coarse_factor_inverse(core, lower):
    n = lower.shape[0]
    vmem = pl.BlockSpec(memory_space=pltpu.VMEM)
    return pl.pallas_call(
        inverse_kernel,
        out_shape=[jax.ShapeDtypeStruct((n, n), bf16)] * 2 + [jax.ShapeDtypeStruct((1,), jnp.int32)],
        in_specs=[pl.BlockSpec(memory_space=pltpu.SMEM), pl.BlockSpec(memory_space=pl.ANY)],
        out_specs=[vmem] * 2 + [pl.BlockSpec(memory_space=pltpu.SMEM)],
        scratch_shapes=[
            pltpu.VMEM((n, n), bf16),
            pltpu.VMEM((n, n), f32),
            pltpu.SemaphoreType.DMA((2 * (n // BLOCK) - 1,)),
        ],
        compiler_params=pltpu.CompilerParams(vmem_limit_bytes=56 * 1024 * 1024),
        cost_estimate=pl.CostEstimate(flops=10**10, bytes_accessed=6 * 2**20, transcendentals=0),
    )(core, lower)


def product_kernel(xh_ref, xl_ref, order_hbm, high_ref, low_ref):
    del order_hbm
    spans = [slice(b, b + BLOCK) for b in range(0, xh_ref.shape[0], BLOCK)]
    parts = [[(xh_ref[row, col], xl_ref[row, col]) for col in spans[: r + 1]] for r, row in enumerate(spans)]
    turned = [[tuple(half.astype(f32).T.astype(bf16) for half in part) for part in row] for row in parts]
    for a, row in enumerate(spans):
        for b, col in enumerate(spans):
            total = None
            for k in range(max(a, b), len(spans)):
                (ah, al), (bh, bl) = turned[k][a], parts[k][b]
                term = dot(ah, bh) + (dot(ah, bl) + dot(al, bh))
                total = term if total is None else total + term
            high_ref[row, col], low_ref[row, col] = split(total)


def coarse_inverse(xh, xl, order):
    n = xh.shape[0]
    vmem = pl.BlockSpec(memory_space=pltpu.VMEM)
    return pl.pallas_call(
        product_kernel,
        out_shape=[jax.ShapeDtypeStruct((n, n), bf16)] * 2,
        in_specs=[vmem, vmem, pl.BlockSpec(memory_space=pl.ANY)],
        out_specs=[vmem] * 2,
        compiler_params=pltpu.CompilerParams(vmem_limit_bytes=50 * 1024 * 1024),
        cost_estimate=pl.CostEstimate(flops=4 * 10**9, bytes_accessed=8 * 2**20, transcendentals=0),
    )(xh, xl, order)


def repeat_kernel(value_ref, out_ref):
    for p in range(out_ref.shape[0]):
        out_ref[p] = value_ref[...]


def repeat(value, count):
    vmem = pl.BlockSpec(memory_space=pltpu.VMEM)
    return pl.pallas_call(
        repeat_kernel,
        out_shape=jax.ShapeDtypeStruct((count,) + value.shape, value.dtype),
        in_specs=[vmem],
        out_specs=vmem,
        compiler_params=pltpu.CompilerParams(vmem_limit_bytes=8 * 1024 * 1024),
    )(value)


def output_kernel(got_ref, answer_ref, resid_ref):
    rows = got_ref.shape[2]
    for p in range(got_ref.shape[0]):
        answer_ref[p * rows : (p + 1) * rows, :] = got_ref[p, 0].astype(f32)
        resid_ref[p * rows : (p + 1) * rows, :] = got_ref[p, 1].astype(f32)


def outputs(got):
    parts, _, rows, count = got.shape
    vmem = pl.BlockSpec(memory_space=pltpu.VMEM)
    return pl.pallas_call(
        output_kernel,
        out_shape=[jax.ShapeDtypeStruct((parts * rows, count), f32)] * 2,
        in_specs=[vmem],
        out_specs=[vmem] * 2,
    )(got)


ROWS = 1024


def feature_kernel(
    core_ref, samples_hbm, mine_hbm, other_hbm, targets_hbm, feat_ref, part_ref, samples, proj, targets, acc, sems
):
    n, parts, panels = samples.shape[0], part_ref.shape[0], proj.shape[0]
    core, rows = core_ref[0], min(ROWS, n)
    get_samples = pltpu.make_async_copy(samples_hbm, samples, sems.at[0])
    get_targets = pltpu.make_async_copy(targets_hbm, targets, sems.at[1])
    get_proj = [
        [
            pltpu.make_async_copy(half.at[:, j], proj.at[j, :, at], sems.at[2 + 2 * j + k])
            for k, (half, at) in enumerate(((mine_hbm, core), (other_hbm, 1 - core)))
        ]
        for j in range(panels)
    ]
    for copy in [get_samples] + sum(get_proj, []) + [get_targets]:
        copy.start()
    get_samples.wait()
    total = None
    for j in range(panels):
        for copy in get_proj[j]:
            copy.wait()
        panel = proj[j].reshape(samples.shape[1], proj.shape[-1])
        if j == panels - 1:
            get_targets.wait()
        for at in range(0, n, rows):
            value = dot(samples[at : at + rows, :], panel)
            if j:
                value = acc[at : at + rows, :] * value
            if j < panels - 1:
                acc[at : at + rows, :] = value
            else:
                feat = (value * (1.0 / math.sqrt(F))).astype(bf16)
                feat_ref[at : at + rows, :] = feat
                term = dot(targets[:, at : at + rows], feat)
                total = term if total is None else total + term
    step = total.shape[0] // parts
    for p in range(parts):
        part_ref[p] = total[p * step : (p + 1) * step, :]


def make_features(core, samples, mine, other, targets_t, parts):
    n = samples.shape[0]
    chips, panels, rows, width = mine.shape
    return pl.pallas_call(
        feature_kernel,
        out_shape=[
            jax.ShapeDtypeStruct((n, width), bf16),
            jax.ShapeDtypeStruct((parts, targets_t.shape[0] // parts, width), f32),
        ],
        in_specs=[pl.BlockSpec(memory_space=pltpu.SMEM)] + [pl.BlockSpec(memory_space=pl.ANY)] * 4,
        out_specs=[pl.BlockSpec(memory_space=pltpu.VMEM)] * 2,
        scratch_shapes=[
            pltpu.VMEM(samples.shape, bf16),
            pltpu.VMEM((panels, chips, 2, rows, width), bf16),
            pltpu.VMEM(targets_t.shape, bf16),
            pltpu.VMEM((n, width), f32),
            pltpu.SemaphoreType.DMA((2 + 2 * panels,)),
        ],
        compiler_params=pltpu.CompilerParams(vmem_limit_bytes=50 * 1024 * 1024),
        cost_estimate=pl.CostEstimate(flops=2 * 10**9, bytes_accessed=5 * 2**20, transcendentals=0),
    )(core, samples, mine, other, targets_t)


SLOTS = 128


def row_sum(value):
    return jnp.sum(value, axis=1, keepdims=True)


def lane(value, k):
    at = lax.broadcasted_iota(jnp.int32, value.shape, 1)
    return row_sum(jnp.where(at == k, value, 0.0))


def gathered(got_ref, halves, count):
    parts = []
    for h in range(halves):
        acc = got_ref[h, :, :count].astype(f32)
        for p in range(h + halves, got_ref.shape[0], halves):
            acc = acc + got_ref[p, :, :count].astype(f32)
        parts.append(acc)
    dots = got_ref[0, :, count:].astype(f32)
    for p in range(1, got_ref.shape[0]):
        dots = dots + got_ref[p, :, count:].astype(f32)
    at = lax.broadcasted_iota(jnp.int32, dots.shape, 1)
    sums = [row_sum(jnp.where((at >= 3 * k) & (at < 3 * k + 3), dots, 0.0)) for k in range(3)]
    return parts, sums


def coarse(parts, inverse):
    high_ref, low_ref, copy = inverse
    rows, total, left = parts[0].shape[0], None, []
    for h, part in enumerate(parts):
        span = slice(h * part.shape[1], (h + 1) * part.shape[1])
        high = part.astype(bf16).astype(f32)
        both = jnp.concatenate([high, part - high], 0).astype(bf16)
        one = dot(both, high_ref[span, :])
        term = one[:rows] + one[rows:]
        total = term if total is None else total + term
        left.append((span, both))
    copy.wait()
    for span, both in left:
        total = total + dot(both, low_ref[span, :])[:rows]
    return total


def next_direction(parity_ref, parts, inverse, resid, scale, energy, factor):
    count = resid.shape[1]
    solved = coarse(parts, inverse)
    product = energy
    mine = solved[:, :count]
    for h, part in enumerate(parts):
        here = solved[:, h * count : (h + 1) * count]
        product = product + row_sum(part * here)
        if h:
            mine = jnp.where(parity_ref[0] == h, here, mine)
    return product, scale * resid + factor * mine


def first_kernel(
    factor, parity_ref, got_ref, high_ref, low_hbm, resid_ref, scale_ref, dir_ref, send_ref, rho_ref, dots_ref, low, sem
):
    count = resid_ref.shape[1]
    fetch = pltpu.make_async_copy(low_hbm, low, sem)
    fetch.start()
    inverse = high_ref, low, fetch
    parts, sums = gathered(got_ref, rho_ref.shape[1] // count, count)
    parts = [part * factor for part in parts]
    product, direction = next_direction(
        parity_ref, parts, inverse, resid_ref[...], scale_ref[...], sums[0], factor
    )
    dir_ref[...] = direction
    for p in range(send_ref.shape[0]):
        send_ref[p] = direction.astype(bf16)
    for h, part in enumerate(parts):
        rho_ref[:, h * count : (h + 1) * count] = part
    at = lax.broadcasted_iota(jnp.int32, dots_ref.shape, 1)
    dots_ref[...] = jnp.where(at == 0, sums[0], jnp.where(at == 1, product, 0.0))


def step_kernel(
    factor, parity_ref, got_ref, high_ref, low_hbm, resid_ref, scale_ref, image_ref, old_ref, rho_ref, dots_ref, answer_ref,
    dir_ref, send_ref, new_rho_ref, new_dots_ref, new_resid_ref, new_answer_ref, low, sem,
):
    count = resid_ref.shape[1]
    fetch = pltpu.make_async_copy(low_hbm, low, sem)
    fetch.start()
    inverse = high_ref, low, fetch
    parts, sums = gathered(got_ref, rho_ref.shape[1] // count, count)
    energy, product = lane(dots_ref[...], 0), lane(dots_ref[...], 1)
    alpha = product / sums[0]
    old = old_ref[...]
    new_answer_ref[...] = answer_ref[...] + alpha * old
    resid = resid_ref[...] - alpha * image_ref[...]
    new_resid_ref[...] = resid
    energy = energy - alpha * (2.0 * sums[1] - alpha * sums[2])
    parts = [
        rho_ref[:, h * count : (h + 1) * count] - alpha * (part * factor) for h, part in enumerate(parts)
    ]
    fresh, fine = next_direction(parity_ref, parts, inverse, resid, scale_ref[...], energy, factor)
    direction = fine + fresh / product * old
    dir_ref[...] = direction
    for p in range(send_ref.shape[0]):
        send_ref[p] = direction.astype(bf16)
    for h, part in enumerate(parts):
        new_rho_ref[:, h * count : (h + 1) * count] = part
    at = lax.broadcasted_iota(jnp.int32, dots_ref.shape, 1)
    new_dots_ref[...] = jnp.where(at == 0, energy, jnp.where(at == 1, fresh, 0.0))


def run_coarse(kernel, factor, n_dp, parity, *operands, more=0):
    rows, count = operands[3].shape
    n = operands[1].shape[0]
    vmem = pl.BlockSpec(memory_space=pltpu.VMEM)
    wide = jax.ShapeDtypeStruct((rows, count), f32)
    outs = [
        wide,
        jax.ShapeDtypeStruct((n_dp, rows, count), bf16),
        jax.ShapeDtypeStruct((rows, n), f32),
        jax.ShapeDtypeStruct((rows, SLOTS), f32),
    ] + [wide] * more
    return pl.pallas_call(
        functools.partial(kernel, factor),
        out_shape=outs,
        in_specs=[pl.BlockSpec(memory_space=pltpu.SMEM), vmem, vmem, pl.BlockSpec(memory_space=pl.ANY)]
        + [vmem] * (len(operands) - 3),
        out_specs=[vmem] * len(outs),
        scratch_shapes=[pltpu.VMEM((n, n), bf16), pltpu.SemaphoreType.DMA],
        compiler_params=pltpu.CompilerParams(vmem_limit_bytes=50 * 1024 * 1024),
        cost_estimate=pl.CostEstimate(flops=10**8, bytes_accessed=5 * 2**20, transcendentals=0),
    )(parity, *operands)


def triple(value):
    high = lax.reduce_precision(value, 8, 7)
    mid = lax.reduce_precision(value - high, 8, 7)
    return jnp.stack([high, mid, value - high - mid], -1).astype(bf16)


def rounded(value):
    return lax.reduce_precision(value, 8, 7).astype(bf16)


def slots(values):
    parts = triple(values)
    flat = parts.reshape(parts.shape[:-2] + (-1,))
    return jnp.pad(flat, ((0, 0),) * (flat.ndim - 1) + ((0, SLOTS - flat.shape[-1]),))


def body(samples, projections, targets, feature_scale, coarse_factor):
    n_dp, n_sk = lax.axis_size(DP), lax.axis_size("sketch")
    count = projections.shape[2]
    width = targets.shape[1]
    mine = width // n_dp
    cols = width // n_sk
    factor = 1.0 / math.sqrt(F // K)
    halves = K // count
    parity = (lax.axis_index("sketch") % halves).astype(jnp.int32).reshape(1)
    n = samples.shape[0]
    scale = feature_scale[None, :]

    core = lax.axis_index("core").astype(jnp.int32).reshape(1)
    mine_proj = lax.all_to_all(repeat(projections, lax.axis_size("z")), "z", 0, 0)
    factor_high, factor_low, core = coarse_factor_inverse(core, coarse_factor)
    mine_proj, core = lax.optimization_barrier((mine_proj, core))
    other_proj = lax.ppermute(mine_proj, "core", [(0, 1), (1, 0)])
    feat, part = make_features(core, samples, mine_proj, other_proj, targets.T, n_dp)

    def scatter_dp(value):
        return jnp.sum(lax.all_to_all(value, DP, 0, 0), 0)

    def gather_sk(value):
        return lax.all_to_all(jnp.broadcast_to(value[None], (n_sk,) + value.shape), "sketch", 0, 0)

    def everywhere(value, dots):
        return gather_sk(jnp.concatenate([value.astype(bf16), slots(dots)], 1))

    def forward(send):
        whole = lax.all_to_all(send, DP, 0, 0).reshape(width, count)
        sums = lax.dot_general(whole, feat, (((1,), (1,)), ((), ())), preferred_element_type=f32)
        return whole, sums.astype(bf16).reshape(n_sk, cols, n)

    resid = scatter_dp(part)
    inv_high, inv_low = coarse_inverse(factor_high, factor_low, resid)
    got = everywhere(resid, row_sum(scale * resid * resid))
    direction, send, rho, dots = run_coarse(
        first_kernel, factor, n_dp, parity, got, inv_high, inv_low, resid, scale
    )
    answer = jnp.zeros_like(resid)
    for step in range(ITERS - 1):
        _, sums = forward(send)
        u = rounded(jnp.sum(lax.all_to_all(sums, "sketch", 0, 0).astype(f32), 0))
        whole = gather_sk(u).reshape(width, n)
        image = scatter_dp(dot(whole, feat).reshape(n_dp, mine, count)) + RIDGE * direction
        weighted = scale * image
        got = everywhere(
            image,
            jnp.concatenate(
                [row_sum(direction * image), row_sum(weighted * resid), row_sum(weighted * image)], 1
            ),
        )
        direction, send, rho, dots, resid, answer = run_coarse(
            step_kernel, factor, n_dp, parity, got, inv_high, inv_low, resid, scale, image, direction, rho, dots, answer,
            more=2,
        )
    whole, sums = forward(send)
    squares = jnp.sum(jnp.square(whole.astype(f32)), 1).reshape(n_sk, cols, 1)
    got = lax.all_to_all(jnp.concatenate([sums, slots(squares)], 2), "sketch", 0, 0).astype(f32)
    total = jnp.sum(got, 0)
    u = rounded(total[:, :n])
    curve = row_sum(total[:, :n] * u.astype(f32)) + (RIDGE / n_dp) * row_sum(total[:, n:])
    got = gather_sk(jnp.concatenate([u, slots(curve)], 1)).reshape(width, n + SLOTS)
    image = dot(got[:, :n], feat)
    sent = jnp.concatenate([image.astype(bf16), got[:, n:]], 1)
    got = lax.all_to_all(sent.reshape(n_dp, mine, count + SLOTS), DP, 0, 0).astype(f32)
    total = jnp.sum(got, 0)
    image = total[:, :count] + RIDGE * direction
    alpha = dots[:, 1:2] / row_sum(total[:, count:])
    out = jnp.stack([answer + alpha * direction, resid - alpha * image]).astype(bf16)
    got = lax.all_to_all(jnp.broadcast_to(out[None], (n_dp,) + out.shape), DP, 0, 0)
    answer, resid = outputs(got)
    return answer.T, resid.T


def solution(mesh):
    chips = mesh.shape["dp"] // 2
    mesh = jax.sharding.Mesh(mesh.devices.reshape(chips, 2, -1), ("z", "core", "sketch"))
    placed = (P(DP, None), P(None, DP, "sketch"), P(DP, None), P("sketch"), P())
    return jax.shard_map(
        body,
        mesh=mesh,
        in_specs=placed,
        out_specs=(P("sketch", None), P("sketch", None)),
        check_vma=False,
    )
```

```python
import functools
import math

import jax
import jax.numpy as jnp
from jax import lax
from jax.experimental import pallas as pl
from jax.experimental.pallas import tpu as pltpu
from jax.sharding import PartitionSpec as P

F = 16384
K = 1024
ITERS = 2
RIDGE = 0.5

f32 = jnp.float32
bf16 = jnp.bfloat16


def split(value):
    high = value.astype(bf16)
    return high, (value - high.astype(f32)).astype(bf16)


def dot(a, b):
    return lax.dot_general(a, b, (((1,), (0,)), ((), ())), preferred_element_type=f32)


def dot_turned(a, b):
    return lax.dot_general(a, b, (((1,), (1,)), ((), ())), preferred_element_type=f32)


def dot3(a, b):
    ah, al = split(a)
    bh, bl = split(b)
    return dot(ah, bh) + (dot(ah, bl) + dot(al, bh))


def dot2_left(a, exact):
    ah, al = split(a)
    return dot(ah, exact) + dot(al, exact)


def dot2_right(exact, b):
    bh, bl = split(b)
    return dot(exact, bh) + dot(exact, bl)


BLOCK = 256
DP = ("z", "core")


def inverse_kernel(core_ref, lower_hbm, high_ref, low_ref, made_ref, lower, inv, sems):
    n = lower.shape[0]
    blocks = n // BLOCK
    spans = [pl.ds(b * BLOCK, BLOCK) for b in range(blocks)]
    parts = [(span, span) for span in spans]
    size = BLOCK
    while size < n:
        parts += [(pl.ds(at + size, size), pl.ds(at, size)) for at in range(0, n, 2 * size)]
        size *= 2
    copies = [
        pltpu.make_async_copy(lower_hbm.at[part], lower.at[part], sems.at[k]) for k, part in enumerate(parts)
    ]
    for copy in copies:
        copy.start()
    made_ref[0] = core_ref[0]
    inv[...] = jnp.zeros_like(inv)
    rows = lax.broadcasted_iota(jnp.int32, (BLOCK, BLOCK), 0)
    cols = lax.broadcasted_iota(jnp.int32, (BLOCK, BLOCK), 1)

    def below(k):
        return ((rows >> k) == (cols >> k) + 1) & ((rows >> (k + 1)) == (cols >> (k + 1)))

    for copy, span in zip(copies, spans):
        copy.wait()
        block = lower[span, span].astype(f32)
        diag = jnp.where(rows == cols, block, 0.0)
        down = 1.0 / jnp.sum(diag, axis=1, keepdims=True)
        across = 1.0 / jnp.sum(diag, axis=0, keepdims=True)
        inv[span, span] = jnp.where(rows == cols, down, jnp.where(below(0), -(block * down) * across, 0.0))

    def level(k, carry):
        mask = below(k)
        for span in spans:
            x = inv[span, span]
            off = jnp.where(mask, lower[span, span].astype(f32), 0.0).astype(bf16)
            inv[span, span] = x - dot3(dot2_left(x, off), x)
        return carry

    lax.fori_loop(1, int(math.log2(BLOCK)), level, 0)
    for copy, (bottom, top) in list(zip(copies, parts))[blocks:]:
        copy.wait()
        a, b = inv[top, top], inv[bottom, bottom]
        inv[bottom, top] = -dot3(b, dot2_right(lower[bottom, top], a))
    for span in spans:
        high_ref[span, :], low_ref[span, :] = split(inv[span, :])


def coarse_factor_inverse(core, lower):
    n = lower.shape[0]
    vmem = pl.BlockSpec(memory_space=pltpu.VMEM)
    return pl.pallas_call(
        inverse_kernel,
        out_shape=[jax.ShapeDtypeStruct((n, n), bf16)] * 2 + [jax.ShapeDtypeStruct((1,), jnp.int32)],
        in_specs=[pl.BlockSpec(memory_space=pltpu.SMEM), pl.BlockSpec(memory_space=pl.ANY)],
        out_specs=[vmem] * 2 + [pl.BlockSpec(memory_space=pltpu.SMEM)],
        scratch_shapes=[
            pltpu.VMEM((n, n), bf16),
            pltpu.VMEM((n, n), f32),
            pltpu.SemaphoreType.DMA((2 * (n // BLOCK) - 1,)),
        ],
        compiler_params=pltpu.CompilerParams(vmem_limit_bytes=56 * 1024 * 1024),
        cost_estimate=pl.CostEstimate(flops=10**10, bytes_accessed=6 * 2**20, transcendentals=0),
    )(core, lower)


def place(a, b):
    return pl.ds((a * (a + 1) // 2 + b) * BLOCK, BLOCK)


def product_kernel(xh_ref, xl_ref, order_hbm, high_ref, low_ref):
    del order_hbm
    spans = [slice(b, b + BLOCK) for b in range(0, xh_ref.shape[0], BLOCK)]
    parts = [[(xh_ref[row, col], xl_ref[row, col]) for col in spans[: r + 1]] for r, row in enumerate(spans)]
    turned = [[tuple(half.astype(f32).T.astype(bf16) for half in part) for part in row] for row in parts]
    for a in range(len(spans)):
        for b in range(a + 1):
            total = None
            for k in range(a, len(spans)):
                (ah, al), (bh, bl) = turned[k][a], parts[k][b]
                term = dot(ah, bh) + (dot(ah, bl) + dot(al, bh))
                total = term if total is None else total + term
            high_ref[place(a, b), :], low_ref[place(a, b), :] = split(total)


def coarse_inverse(xh, xl, order):
    n = xh.shape[0]
    blocks = n // BLOCK
    vmem = pl.BlockSpec(memory_space=pltpu.VMEM)
    return pl.pallas_call(
        product_kernel,
        out_shape=[jax.ShapeDtypeStruct((blocks * (blocks + 1) // 2 * BLOCK, BLOCK), bf16)] * 2,
        in_specs=[vmem, vmem, pl.BlockSpec(memory_space=pl.ANY)],
        out_specs=[vmem] * 2,
        compiler_params=pltpu.CompilerParams(vmem_limit_bytes=52 * 1024 * 1024),
        cost_estimate=pl.CostEstimate(flops=4 * 10**9, bytes_accessed=8 * 2**20, transcendentals=0),
    )(xh, xl, order)


def repeat_kernel(value_ref, out_ref):
    for p in range(out_ref.shape[0]):
        out_ref[p] = value_ref[...]


def repeat(value, count):
    vmem = pl.BlockSpec(memory_space=pltpu.VMEM)
    return pl.pallas_call(
        repeat_kernel,
        out_shape=jax.ShapeDtypeStruct((count,) + value.shape, value.dtype),
        in_specs=[vmem],
        out_specs=vmem,
        compiler_params=pltpu.CompilerParams(vmem_limit_bytes=8 * 1024 * 1024),
    )(value)


def output_kernel(got_ref, answer_ref, resid_ref):
    rows = got_ref.shape[2]
    for p in range(got_ref.shape[0]):
        answer_ref[p * rows : (p + 1) * rows, :] = got_ref[p, 0].astype(f32)
        resid_ref[p * rows : (p + 1) * rows, :] = got_ref[p, 1].astype(f32)


def outputs(got):
    parts, _, rows, count = got.shape
    vmem = pl.BlockSpec(memory_space=pltpu.VMEM)
    return pl.pallas_call(
        output_kernel,
        out_shape=[jax.ShapeDtypeStruct((parts * rows, count), f32)] * 2,
        in_specs=[vmem],
        out_specs=[vmem] * 2,
    )(got)


def feature_kernel(
    core_ref, samples_hbm, mine_ref, other_ref, targets_hbm, feat_ref, part_ref, proj, samples_ref, targets_ref, sems
):
    core = core_ref[0]
    get_samples = pltpu.make_async_copy(samples_hbm, samples_ref, sems.at[0])
    get_targets = pltpu.make_async_copy(targets_hbm, targets_ref, sems.at[1])
    get_samples.start()
    get_targets.start()
    for j in range(proj.shape[0]):
        proj[j, :, core] = mine_ref[:, j]
        proj[j, :, 1 - core] = other_ref[:, j]
    get_samples.wait()
    samples, value = samples_ref[...], None
    for j in range(proj.shape[0]):
        panel = dot(samples, proj[j].reshape(samples.shape[1], proj.shape[-1]))
        value = panel if value is None else value * panel
    feat = (value * (1.0 / math.sqrt(F))).astype(bf16)
    feat_ref[...] = feat
    get_targets.wait()
    total = dot(targets_ref[...], feat)
    step = part_ref.shape[1]
    for p in range(part_ref.shape[0]):
        part_ref[p] = total[p * step : (p + 1) * step, :]


def make_features(core, samples, mine, other, targets_t, parts):
    n = samples.shape[0]
    chips, panels, rows, width = mine.shape
    vmem, anywhere = pl.BlockSpec(memory_space=pltpu.VMEM), pl.BlockSpec(memory_space=pl.ANY)
    return pl.pallas_call(
        feature_kernel,
        out_shape=[
            jax.ShapeDtypeStruct((n, width), bf16),
            jax.ShapeDtypeStruct((parts, targets_t.shape[0] // parts, width), f32),
        ],
        in_specs=[pl.BlockSpec(memory_space=pltpu.SMEM), anywhere, vmem, vmem, anywhere],
        out_specs=[vmem] * 2,
        scratch_shapes=[
            pltpu.VMEM((panels, chips, 2, rows, width), bf16),
            pltpu.VMEM(samples.shape, bf16),
            pltpu.VMEM(targets_t.shape, bf16),
            pltpu.SemaphoreType.DMA((2,)),
        ],
        compiler_params=pltpu.CompilerParams(vmem_limit_bytes=49 * 1024 * 1024),
        cost_estimate=pl.CostEstimate(flops=2 * 10**9, bytes_accessed=5 * 2**20, transcendentals=0),
    )(core, samples, mine, other, targets_t)


SLOTS = 128


def row_sum(value):
    return jnp.sum(value, axis=1, keepdims=True)


def lane(value, k):
    at = lax.broadcasted_iota(jnp.int32, value.shape, 1)
    return row_sum(jnp.where(at == k, value, 0.0))


def gathered(got_ref, halves, count):
    parts = []
    for h in range(halves):
        acc = got_ref[h, :, :count].astype(f32)
        for p in range(h + halves, got_ref.shape[0], halves):
            acc = acc + got_ref[p, :, :count].astype(f32)
        parts.append(acc)
    dots = got_ref[0, :, count:].astype(f32)
    for p in range(1, got_ref.shape[0]):
        dots = dots + got_ref[p, :, count:].astype(f32)
    at = lax.broadcasted_iota(jnp.int32, dots.shape, 1)
    sums = [row_sum(jnp.where((at >= 3 * k) & (at < 3 * k + 3), dots, 0.0)) for k in range(3)]
    return parts, sums


def coarse(parts, inverse):
    high_ref, low_ref, fetch = inverse
    rows, sides = parts[0].shape[0], []
    for part in parts:
        high = part.astype(bf16).astype(f32)
        both = jnp.concatenate([high, part - high], 0).astype(bf16)
        sides += [both[:, at : at + BLOCK] for at in range(0, part.shape[1], BLOCK)]
    blocks = range(len(sides))

    def times(ref, both, a, b):
        return dot(both, ref[place(a, b), :]) if a >= b else dot_turned(both, ref[place(b, a), :])

    solved = []
    for b in blocks:
        one = sum(times(high_ref, sides[a], a, b) for a in blocks)
        solved.append(one[:rows] + one[rows:])
    fetch.wait()
    for b in blocks:
        solved[b] = solved[b] + sum(times(low_ref, sides[a], a, b) for a in blocks)[:rows]
    return jnp.concatenate(solved, 1)


def next_direction(parity_ref, parts, inverse, resid, scale, energy, factor):
    count = resid.shape[1]
    solved = coarse(parts, inverse)
    product = energy
    mine = solved[:, :count]
    for h, part in enumerate(parts):
        here = solved[:, h * count : (h + 1) * count]
        product = product + row_sum(part * here)
        if h:
            mine = jnp.where(parity_ref[0] == h, here, mine)
    return product, scale * resid + factor * mine


def first_kernel(
    factor, parity_ref, got_ref, high_ref, low_hbm, resid_ref, scale_ref, dir_ref, send_ref, rho_ref, dots_ref, low, sem
):
    count = resid_ref.shape[1]
    fetch = pltpu.make_async_copy(low_hbm, low, sem)
    fetch.start()
    inverse = high_ref, low, fetch
    parts, sums = gathered(got_ref, rho_ref.shape[1] // count, count)
    parts = [part * factor for part in parts]
    product, direction = next_direction(
        parity_ref, parts, inverse, resid_ref[...], scale_ref[...], sums[0], factor
    )
    dir_ref[...] = direction
    for p in range(send_ref.shape[0]):
        send_ref[p] = direction.astype(bf16)
    for h, part in enumerate(parts):
        rho_ref[:, h * count : (h + 1) * count] = part
    at = lax.broadcasted_iota(jnp.int32, dots_ref.shape, 1)
    dots_ref[...] = jnp.where(at == 0, sums[0], jnp.where(at == 1, product, 0.0))


def step_kernel(
    factor, parity_ref, got_ref, high_ref, low_hbm, resid_ref, scale_ref, image_ref, old_ref, rho_ref, dots_ref, answer_ref,
    dir_ref, send_ref, new_rho_ref, new_dots_ref, new_resid_ref, new_answer_ref, low, sem,
):
    count = resid_ref.shape[1]
    fetch = pltpu.make_async_copy(low_hbm, low, sem)
    fetch.start()
    inverse = high_ref, low, fetch
    parts, sums = gathered(got_ref, rho_ref.shape[1] // count, count)
    energy, product = lane(dots_ref[...], 0), lane(dots_ref[...], 1)
    alpha = product / sums[0]
    old = old_ref[...]
    new_answer_ref[...] = answer_ref[...] + alpha * old
    resid = resid_ref[...] - alpha * image_ref[...]
    new_resid_ref[...] = resid
    energy = energy - alpha * (2.0 * sums[1] - alpha * sums[2])
    parts = [
        rho_ref[:, h * count : (h + 1) * count] - alpha * (part * factor) for h, part in enumerate(parts)
    ]
    fresh, fine = next_direction(parity_ref, parts, inverse, resid, scale_ref[...], energy, factor)
    direction = fine + fresh / product * old
    dir_ref[...] = direction
    for p in range(send_ref.shape[0]):
        send_ref[p] = direction.astype(bf16)
    for h, part in enumerate(parts):
        new_rho_ref[:, h * count : (h + 1) * count] = part
    at = lax.broadcasted_iota(jnp.int32, dots_ref.shape, 1)
    new_dots_ref[...] = jnp.where(at == 0, energy, jnp.where(at == 1, fresh, 0.0))


def run_coarse(kernel, factor, n_dp, parity, *operands, more=0):
    rows, count = operands[3].shape
    vmem = pl.BlockSpec(memory_space=pltpu.VMEM)
    wide = jax.ShapeDtypeStruct((rows, count), f32)
    outs = [
        wide,
        jax.ShapeDtypeStruct((n_dp, rows, count), bf16),
        jax.ShapeDtypeStruct((rows, K), f32),
        jax.ShapeDtypeStruct((rows, SLOTS), f32),
    ] + [wide] * more
    return pl.pallas_call(
        functools.partial(kernel, factor),
        out_shape=outs,
        in_specs=[pl.BlockSpec(memory_space=pltpu.SMEM), vmem, vmem, pl.BlockSpec(memory_space=pl.ANY)]
        + [vmem] * (len(operands) - 3),
        out_specs=[vmem] * len(outs),
        scratch_shapes=[pltpu.VMEM(operands[2].shape, bf16), pltpu.SemaphoreType.DMA],
        compiler_params=pltpu.CompilerParams(vmem_limit_bytes=52 * 1024 * 1024),
        cost_estimate=pl.CostEstimate(flops=10**8, bytes_accessed=5 * 2**20, transcendentals=0),
    )(parity, *operands)


def triple(value):
    high = lax.reduce_precision(value, 8, 7)
    mid = lax.reduce_precision(value - high, 8, 7)
    return jnp.stack([high, mid, value - high - mid], -1).astype(bf16)


def rounded(value):
    return lax.reduce_precision(value, 8, 7).astype(bf16)


def slots(values):
    parts = triple(values)
    flat = parts.reshape(parts.shape[:-2] + (-1,))
    return jnp.pad(flat, ((0, 0),) * (flat.ndim - 1) + ((0, SLOTS - flat.shape[-1]),))


def body(samples, projections, targets, feature_scale, coarse_factor):
    n_dp, n_sk = lax.axis_size(DP), lax.axis_size("sketch")
    count = projections.shape[2]
    width = targets.shape[1]
    mine = width // n_dp
    cols = width // n_sk
    factor = 1.0 / math.sqrt(F // K)
    halves = K // count
    parity = (lax.axis_index("sketch") % halves).astype(jnp.int32).reshape(1)
    n = samples.shape[0]
    scale = feature_scale[None, :]

    core = lax.axis_index("core").astype(jnp.int32).reshape(1)
    mine_proj = lax.all_to_all(repeat(projections, lax.axis_size("z")), "z", 0, 0)
    factor_high, factor_low, core = coarse_factor_inverse(core, coarse_factor)
    mine_proj, core = lax.optimization_barrier((mine_proj, core))
    other_proj = lax.ppermute(mine_proj, "core", [(0, 1), (1, 0)])
    feat, part = make_features(core, samples, mine_proj, other_proj, targets.T, n_dp)

    def scatter_dp(value):
        return jnp.sum(lax.all_to_all(value, DP, 0, 0), 0)

    def gather_sk(value):
        return lax.all_to_all(jnp.broadcast_to(value[None], (n_sk,) + value.shape), "sketch", 0, 0)

    def everywhere(value, dots):
        return gather_sk(jnp.concatenate([value.astype(bf16), slots(dots)], 1))

    def forward(send):
        whole = lax.all_to_all(send, DP, 0, 0).reshape(width, count)
        sums = lax.dot_general(whole, feat, (((1,), (1,)), ((), ())), preferred_element_type=f32)
        return whole, sums.astype(bf16).reshape(n_sk, cols, n)

    resid = scatter_dp(part)
    inv_high, inv_low = coarse_inverse(factor_high, factor_low, resid)
    got = everywhere(resid, row_sum(scale * resid * resid))
    direction, send, rho, dots = run_coarse(
        first_kernel, factor, n_dp, parity, got, inv_high, inv_low, resid, scale
    )
    answer = jnp.zeros_like(resid)
    for step in range(ITERS - 1):
        _, sums = forward(send)
        u = rounded(jnp.sum(lax.all_to_all(sums, "sketch", 0, 0).astype(f32), 0))
        whole = gather_sk(u).reshape(width, n)
        image = scatter_dp(dot(whole, feat).reshape(n_dp, mine, count)) + RIDGE * direction
        weighted = scale * image
        got = everywhere(
            image,
            jnp.concatenate(
                [row_sum(direction * image), row_sum(weighted * resid), row_sum(weighted * image)], 1
            ),
        )
        direction, send, rho, dots, resid, answer = run_coarse(
            step_kernel, factor, n_dp, parity, got, inv_high, inv_low, resid, scale, image, direction, rho, dots, answer,
            more=2,
        )
    whole, sums = forward(send)
    squares = jnp.sum(jnp.square(whole.astype(f32)), 1).reshape(n_sk, cols, 1)
    got = lax.all_to_all(jnp.concatenate([sums, slots(squares)], 2), "sketch", 0, 0).astype(f32)
    total = jnp.sum(got, 0)
    u = rounded(total[:, :n])
    curve = row_sum(total[:, :n] * u.astype(f32)) + (RIDGE / n_dp) * row_sum(total[:, n:])
    got = gather_sk(jnp.concatenate([u, slots(curve)], 1)).reshape(width, n + SLOTS)
    image = dot(got[:, :n], feat)
    sent = jnp.concatenate([image.astype(bf16), got[:, n:]], 1)
    got = lax.all_to_all(sent.reshape(n_dp, mine, count + SLOTS), DP, 0, 0).astype(f32)
    total = jnp.sum(got, 0)
    image = total[:, :count] + RIDGE * direction
    alpha = dots[:, 1:2] / row_sum(total[:, count:])
    out = jnp.stack([answer + alpha * direction, resid - alpha * image]).astype(bf16)
    got = lax.all_to_all(jnp.broadcast_to(out[None], (n_dp,) + out.shape), DP, 0, 0)
    answer, resid = outputs(got)
    return answer.T, resid.T


def solution(mesh):
    chips = mesh.shape["dp"] // 2
    mesh = jax.sharding.Mesh(mesh.devices.reshape(chips, 2, -1), ("z", "core", "sketch"))
    placed = (P(DP, None), P(None, DP, "sketch"), P(DP, None), P("sketch"), P())
    return jax.shard_map(
        body,
        mesh=mesh,
        in_specs=placed,
        out_specs=(P("sketch", None), P("sketch", None)),
        check_vma=False,
    )
```

```python
import functools
import math

import jax
import jax.numpy as jnp
from jax import lax
from jax.experimental import pallas as pl
from jax.experimental.pallas import tpu as pltpu
from jax.sharding import PartitionSpec as P

F = 16384
K = 1024
ITERS = 2
RIDGE = 0.5

f32 = jnp.float32
bf16 = jnp.bfloat16


def split(value):
    high = value.astype(bf16)
    return high, (value - high.astype(f32)).astype(bf16)


def dot(a, b):
    return lax.dot_general(a, b, (((1,), (0,)), ((), ())), preferred_element_type=f32)


def dot_turned(a, b):
    return lax.dot_general(a, b, (((1,), (1,)), ((), ())), preferred_element_type=f32)


def dot3(a, b):
    ah, al = split(a)
    bh, bl = split(b)
    return dot(ah, bh) + (dot(ah, bl) + dot(al, bh))


def dot2_left(a, exact):
    ah, al = split(a)
    return dot(ah, exact) + dot(al, exact)


def dot2_right(exact, b):
    bh, bl = split(b)
    return dot(exact, bh) + dot(exact, bl)


BLOCK = 256
DP = ("z", "core")


def inverse_kernel(core_ref, lower_hbm, high_ref, low_ref, made_ref, lower, inv, sems):
    n = lower.shape[0]
    blocks = n // BLOCK
    spans = [pl.ds(b * BLOCK, BLOCK) for b in range(blocks)]
    parts = [(span, span) for span in spans]
    size = BLOCK
    while size < n:
        parts += [(pl.ds(at + size, size), pl.ds(at, size)) for at in range(0, n, 2 * size)]
        size *= 2
    copies = [
        pltpu.make_async_copy(lower_hbm.at[part], lower.at[part], sems.at[k]) for k, part in enumerate(parts)
    ]
    for copy in copies:
        copy.start()
    made_ref[0] = core_ref[0]
    inv[...] = jnp.zeros_like(inv)
    rows = lax.broadcasted_iota(jnp.int32, (BLOCK, BLOCK), 0)
    cols = lax.broadcasted_iota(jnp.int32, (BLOCK, BLOCK), 1)

    def below(k):
        return ((rows >> k) == (cols >> k) + 1) & ((rows >> (k + 1)) == (cols >> (k + 1)))

    for copy, span in zip(copies, spans):
        copy.wait()
        block = lower[span, span].astype(f32)
        diag = jnp.where(rows == cols, block, 0.0)
        down = 1.0 / jnp.sum(diag, axis=1, keepdims=True)
        across = 1.0 / jnp.sum(diag, axis=0, keepdims=True)
        inv[span, span] = jnp.where(rows == cols, down, jnp.where(below(0), -(block * down) * across, 0.0))

    def level(k, carry):
        mask = below(k)
        for span in spans:
            x = inv[span, span]
            off = jnp.where(mask, lower[span, span].astype(f32), 0.0).astype(bf16)
            inv[span, span] = x - dot3(dot2_left(x, off), x)
        return carry

    lax.fori_loop(1, int(math.log2(BLOCK)), level, 0)
    for copy, (bottom, top) in list(zip(copies, parts))[blocks:]:
        copy.wait()
        a, b = inv[top, top], inv[bottom, bottom]
        inv[bottom, top] = -dot3(b, dot2_right(lower[bottom, top], a))
    for span in spans:
        high_ref[span, :], low_ref[span, :] = split(inv[span, :])


def coarse_factor_inverse(core, lower):
    n = lower.shape[0]
    vmem = pl.BlockSpec(memory_space=pltpu.VMEM)
    return pl.pallas_call(
        inverse_kernel,
        out_shape=[jax.ShapeDtypeStruct((n, n), bf16)] * 2 + [jax.ShapeDtypeStruct((1,), jnp.int32)],
        in_specs=[pl.BlockSpec(memory_space=pltpu.SMEM), pl.BlockSpec(memory_space=pl.ANY)],
        out_specs=[vmem] * 2 + [pl.BlockSpec(memory_space=pltpu.SMEM)],
        scratch_shapes=[
            pltpu.VMEM((n, n), bf16),
            pltpu.VMEM((n, n), f32),
            pltpu.SemaphoreType.DMA((2 * (n // BLOCK) - 1,)),
        ],
        compiler_params=pltpu.CompilerParams(vmem_limit_bytes=56 * 1024 * 1024),
        cost_estimate=pl.CostEstimate(flops=10**10, bytes_accessed=6 * 2**20, transcendentals=0),
    )(core, lower)


def place(a, b):
    return pl.ds((a * (a + 1) // 2 + b) * BLOCK, BLOCK)


def product_kernel(xh_ref, xl_ref, order_hbm, high_ref, low_ref):
    del order_hbm
    spans = [slice(b, b + BLOCK) for b in range(0, xh_ref.shape[0], BLOCK)]
    parts = [[(xh_ref[row, col], xl_ref[row, col]) for col in spans[: r + 1]] for r, row in enumerate(spans)]
    turned = [[tuple(half.astype(f32).T.astype(bf16) for half in part) for part in row] for row in parts]
    for a in range(len(spans)):
        for b in range(a + 1):
            total = None
            for k in range(a, len(spans)):
                (ah, al), (bh, bl) = turned[k][a], parts[k][b]
                term = dot(ah, bh) + (dot(ah, bl) + dot(al, bh))
                total = term if total is None else total + term
            high_ref[place(a, b), :], low_ref[place(a, b), :] = split(total)


def coarse_inverse(xh, xl, order):
    n = xh.shape[0]
    blocks = n // BLOCK
    vmem = pl.BlockSpec(memory_space=pltpu.VMEM)
    return pl.pallas_call(
        product_kernel,
        out_shape=[jax.ShapeDtypeStruct((blocks * (blocks + 1) // 2 * BLOCK, BLOCK), bf16)] * 2,
        in_specs=[vmem, vmem, pl.BlockSpec(memory_space=pl.ANY)],
        out_specs=[vmem] * 2,
        compiler_params=pltpu.CompilerParams(vmem_limit_bytes=52 * 1024 * 1024),
        cost_estimate=pl.CostEstimate(flops=4 * 10**9, bytes_accessed=8 * 2**20, transcendentals=0),
    )(xh, xl, order)


def repeat_kernel(value_hbm, out_hbm, value, sems):
    get = pltpu.make_async_copy(value_hbm, value, sems.at[0])
    get.start()
    get.wait()
    puts = [pltpu.make_async_copy(value, out_hbm.at[p], sems.at[p + 1]) for p in range(out_hbm.shape[0])]
    for put in puts:
        put.start()
    for put in puts:
        put.wait()


def repeat(value, count):
    anywhere = pl.BlockSpec(memory_space=pl.ANY)
    return pl.pallas_call(
        repeat_kernel,
        out_shape=jax.ShapeDtypeStruct((count,) + value.shape, value.dtype),
        in_specs=[anywhere],
        out_specs=anywhere,
        scratch_shapes=[pltpu.VMEM(value.shape, value.dtype), pltpu.SemaphoreType.DMA((count + 1,))],
        compiler_params=pltpu.CompilerParams(vmem_limit_bytes=56 * 1024 * 1024),
    )(value)


def output_kernel(got_ref, answer_hbm, resid_hbm, value, sems):
    rows, puts = got_ref.shape[2], []
    for k, out in enumerate((answer_hbm, resid_hbm)):
        for p in range(got_ref.shape[0]):
            value[k, p * rows : (p + 1) * rows, :] = got_ref[p, k].astype(f32)
        puts.append(pltpu.make_async_copy(value.at[k], out, sems.at[k]))
        puts[k].start()
    for put in puts:
        put.wait()


def outputs(got):
    parts, _, rows, count = got.shape
    return pl.pallas_call(
        output_kernel,
        out_shape=[jax.ShapeDtypeStruct((parts * rows, count), f32)] * 2,
        in_specs=[pl.BlockSpec(memory_space=pltpu.VMEM)],
        out_specs=[pl.BlockSpec(memory_space=pl.ANY)] * 2,
        scratch_shapes=[pltpu.VMEM((2, parts * rows, count), f32), pltpu.SemaphoreType.DMA((2,))],
        compiler_params=pltpu.CompilerParams(vmem_limit_bytes=8 * 1024 * 1024),
    )(got)


def feature_kernel(
    core_ref, samples_hbm, mine_ref, other_ref, targets_hbm, feat_ref, part_ref, proj, samples_ref, targets_ref, sems
):
    core = core_ref[0]
    get_samples = pltpu.make_async_copy(samples_hbm, samples_ref, sems.at[0])
    get_targets = pltpu.make_async_copy(targets_hbm, targets_ref, sems.at[1])
    get_samples.start()
    get_targets.start()
    for j in range(proj.shape[0]):
        proj[j, :, core] = mine_ref[:, j]
        proj[j, :, 1 - core] = other_ref[:, j]
    get_samples.wait()
    samples, value = samples_ref[...], None
    for j in range(proj.shape[0]):
        panel = dot(samples, proj[j].reshape(samples.shape[1], proj.shape[-1]))
        value = panel if value is None else value * panel
    feat = (value * (1.0 / math.sqrt(F))).astype(bf16)
    feat_ref[...] = feat
    get_targets.wait()
    total = dot(targets_ref[...], feat)
    step = part_ref.shape[1]
    for p in range(part_ref.shape[0]):
        part_ref[p] = total[p * step : (p + 1) * step, :]


def make_features(core, samples, mine, other, targets_t, parts):
    n = samples.shape[0]
    chips, panels, rows, width = mine.shape
    vmem, anywhere = pl.BlockSpec(memory_space=pltpu.VMEM), pl.BlockSpec(memory_space=pl.ANY)
    return pl.pallas_call(
        feature_kernel,
        out_shape=[
            jax.ShapeDtypeStruct((n, width), bf16),
            jax.ShapeDtypeStruct((parts, targets_t.shape[0] // parts, width), f32),
        ],
        in_specs=[pl.BlockSpec(memory_space=pltpu.SMEM), anywhere, vmem, vmem, anywhere],
        out_specs=[vmem] * 2,
        scratch_shapes=[
            pltpu.VMEM((panels, chips, 2, rows, width), bf16),
            pltpu.VMEM(samples.shape, bf16),
            pltpu.VMEM(targets_t.shape, bf16),
            pltpu.SemaphoreType.DMA((2,)),
        ],
        compiler_params=pltpu.CompilerParams(vmem_limit_bytes=49 * 1024 * 1024),
        cost_estimate=pl.CostEstimate(flops=2 * 10**9, bytes_accessed=5 * 2**20, transcendentals=0),
    )(core, samples, mine, other, targets_t)


SLOTS = 128


def row_sum(value):
    return jnp.sum(value, axis=1, keepdims=True)


def lane(value, k):
    at = lax.broadcasted_iota(jnp.int32, value.shape, 1)
    return row_sum(jnp.where(at == k, value, 0.0))


def lanes_of(values):
    at = lax.broadcasted_iota(jnp.int32, (values[0].shape[0], SLOTS), 1)
    total = jnp.zeros(at.shape, f32)
    for k, value in enumerate(values):
        for piece in range(3):
            part = value.astype(bf16).astype(f32)
            total = jnp.where(at == 3 * k + piece, part, total)
            value = value - part
    return total


def summed(ref):
    total = ref[0].astype(f32)
    for p in range(1, ref.shape[0]):
        total = total + ref[p].astype(f32)
    return total


def spread(send_ref, value, dots):
    sent = jnp.concatenate([value, lanes_of(dots)], 1).astype(bf16)
    for p in range(send_ref.shape[0]):
        send_ref[p] = sent


def first_send_kernel(got_ref, scale_ref, value_ref, send_ref):
    value = summed(got_ref)
    value_ref[...] = value
    spread(send_ref, value, [row_sum(scale_ref[...] * value * value)])


def step_send_kernel(got_ref, scale_ref, direction_ref, resid_ref, value_ref, send_ref):
    direction = direction_ref[...]
    value = summed(got_ref) + RIDGE * direction
    value_ref[...] = value
    weighted = scale_ref[...] * value
    spread(
        send_ref, value, [row_sum(direction * value), row_sum(weighted * resid_ref[...]), row_sum(weighted * value)]
    )


def run_send(kernel, n_sk, got, *operands):
    _, rows, count = got.shape
    vmem = pl.BlockSpec(memory_space=pltpu.VMEM)
    return pl.pallas_call(
        kernel,
        out_shape=[
            jax.ShapeDtypeStruct((rows, count), f32),
            jax.ShapeDtypeStruct((n_sk, rows, count + SLOTS), bf16),
        ],
        in_specs=[vmem] * (1 + len(operands)),
        out_specs=[vmem] * 2,
        compiler_params=pltpu.CompilerParams(vmem_limit_bytes=8 * 1024 * 1024),
    )(got, *operands)


def last_u_kernel(share, got_ref, send_ref):
    total = summed(got_ref)
    n = total.shape[1] - SLOTS
    u = total[:, :n].astype(bf16).astype(f32)
    spread(send_ref, u, [row_sum(total[:, :n] * u) + share * row_sum(total[:, n:])])


def run_last_u(share, got):
    vmem = pl.BlockSpec(memory_space=pltpu.VMEM)
    return pl.pallas_call(
        functools.partial(last_u_kernel, share),
        out_shape=jax.ShapeDtypeStruct(got.shape, bf16),
        in_specs=[vmem],
        out_specs=vmem,
        compiler_params=pltpu.CompilerParams(vmem_limit_bytes=8 * 1024 * 1024),
    )(got)


def gathered(got_ref, halves, count):
    parts = []
    for h in range(halves):
        acc = got_ref[h, :, :count].astype(f32)
        for p in range(h + halves, got_ref.shape[0], halves):
            acc = acc + got_ref[p, :, :count].astype(f32)
        parts.append(acc)
    dots = got_ref[0, :, count:].astype(f32)
    for p in range(1, got_ref.shape[0]):
        dots = dots + got_ref[p, :, count:].astype(f32)
    at = lax.broadcasted_iota(jnp.int32, dots.shape, 1)
    sums = [row_sum(jnp.where((at >= 3 * k) & (at < 3 * k + 3), dots, 0.0)) for k in range(3)]
    return parts, sums


def fetch_blocks(low_hbm, low, sems):
    spans = [pl.ds(at, BLOCK) for at in range(0, low.shape[0], BLOCK)]
    copies = [pltpu.make_async_copy(low_hbm.at[span], low.at[span], sems.at[k]) for k, span in enumerate(spans)]
    for copy in copies:
        copy.start()
    return copies


def coarse(parts, inverse):
    high_ref, low_ref, fetch = inverse
    rows, sides = parts[0].shape[0], []
    for part in parts:
        high = part.astype(bf16).astype(f32)
        both = jnp.concatenate([high, part - high], 0).astype(bf16)
        sides += [both[:, at : at + BLOCK] for at in range(0, part.shape[1], BLOCK)]
    blocks = range(len(sides))

    def times(ref, both, a, b):
        return dot(both, ref[place(a, b), :]) if a >= b else dot_turned(both, ref[place(b, a), :])

    solved = []
    for b in blocks:
        one = sum(times(high_ref, sides[a], a, b) for a in blocks)
        solved.append(one[:rows] + one[rows:])
    for copy in fetch:
        copy.wait()
    for b in blocks:
        solved[b] = solved[b] + sum(times(low_ref, sides[a], a, b) for a in blocks)[:rows]
    return jnp.concatenate(solved, 1)


def next_direction(parity_ref, parts, inverse, resid, scale, energy, factor):
    count = resid.shape[1]
    solved = coarse(parts, inverse)
    product = energy
    mine = solved[:, :count]
    for h, part in enumerate(parts):
        here = solved[:, h * count : (h + 1) * count]
        product = product + row_sum(part * here)
        if h:
            mine = jnp.where(parity_ref[0] == h, here, mine)
    return product, scale * resid + factor * mine


def first_kernel(
    factor, parity_ref, got_ref, high_ref, low_hbm, resid_ref, scale_ref, dir_ref, send_ref, rho_ref, dots_ref, low, sems
):
    count = resid_ref.shape[1]
    inverse = high_ref, low, fetch_blocks(low_hbm, low, sems)
    parts, sums = gathered(got_ref, rho_ref.shape[1] // count, count)
    parts = [part * factor for part in parts]
    product, direction = next_direction(
        parity_ref, parts, inverse, resid_ref[...], scale_ref[...], sums[0], factor
    )
    dir_ref[...] = direction
    for p in range(send_ref.shape[0]):
        send_ref[p] = direction.astype(bf16)
    for h, part in enumerate(parts):
        rho_ref[:, h * count : (h + 1) * count] = part
    at = lax.broadcasted_iota(jnp.int32, dots_ref.shape, 1)
    dots_ref[...] = jnp.where(at == 0, sums[0], jnp.where(at == 1, product, 0.0))


def step_kernel(
    factor, parity_ref, got_ref, high_ref, low_hbm, resid_ref, scale_ref, image_ref, old_ref, rho_ref, dots_ref, answer_ref,
    dir_ref, send_ref, new_rho_ref, new_dots_ref, new_resid_ref, new_answer_ref, low, sems,
):
    count = resid_ref.shape[1]
    inverse = high_ref, low, fetch_blocks(low_hbm, low, sems)
    parts, sums = gathered(got_ref, rho_ref.shape[1] // count, count)
    energy, product = lane(dots_ref[...], 0), lane(dots_ref[...], 1)
    alpha = product / sums[0]
    old = old_ref[...]
    new_answer_ref[...] = answer_ref[...] + alpha * old
    resid = resid_ref[...] - alpha * image_ref[...]
    new_resid_ref[...] = resid
    energy = energy - alpha * (2.0 * sums[1] - alpha * sums[2])
    parts = [
        rho_ref[:, h * count : (h + 1) * count] - alpha * (part * factor) for h, part in enumerate(parts)
    ]
    fresh, fine = next_direction(parity_ref, parts, inverse, resid, scale_ref[...], energy, factor)
    direction = fine + fresh / product * old
    dir_ref[...] = direction
    for p in range(send_ref.shape[0]):
        send_ref[p] = direction.astype(bf16)
    for h, part in enumerate(parts):
        new_rho_ref[:, h * count : (h + 1) * count] = part
    at = lax.broadcasted_iota(jnp.int32, dots_ref.shape, 1)
    new_dots_ref[...] = jnp.where(at == 0, energy, jnp.where(at == 1, fresh, 0.0))


def run_coarse(kernel, factor, n_dp, parity, *operands, more=0):
    rows, count = operands[3].shape
    vmem = pl.BlockSpec(memory_space=pltpu.VMEM)
    wide = jax.ShapeDtypeStruct((rows, count), f32)
    outs = [
        wide,
        jax.ShapeDtypeStruct((n_dp, rows, count), bf16),
        jax.ShapeDtypeStruct((rows, K), f32),
        jax.ShapeDtypeStruct((rows, SLOTS), f32),
    ] + [wide] * more
    return pl.pallas_call(
        functools.partial(kernel, factor),
        out_shape=outs,
        in_specs=[pl.BlockSpec(memory_space=pltpu.SMEM), vmem, vmem, pl.BlockSpec(memory_space=pl.ANY)]
        + [vmem] * (len(operands) - 3),
        out_specs=[vmem] * len(outs),
        scratch_shapes=[
            pltpu.VMEM(operands[2].shape, bf16),
            pltpu.SemaphoreType.DMA((operands[2].shape[0] // BLOCK,)),
        ],
        compiler_params=pltpu.CompilerParams(vmem_limit_bytes=52 * 1024 * 1024),
        cost_estimate=pl.CostEstimate(flops=10**8, bytes_accessed=5 * 2**20, transcendentals=0),
    )(parity, *operands)


def rounded(value):
    return lax.reduce_precision(value, 8, 7).astype(bf16)


def triple(value):
    high = lax.reduce_precision(value, 8, 7)
    mid = lax.reduce_precision(value - high, 8, 7)
    return jnp.stack([high, mid, value - high - mid], -1).astype(bf16)


def slots(values):
    parts = triple(values)
    flat = parts.reshape(parts.shape[:-2] + (-1,))
    return jnp.pad(flat, ((0, 0),) * (flat.ndim - 1) + ((0, SLOTS - flat.shape[-1]),))


def body(samples, projections, targets, feature_scale, coarse_factor):
    n_dp, n_sk = lax.axis_size(DP), lax.axis_size("sketch")
    count = projections.shape[2]
    width = targets.shape[1]
    mine = width // n_dp
    cols = width // n_sk
    factor = 1.0 / math.sqrt(F // K)
    halves = K // count
    parity = (lax.axis_index("sketch") % halves).astype(jnp.int32).reshape(1)
    n = samples.shape[0]
    scale = feature_scale[None, :]

    core = lax.axis_index("core").astype(jnp.int32).reshape(1)
    mine_proj = lax.all_to_all(repeat(projections, lax.axis_size("z")), "z", 0, 0)
    factor_high, factor_low, core = coarse_factor_inverse(core, coarse_factor)
    mine_proj, core = lax.optimization_barrier((mine_proj, core))
    other_proj = lax.ppermute(mine_proj, "core", [(0, 1), (1, 0)])
    feat, part = make_features(core, samples, mine_proj, other_proj, targets.T, n_dp)

    def scatter_dp(value):
        return lax.all_to_all(value, DP, 0, 0)

    def gather_sk(value):
        return lax.all_to_all(jnp.broadcast_to(value[None], (n_sk,) + value.shape), "sketch", 0, 0)

    def forward(send):
        whole = lax.all_to_all(send, DP, 0, 0).reshape(width, count)
        sums = lax.dot_general(whole, feat, (((1,), (1,)), ((), ())), preferred_element_type=f32)
        return whole, sums.astype(bf16).reshape(n_sk, cols, n)

    resid, sent = run_send(first_send_kernel, n_sk, scatter_dp(part), scale)
    inv_high, inv_low = coarse_inverse(factor_high, factor_low, resid)
    got = lax.all_to_all(sent, "sketch", 0, 0)
    direction, send, rho, dots = run_coarse(
        first_kernel, factor, n_dp, parity, got, inv_high, inv_low, resid, scale
    )
    answer = jnp.zeros_like(resid)
    for step in range(ITERS - 1):
        _, sums = forward(send)
        u = rounded(jnp.sum(lax.all_to_all(sums, "sketch", 0, 0).astype(f32), 0))
        whole = gather_sk(u).reshape(width, n)
        parts = scatter_dp(dot(whole, feat).reshape(n_dp, mine, count))
        image, sent = run_send(step_send_kernel, n_sk, parts, scale, direction, resid)
        got = lax.all_to_all(sent, "sketch", 0, 0)
        direction, send, rho, dots, resid, answer = run_coarse(
            step_kernel, factor, n_dp, parity, got, inv_high, inv_low, resid, scale, image, direction, rho, dots, answer,
            more=2,
        )
    whole, sums = forward(send)
    squares = jnp.sum(jnp.square(whole.astype(f32)), 1).reshape(n_sk, cols, 1)
    got = lax.all_to_all(jnp.concatenate([sums, slots(squares)], 2), "sketch", 0, 0)
    sent = run_last_u(RIDGE / n_dp, got)
    got = lax.all_to_all(sent, "sketch", 0, 0).reshape(width, n + SLOTS)
    image = dot(got[:, :n], feat)
    sent = jnp.concatenate([image.astype(bf16), got[:, n:]], 1)
    got = lax.all_to_all(sent.reshape(n_dp, mine, count + SLOTS), DP, 0, 0).astype(f32)
    total = jnp.sum(got, 0)
    image = total[:, :count] + RIDGE * direction
    alpha = dots[:, 1:2] / row_sum(total[:, count:])
    out = jnp.stack([answer + alpha * direction, resid - alpha * image]).astype(bf16)
    got = lax.all_to_all(jnp.broadcast_to(out[None], (n_dp,) + out.shape), DP, 0, 0)
    answer, resid = outputs(got)
    return answer.T, resid.T


def solution(mesh):
    chips = mesh.shape["dp"] // 2
    mesh = jax.sharding.Mesh(mesh.devices.reshape(chips, 2, -1), ("z", "core", "sketch"))
    placed = (P(DP, None), P(None, DP, "sketch"), P(DP, None), P("sketch"), P())
    return jax.shard_map(
        body,
        mesh=mesh,
        in_specs=placed,
        out_specs=(P("sketch", None), P("sketch", None)),
        check_vma=False,
    )
```

```python
import functools
import math

import jax
import jax.numpy as jnp
from jax import lax
from jax.experimental import pallas as pl
from jax.experimental.pallas import tpu as pltpu
from jax.sharding import PartitionSpec as P

F = 16384
K = 1024
ITERS = 2
RIDGE = 0.5

f32 = jnp.float32
bf16 = jnp.bfloat16


def split(value):
    high = value.astype(bf16)
    return high, (value - high.astype(f32)).astype(bf16)


def dot(a, b):
    return lax.dot_general(a, b, (((1,), (0,)), ((), ())), preferred_element_type=f32)


def dot_turned(a, b):
    return lax.dot_general(a, b, (((1,), (1,)), ((), ())), preferred_element_type=f32)


def dot3(a, b):
    ah, al = split(a)
    bh, bl = split(b)
    return dot(ah, bh) + (dot(ah, bl) + dot(al, bh))


def dot2_left(a, exact):
    ah, al = split(a)
    return dot(ah, exact) + dot(al, exact)


def dot2_right(exact, b):
    bh, bl = split(b)
    return dot(exact, bh) + dot(exact, bl)


BLOCK = 256
DP = ("z", "core")


def inverse_kernel(core_ref, lower_hbm, high_ref, low_ref, made_ref, lower, inv, sems):
    n = lower.shape[0]
    blocks = n // BLOCK
    spans = [pl.ds(b * BLOCK, BLOCK) for b in range(blocks)]
    parts = [(span, span) for span in spans]
    size = BLOCK
    while size < n:
        parts += [(pl.ds(at + size, size), pl.ds(at, size)) for at in range(0, n, 2 * size)]
        size *= 2
    copies = [
        pltpu.make_async_copy(lower_hbm.at[part], lower.at[part], sems.at[k]) for k, part in enumerate(parts)
    ]
    for copy in copies:
        copy.start()
    made_ref[0] = core_ref[0]
    inv[...] = jnp.zeros_like(inv)
    rows = lax.broadcasted_iota(jnp.int32, (BLOCK, BLOCK), 0)
    cols = lax.broadcasted_iota(jnp.int32, (BLOCK, BLOCK), 1)

    def below(k):
        return ((rows >> k) == (cols >> k) + 1) & ((rows >> (k + 1)) == (cols >> (k + 1)))

    for copy, span in zip(copies, spans):
        copy.wait()
        block = lower[span, span].astype(f32)
        diag = jnp.where(rows == cols, block, 0.0)
        down = 1.0 / jnp.sum(diag, axis=1, keepdims=True)
        across = 1.0 / jnp.sum(diag, axis=0, keepdims=True)
        inv[span, span] = jnp.where(rows == cols, down, jnp.where(below(0), -(block * down) * across, 0.0))

    def level(k, carry):
        mask = below(k)
        for span in spans:
            x = inv[span, span]
            off = jnp.where(mask, lower[span, span].astype(f32), 0.0).astype(bf16)
            inv[span, span] = x - dot3(dot2_left(x, off), x)
        return carry

    lax.fori_loop(1, int(math.log2(BLOCK)), level, 0)
    for copy, (bottom, top) in list(zip(copies, parts))[blocks:]:
        copy.wait()
        a, b = inv[top, top], inv[bottom, bottom]
        inv[bottom, top] = -dot3(b, dot2_right(lower[bottom, top], a))
    for span in spans:
        high_ref[span, :], low_ref[span, :] = split(inv[span, :])


def coarse_factor_inverse(core, lower):
    n = lower.shape[0]
    vmem = pl.BlockSpec(memory_space=pltpu.VMEM)
    return pl.pallas_call(
        inverse_kernel,
        out_shape=[jax.ShapeDtypeStruct((n, n), bf16)] * 2 + [jax.ShapeDtypeStruct((1,), jnp.int32)],
        in_specs=[pl.BlockSpec(memory_space=pltpu.SMEM), pl.BlockSpec(memory_space=pl.ANY)],
        out_specs=[vmem] * 2 + [pl.BlockSpec(memory_space=pltpu.SMEM)],
        scratch_shapes=[
            pltpu.VMEM((n, n), bf16),
            pltpu.VMEM((n, n), f32),
            pltpu.SemaphoreType.DMA((2 * (n // BLOCK) - 1,)),
        ],
        compiler_params=pltpu.CompilerParams(vmem_limit_bytes=56 * 1024 * 1024),
        cost_estimate=pl.CostEstimate(flops=10**10, bytes_accessed=6 * 2**20, transcendentals=0),
    )(core, lower)


def place(a, b):
    return pl.ds((a * (a + 1) // 2 + b) * BLOCK, BLOCK)


def product_kernel(xh_ref, xl_ref, order_hbm, high_ref, low_ref):
    del order_hbm
    spans = [slice(b, b + BLOCK) for b in range(0, xh_ref.shape[0], BLOCK)]
    parts = [[(xh_ref[row, col], xl_ref[row, col]) for col in spans[: r + 1]] for r, row in enumerate(spans)]
    turned = [[tuple(half.astype(f32).T.astype(bf16) for half in part) for part in row] for row in parts]
    for a in range(len(spans)):
        for b in range(a + 1):
            total = None
            for k in range(a, len(spans)):
                (ah, al), (bh, bl) = turned[k][a], parts[k][b]
                term = dot(ah, bh) + (dot(ah, bl) + dot(al, bh))
                total = term if total is None else total + term
            high_ref[place(a, b), :], low_ref[place(a, b), :] = split(total)


def coarse_inverse(xh, xl, order):
    n = xh.shape[0]
    blocks = n // BLOCK
    vmem = pl.BlockSpec(memory_space=pltpu.VMEM)
    return pl.pallas_call(
        product_kernel,
        out_shape=[jax.ShapeDtypeStruct((blocks * (blocks + 1) // 2 * BLOCK, BLOCK), bf16)] * 2,
        in_specs=[vmem, vmem, pl.BlockSpec(memory_space=pl.ANY)],
        out_specs=[vmem] * 2,
        compiler_params=pltpu.CompilerParams(vmem_limit_bytes=52 * 1024 * 1024),
        cost_estimate=pl.CostEstimate(flops=4 * 10**9, bytes_accessed=8 * 2**20, transcendentals=0),
    )(xh, xl, order)


def repeat_kernel(value_hbm, out_hbm, value, sems):
    get = pltpu.make_async_copy(value_hbm, value, sems.at[0])
    get.start()
    get.wait()
    puts = [pltpu.make_async_copy(value, out_hbm.at[p], sems.at[p + 1]) for p in range(out_hbm.shape[0])]
    for put in puts:
        put.start()
    for put in puts:
        put.wait()


def repeat(value, count):
    anywhere = pl.BlockSpec(memory_space=pl.ANY)
    return pl.pallas_call(
        repeat_kernel,
        out_shape=jax.ShapeDtypeStruct((count,) + value.shape, value.dtype),
        in_specs=[anywhere],
        out_specs=anywhere,
        scratch_shapes=[pltpu.VMEM(value.shape, value.dtype), pltpu.SemaphoreType.DMA((count + 1,))],
        compiler_params=pltpu.CompilerParams(vmem_limit_bytes=56 * 1024 * 1024),
    )(value)


def output_kernel(got_ref, answer_hbm, resid_hbm, value, sems):
    rows, puts = got_ref.shape[2], []
    for k, out in enumerate((answer_hbm, resid_hbm)):
        for p in range(got_ref.shape[0]):
            value[k, p * rows : (p + 1) * rows, :] = got_ref[p, k].astype(f32)
        puts.append(pltpu.make_async_copy(value.at[k], out, sems.at[k]))
        puts[k].start()
    for put in puts:
        put.wait()


def outputs(got):
    parts, _, rows, count = got.shape
    return pl.pallas_call(
        output_kernel,
        out_shape=[jax.ShapeDtypeStruct((parts * rows, count), f32)] * 2,
        in_specs=[pl.BlockSpec(memory_space=pltpu.VMEM)],
        out_specs=[pl.BlockSpec(memory_space=pl.ANY)] * 2,
        scratch_shapes=[pltpu.VMEM((2, parts * rows, count), f32), pltpu.SemaphoreType.DMA((2,))],
        compiler_params=pltpu.CompilerParams(vmem_limit_bytes=8 * 1024 * 1024),
    )(got)


def feature_kernel(core_ref, samples_ref, mine_ref, other_ref, targets_ref, feat_ref, part_ref, proj):
    core = core_ref[0]
    for j in range(proj.shape[0]):
        proj[j, :, core] = mine_ref[:, j]
        proj[j, :, 1 - core] = other_ref[:, j]
    samples, value = samples_ref[...], None
    for j in range(proj.shape[0]):
        panel = dot(samples, proj[j].reshape(samples.shape[1], proj.shape[-1]))
        value = panel if value is None else value * panel
    feat = (value * (1.0 / math.sqrt(F))).astype(bf16)
    feat_ref[...] = feat
    total = dot(targets_ref[...], feat)
    step = part_ref.shape[1]
    for p in range(part_ref.shape[0]):
        part_ref[p] = total[p * step : (p + 1) * step, :]


def make_features(core, samples, mine, other, targets_t, parts):
    n = samples.shape[0]
    chips, panels, rows, width = mine.shape
    vmem = pl.BlockSpec(memory_space=pltpu.VMEM)
    return pl.pallas_call(
        feature_kernel,
        out_shape=[
            jax.ShapeDtypeStruct((n, width), bf16),
            jax.ShapeDtypeStruct((parts, targets_t.shape[0] // parts, width), f32),
        ],
        in_specs=[pl.BlockSpec(memory_space=pltpu.SMEM)] + [vmem] * 4,
        out_specs=[vmem] * 2,
        scratch_shapes=[pltpu.VMEM((panels, chips, 2, rows, width), bf16)],
        compiler_params=pltpu.CompilerParams(vmem_limit_bytes=49 * 1024 * 1024),
        cost_estimate=pl.CostEstimate(flops=2 * 10**9, bytes_accessed=5 * 2**20, transcendentals=0),
    )(core, samples, mine, other, targets_t)


SLOTS = 128


def row_sum(value):
    return jnp.sum(value, axis=1, keepdims=True)


def lane(value, k):
    at = lax.broadcasted_iota(jnp.int32, value.shape, 1)
    return row_sum(jnp.where(at == k, value, 0.0))


def lanes_of(values):
    at = lax.broadcasted_iota(jnp.int32, (values[0].shape[0], SLOTS), 1)
    total = jnp.zeros(at.shape, f32)
    for k, value in enumerate(values):
        for piece in range(3):
            part = value.astype(bf16).astype(f32)
            total = jnp.where(at == 3 * k + piece, part, total)
            value = value - part
    return total


def summed(ref):
    total = ref[0].astype(f32)
    for p in range(1, ref.shape[0]):
        total = total + ref[p].astype(f32)
    return total


def spread(send_ref, value, dots):
    sent = jnp.concatenate([value, lanes_of(dots)], 1).astype(bf16)
    for p in range(send_ref.shape[0]):
        send_ref[p] = sent


def first_send_kernel(got_ref, scale_ref, value_ref, send_ref):
    value = summed(got_ref)
    value_ref[...] = value
    spread(send_ref, value, [row_sum(scale_ref[...] * value * value)])


def step_send_kernel(got_ref, scale_ref, direction_ref, resid_ref, value_ref, send_ref):
    direction = direction_ref[...]
    value = summed(got_ref) + RIDGE * direction
    value_ref[...] = value
    weighted = scale_ref[...] * value
    spread(
        send_ref, value, [row_sum(direction * value), row_sum(weighted * resid_ref[...]), row_sum(weighted * value)]
    )


def run_send(kernel, n_sk, got, *operands):
    _, rows, count = got.shape
    vmem = pl.BlockSpec(memory_space=pltpu.VMEM)
    return pl.pallas_call(
        kernel,
        out_shape=[
            jax.ShapeDtypeStruct((rows, count), f32),
            jax.ShapeDtypeStruct((n_sk, rows, count + SLOTS), bf16),
        ],
        in_specs=[vmem] * (1 + len(operands)),
        out_specs=[vmem] * 2,
        compiler_params=pltpu.CompilerParams(vmem_limit_bytes=8 * 1024 * 1024),
    )(got, *operands)


def last_sums_kernel(whole_ref, sums_ref, send_ref):
    parts, rows, cols = whole_ref.shape[0], whole_ref.shape[1], send_ref.shape[1]
    for p in range(parts):
        value = whole_ref[p].astype(f32)
        sent = jnp.concatenate([sums_ref[p * rows : (p + 1) * rows, :], lanes_of([row_sum(value * value)])], 1)
        for k in range(rows // cols):
            send_ref[p * (rows // cols) + k] = sent[k * cols : (k + 1) * cols, :].astype(bf16)


def run_last_sums(n_sk, whole, sums):
    width, n = sums.shape
    vmem = pl.BlockSpec(memory_space=pltpu.VMEM)
    return pl.pallas_call(
        last_sums_kernel,
        out_shape=jax.ShapeDtypeStruct((n_sk, width // n_sk, n + SLOTS), bf16),
        in_specs=[vmem] * 2,
        out_specs=vmem,
        compiler_params=pltpu.CompilerParams(vmem_limit_bytes=8 * 1024 * 1024),
    )(whole, sums)


def last_u_kernel(share, got_ref, send_ref):
    total = summed(got_ref)
    n = total.shape[1] - SLOTS
    u = total[:, :n].astype(bf16).astype(f32)
    spread(send_ref, u, [row_sum(total[:, :n] * u) + share * row_sum(total[:, n:])])


def run_last_u(share, got):
    vmem = pl.BlockSpec(memory_space=pltpu.VMEM)
    return pl.pallas_call(
        functools.partial(last_u_kernel, share),
        out_shape=jax.ShapeDtypeStruct(got.shape, bf16),
        in_specs=[vmem],
        out_specs=vmem,
        compiler_params=pltpu.CompilerParams(vmem_limit_bytes=8 * 1024 * 1024),
    )(got)


def gathered(got_ref, halves, count):
    parts = []
    for h in range(halves):
        acc = got_ref[h, :, :count].astype(f32)
        for p in range(h + halves, got_ref.shape[0], halves):
            acc = acc + got_ref[p, :, :count].astype(f32)
        parts.append(acc)
    dots = got_ref[0, :, count:].astype(f32)
    for p in range(1, got_ref.shape[0]):
        dots = dots + got_ref[p, :, count:].astype(f32)
    at = lax.broadcasted_iota(jnp.int32, dots.shape, 1)
    sums = [row_sum(jnp.where((at >= 3 * k) & (at < 3 * k + 3), dots, 0.0)) for k in range(3)]
    return parts, sums


def coarse(parts, inverse):
    high_ref, low_ref = inverse
    rows, sides = parts[0].shape[0], []
    for part in parts:
        high = part.astype(bf16).astype(f32)
        both = jnp.concatenate([high, part - high], 0).astype(bf16)
        sides += [both[:, at : at + BLOCK] for at in range(0, part.shape[1], BLOCK)]
    blocks = range(len(sides))

    def times(ref, both, a, b):
        return dot(both, ref[place(a, b), :]) if a >= b else dot_turned(both, ref[place(b, a), :])

    solved = []
    for b in blocks:
        one = sum(times(high_ref, sides[a], a, b) for a in blocks)
        solved.append(one[:rows] + one[rows:])
    for b in blocks:
        solved[b] = solved[b] + sum(times(low_ref, sides[a], a, b) for a in blocks)[:rows]
    return jnp.concatenate(solved, 1)


def next_direction(parity_ref, parts, inverse, resid, scale, energy, factor):
    count = resid.shape[1]
    solved = coarse(parts, inverse)
    product = energy
    mine = solved[:, :count]
    for h, part in enumerate(parts):
        here = solved[:, h * count : (h + 1) * count]
        product = product + row_sum(part * here)
        if h:
            mine = jnp.where(parity_ref[0] == h, here, mine)
    return product, scale * resid + factor * mine


def first_kernel(
    factor, parity_ref, got_ref, high_ref, low_ref, resid_ref, scale_ref, dir_ref, send_ref, rho_ref, dots_ref
):
    count = resid_ref.shape[1]
    inverse = high_ref, low_ref
    parts, sums = gathered(got_ref, rho_ref.shape[1] // count, count)
    parts = [part * factor for part in parts]
    product, direction = next_direction(
        parity_ref, parts, inverse, resid_ref[...], scale_ref[...], sums[0], factor
    )
    dir_ref[...] = direction
    for p in range(send_ref.shape[0]):
        send_ref[p] = direction.astype(bf16)
    for h, part in enumerate(parts):
        rho_ref[:, h * count : (h + 1) * count] = part
    at = lax.broadcasted_iota(jnp.int32, dots_ref.shape, 1)
    dots_ref[...] = jnp.where(at == 0, sums[0], jnp.where(at == 1, product, 0.0))


def step_kernel(
    factor, parity_ref, got_ref, high_ref, low_ref, resid_ref, scale_ref, image_ref, old_ref, rho_ref, dots_ref, answer_ref,
    dir_ref, send_ref, new_rho_ref, new_dots_ref, new_resid_ref, new_answer_ref,
):
    count = resid_ref.shape[1]
    inverse = high_ref, low_ref
    parts, sums = gathered(got_ref, rho_ref.shape[1] // count, count)
    energy, product = lane(dots_ref[...], 0), lane(dots_ref[...], 1)
    alpha = product / sums[0]
    old = old_ref[...]
    new_answer_ref[...] = answer_ref[...] + alpha * old
    resid = resid_ref[...] - alpha * image_ref[...]
    new_resid_ref[...] = resid
    energy = energy - alpha * (2.0 * sums[1] - alpha * sums[2])
    parts = [
        rho_ref[:, h * count : (h + 1) * count] - alpha * (part * factor) for h, part in enumerate(parts)
    ]
    fresh, fine = next_direction(parity_ref, parts, inverse, resid, scale_ref[...], energy, factor)
    direction = fine + fresh / product * old
    dir_ref[...] = direction
    for p in range(send_ref.shape[0]):
        send_ref[p] = direction.astype(bf16)
    for h, part in enumerate(parts):
        new_rho_ref[:, h * count : (h + 1) * count] = part
    at = lax.broadcasted_iota(jnp.int32, dots_ref.shape, 1)
    new_dots_ref[...] = jnp.where(at == 0, energy, jnp.where(at == 1, fresh, 0.0))


def run_coarse(kernel, factor, n_dp, parity, *operands, more=0):
    rows, count = operands[3].shape
    vmem = pl.BlockSpec(memory_space=pltpu.VMEM)
    wide = jax.ShapeDtypeStruct((rows, count), f32)
    outs = [
        wide,
        jax.ShapeDtypeStruct((n_dp, rows, count), bf16),
        jax.ShapeDtypeStruct((rows, K), f32),
        jax.ShapeDtypeStruct((rows, SLOTS), f32),
    ] + [wide] * more
    return pl.pallas_call(
        functools.partial(kernel, factor),
        out_shape=outs,
        in_specs=[pl.BlockSpec(memory_space=pltpu.SMEM)] + [vmem] * len(operands),
        out_specs=[vmem] * len(outs),
        compiler_params=pltpu.CompilerParams(vmem_limit_bytes=50 * 1024 * 1024),
        cost_estimate=pl.CostEstimate(flops=10**8, bytes_accessed=5 * 2**20, transcendentals=0),
    )(parity, *operands)


def rounded(value):
    return lax.reduce_precision(value, 8, 7).astype(bf16)


def rounded(value):
    return lax.reduce_precision(value, 8, 7).astype(bf16)


def triple(value):
    high = lax.reduce_precision(value, 8, 7)
    mid = lax.reduce_precision(value - high, 8, 7)
    return jnp.stack([high, mid, value - high - mid], -1).astype(bf16)


def body(samples, projections, targets, feature_scale, coarse_factor):
    n_dp, n_sk = lax.axis_size(DP), lax.axis_size("sketch")
    count = projections.shape[2]
    width = targets.shape[1]
    mine = width // n_dp
    cols = width // n_sk
    factor = 1.0 / math.sqrt(F // K)
    halves = K // count
    parity = (lax.axis_index("sketch") % halves).astype(jnp.int32).reshape(1)
    n = samples.shape[0]
    scale = feature_scale[None, :]

    core = lax.axis_index("core").astype(jnp.int32).reshape(1)
    mine_proj = lax.all_to_all(repeat(projections, lax.axis_size("z")), "z", 0, 0)
    factor_high, factor_low, core = coarse_factor_inverse(core, coarse_factor)
    mine_proj, core = lax.optimization_barrier((mine_proj, core))
    other_proj = lax.ppermute(mine_proj, "core", [(0, 1), (1, 0)])
    feat, part = make_features(core, samples, mine_proj, other_proj, targets.T, n_dp)

    def scatter_dp(value):
        return lax.all_to_all(value, DP, 0, 0)

    def gather_sk(value):
        return lax.all_to_all(jnp.broadcast_to(value[None], (n_sk,) + value.shape), "sketch", 0, 0)

    def forward(send):
        whole = lax.all_to_all(send, DP, 0, 0)
        return whole, dot_turned(whole.reshape(width, count), feat)

    resid, sent = run_send(first_send_kernel, n_sk, scatter_dp(part), scale)
    inv_high, inv_low = coarse_inverse(factor_high, factor_low, resid)
    got = lax.all_to_all(sent, "sketch", 0, 0)
    direction, send, rho, dots = run_coarse(
        first_kernel, factor, n_dp, parity, got, inv_high, inv_low, resid, scale
    )
    answer = jnp.zeros_like(resid)
    for step in range(ITERS - 1):
        _, sums = forward(send)
        sums = lax.all_to_all(sums.astype(bf16).reshape(n_sk, cols, n), "sketch", 0, 0)
        u = rounded(jnp.sum(sums.astype(f32), 0))
        whole = gather_sk(u).reshape(width, n)
        parts = scatter_dp(dot(whole, feat).reshape(n_dp, mine, count))
        image, sent = run_send(step_send_kernel, n_sk, parts, scale, direction, resid)
        got = lax.all_to_all(sent, "sketch", 0, 0)
        direction, send, rho, dots, resid, answer = run_coarse(
            step_kernel, factor, n_dp, parity, got, inv_high, inv_low, resid, scale, image, direction, rho, dots, answer,
            more=2,
        )
    whole, sums = forward(send)
    got = lax.all_to_all(run_last_sums(n_sk, whole, sums), "sketch", 0, 0)
    sent = run_last_u(RIDGE / n_dp, got)
    got = lax.all_to_all(sent, "sketch", 0, 0).reshape(width, n + SLOTS)
    image = dot(got[:, :n], feat)
    sent = jnp.concatenate([image.astype(bf16), got[:, n:]], 1)
    got = lax.all_to_all(sent.reshape(n_dp, mine, count + SLOTS), DP, 0, 0).astype(f32)
    total = jnp.sum(got, 0)
    image = total[:, :count] + RIDGE * direction
    alpha = dots[:, 1:2] / row_sum(total[:, count:])
    out = jnp.stack([answer + alpha * direction, resid - alpha * image]).astype(bf16)
    got = lax.all_to_all(jnp.broadcast_to(out[None], (n_dp,) + out.shape), DP, 0, 0)
    answer, resid = outputs(got)
    return answer.T, resid.T


def solution(mesh):
    chips = mesh.shape["dp"] // 2
    mesh = jax.sharding.Mesh(mesh.devices.reshape(chips, 2, -1), ("z", "core", "sketch"))
    placed = (P(DP, None), P(None, DP, "sketch"), P(DP, None), P("sketch"), P())
    return jax.shard_map(
        body,
        mesh=mesh,
        in_specs=placed,
        out_specs=(P("sketch", None), P("sketch", None)),
        check_vma=False,
    )
```

```python
import functools
import math

import jax
import jax.numpy as jnp
from jax import lax
from jax.experimental import pallas as pl
from jax.experimental.pallas import tpu as pltpu
from jax.sharding import PartitionSpec as P

F = 16384
K = 1024
ITERS = 2
RIDGE = 0.5

f32 = jnp.float32
bf16 = jnp.bfloat16


def split(value):
    high = value.astype(bf16)
    return high, (value - high.astype(f32)).astype(bf16)


def dot(a, b):
    return lax.dot_general(a, b, (((1,), (0,)), ((), ())), preferred_element_type=f32)


def dot_turned(a, b):
    return lax.dot_general(a, b, (((1,), (1,)), ((), ())), preferred_element_type=f32)


def dot3(a, b):
    ah, al = split(a)
    bh, bl = split(b)
    return dot(ah, bh) + (dot(ah, bl) + dot(al, bh))


def dot2_left(a, exact):
    ah, al = split(a)
    return dot(ah, exact) + dot(al, exact)


def dot2_right(exact, b):
    bh, bl = split(b)
    return dot(exact, bh) + dot(exact, bl)


BLOCK = 256
DP = ("z", "core")


def inverse_kernel(core_ref, parity_ref, lower_hbm, high_ref, low_ref, made_core_ref, made_parity_ref, lower, inv, sems):
    n = lower.shape[0]
    blocks = n // BLOCK
    spans = [pl.ds(b * BLOCK, BLOCK) for b in range(blocks)]
    parts = [(span, span) for span in spans]
    size = BLOCK
    while size < n:
        parts += [(pl.ds(at + size, size), pl.ds(at, size)) for at in range(0, n, 2 * size)]
        size *= 2
    copies = [
        pltpu.make_async_copy(lower_hbm.at[part], lower.at[part], sems.at[k]) for k, part in enumerate(parts)
    ]
    for copy in copies:
        copy.start()
    made_core_ref[0], made_parity_ref[0] = core_ref[0], parity_ref[0]
    inv[...] = jnp.zeros_like(inv)
    rows = lax.broadcasted_iota(jnp.int32, (BLOCK, BLOCK), 0)
    cols = lax.broadcasted_iota(jnp.int32, (BLOCK, BLOCK), 1)

    def below(k):
        return ((rows >> k) == (cols >> k) + 1) & ((rows >> (k + 1)) == (cols >> (k + 1)))

    for copy, span in zip(copies, spans):
        copy.wait()
        block = lower[span, span].astype(f32)
        diag = jnp.where(rows == cols, block, 0.0)
        down = 1.0 / jnp.sum(diag, axis=1, keepdims=True)
        across = 1.0 / jnp.sum(diag, axis=0, keepdims=True)
        inv[span, span] = jnp.where(rows == cols, down, jnp.where(below(0), -(block * down) * across, 0.0))

    def level(k, carry):
        mask = below(k)
        for span in spans:
            x = inv[span, span]
            off = jnp.where(mask, lower[span, span].astype(f32), 0.0).astype(bf16)
            inv[span, span] = x - dot3(dot2_left(x, off), x)
        return carry

    lax.fori_loop(1, int(math.log2(BLOCK)), level, 0)
    for copy, (bottom, top) in list(zip(copies, parts))[blocks:]:
        copy.wait()
        a, b = inv[top, top], inv[bottom, bottom]
        inv[bottom, top] = -dot3(b, dot2_right(lower[bottom, top], a))
    for span in spans:
        high_ref[span, :], low_ref[span, :] = split(inv[span, :])


def coarse_factor_inverse(core, parity, lower):
    n = lower.shape[0]
    vmem = pl.BlockSpec(memory_space=pltpu.VMEM)
    return pl.pallas_call(
        inverse_kernel,
        out_shape=[jax.ShapeDtypeStruct((n, n), bf16)] * 2 + [jax.ShapeDtypeStruct((1,), jnp.int32)] * 2,
        in_specs=[pl.BlockSpec(memory_space=pltpu.SMEM)] * 2 + [pl.BlockSpec(memory_space=pl.ANY)],
        out_specs=[vmem] * 2 + [pl.BlockSpec(memory_space=pltpu.SMEM)] * 2,
        scratch_shapes=[
            pltpu.VMEM((n, n), bf16),
            pltpu.VMEM((n, n), f32),
            pltpu.SemaphoreType.DMA((2 * (n // BLOCK) - 1,)),
        ],
        compiler_params=pltpu.CompilerParams(vmem_limit_bytes=56 * 1024 * 1024),
        cost_estimate=pl.CostEstimate(flops=10**10, bytes_accessed=6 * 2**20, transcendentals=0),
    )(core, parity, lower)


def place(a, b):
    return pl.ds((a * (a + 1) // 2 + b) * BLOCK, BLOCK)


def product_kernel(xh_ref, xl_ref, order_hbm, high_ref, low_ref):
    del order_hbm
    spans = [slice(b, b + BLOCK) for b in range(0, xh_ref.shape[0], BLOCK)]
    parts = [[(xh_ref[row, col], xl_ref[row, col]) for col in spans[: r + 1]] for r, row in enumerate(spans)]
    turned = [[tuple(half.astype(f32).T.astype(bf16) for half in part) for part in row] for row in parts]
    for a in range(len(spans)):
        for b in range(a + 1):
            total = None
            for k in range(a, len(spans)):
                (ah, al), (bh, bl) = turned[k][a], parts[k][b]
                term = dot(ah, bh) + (dot(ah, bl) + dot(al, bh))
                total = term if total is None else total + term
            high_ref[place(a, b), :], low_ref[place(a, b), :] = split(total)


def coarse_inverse(xh, xl, order):
    n = xh.shape[0]
    blocks = n // BLOCK
    vmem = pl.BlockSpec(memory_space=pltpu.VMEM)
    return pl.pallas_call(
        product_kernel,
        out_shape=[jax.ShapeDtypeStruct((blocks * (blocks + 1) // 2 * BLOCK, BLOCK), bf16)] * 2,
        in_specs=[vmem, vmem, pl.BlockSpec(memory_space=pl.ANY)],
        out_specs=[vmem] * 2,
        compiler_params=pltpu.CompilerParams(vmem_limit_bytes=52 * 1024 * 1024),
        cost_estimate=pl.CostEstimate(flops=4 * 10**9, bytes_accessed=8 * 2**20, transcendentals=0),
    )(xh, xl, order)


def repeat_kernel(value_hbm, out_hbm, value, sems):
    get = pltpu.make_async_copy(value_hbm, value, sems.at[0])
    get.start()
    get.wait()
    puts = [pltpu.make_async_copy(value, out_hbm.at[p], sems.at[p + 1]) for p in range(out_hbm.shape[0])]
    for put in puts:
        put.start()
    for put in puts:
        put.wait()


def repeat(value, count):
    anywhere = pl.BlockSpec(memory_space=pl.ANY)
    return pl.pallas_call(
        repeat_kernel,
        out_shape=jax.ShapeDtypeStruct((count,) + value.shape, value.dtype),
        in_specs=[anywhere],
        out_specs=anywhere,
        scratch_shapes=[pltpu.VMEM(value.shape, value.dtype), pltpu.SemaphoreType.DMA((count + 1,))],
        compiler_params=pltpu.CompilerParams(vmem_limit_bytes=56 * 1024 * 1024),
    )(value)


def output_kernel(got_ref, answer_hbm, resid_hbm, value, sems):
    rows, puts = got_ref.shape[2], []
    for k, out in enumerate((answer_hbm, resid_hbm)):
        for p in range(got_ref.shape[0]):
            value[k, p * rows : (p + 1) * rows, :] = got_ref[p, k].astype(f32)
        puts.append(pltpu.make_async_copy(value.at[k], out, sems.at[k]))
        puts[k].start()
    for put in puts:
        put.wait()


def outputs(got):
    parts, _, rows, count = got.shape
    return pl.pallas_call(
        output_kernel,
        out_shape=[jax.ShapeDtypeStruct((parts * rows, count), f32)] * 2,
        in_specs=[pl.BlockSpec(memory_space=pltpu.VMEM)],
        out_specs=[pl.BlockSpec(memory_space=pl.ANY)] * 2,
        scratch_shapes=[pltpu.VMEM((2, parts * rows, count), f32), pltpu.SemaphoreType.DMA((2,))],
        compiler_params=pltpu.CompilerParams(vmem_limit_bytes=8 * 1024 * 1024),
    )(got)


def feature_kernel(core_ref, samples_ref, mine_ref, other_ref, targets_ref, feat_ref, part_ref, proj):
    core = core_ref[0]
    for j in range(proj.shape[0]):
        proj[j, :, core] = mine_ref[:, j]
        proj[j, :, 1 - core] = other_ref[:, j]
    samples, value = samples_ref[...], None
    for j in range(proj.shape[0]):
        panel = dot(samples, proj[j].reshape(samples.shape[1], proj.shape[-1]))
        value = panel if value is None else value * panel
    feat = (value * (1.0 / math.sqrt(F))).astype(bf16)
    feat_ref[...] = feat
    total = dot(targets_ref[...], feat)
    step = part_ref.shape[1]
    for p in range(part_ref.shape[0]):
        part_ref[p] = total[p * step : (p + 1) * step, :]


def make_features(core, samples, mine, other, targets_t, parts):
    n = samples.shape[0]
    chips, panels, rows, width = mine.shape
    vmem = pl.BlockSpec(memory_space=pltpu.VMEM)
    return pl.pallas_call(
        feature_kernel,
        out_shape=[
            jax.ShapeDtypeStruct((n, width), bf16),
            jax.ShapeDtypeStruct((parts, targets_t.shape[0] // parts, width), f32),
        ],
        in_specs=[pl.BlockSpec(memory_space=pltpu.SMEM)] + [vmem] * 4,
        out_specs=[vmem] * 2,
        scratch_shapes=[pltpu.VMEM((panels, chips, 2, rows, width), bf16)],
        compiler_params=pltpu.CompilerParams(vmem_limit_bytes=49 * 1024 * 1024),
        cost_estimate=pl.CostEstimate(flops=2 * 10**9, bytes_accessed=5 * 2**20, transcendentals=0),
    )(core, samples, mine, other, targets_t)


SLOTS = 128


def row_sum(value):
    return jnp.sum(value, axis=1, keepdims=True)


def lane(value, k):
    at = lax.broadcasted_iota(jnp.int32, value.shape, 1)
    return row_sum(jnp.where(at == k, value, 0.0))


def lanes_of(values):
    at = lax.broadcasted_iota(jnp.int32, (values[0].shape[0], SLOTS), 1)
    total = jnp.zeros(at.shape, f32)
    for k, value in enumerate(values):
        for piece in range(3):
            part = value.astype(bf16).astype(f32)
            total = jnp.where(at == 3 * k + piece, part, total)
            value = value - part
    return total


def summed(ref):
    total = ref[0].astype(f32)
    for p in range(1, ref.shape[0]):
        total = total + ref[p].astype(f32)
    return total


def spread(send_ref, value, dots):
    sent = jnp.concatenate([value, lanes_of(dots)], 1).astype(bf16)
    for p in range(send_ref.shape[0]):
        send_ref[p] = sent


def first_send_kernel(got_ref, scale_ref, value_ref, send_ref):
    value = summed(got_ref)
    value_ref[...] = value
    spread(send_ref, value, [row_sum(scale_ref[...] * value * value)])


def step_send_kernel(got_ref, scale_ref, direction_ref, resid_ref, value_ref, send_ref):
    direction = direction_ref[...]
    value = summed(got_ref) + RIDGE * direction
    value_ref[...] = value
    weighted = scale_ref[...] * value
    spread(
        send_ref, value, [row_sum(direction * value), row_sum(weighted * resid_ref[...]), row_sum(weighted * value)]
    )


def run_send(kernel, n_sk, got, *operands):
    _, rows, count = got.shape
    vmem = pl.BlockSpec(memory_space=pltpu.VMEM)
    return pl.pallas_call(
        kernel,
        out_shape=[
            jax.ShapeDtypeStruct((rows, count), f32),
            jax.ShapeDtypeStruct((n_sk, rows, count + SLOTS), bf16),
        ],
        in_specs=[vmem] * (1 + len(operands)),
        out_specs=[vmem] * 2,
        compiler_params=pltpu.CompilerParams(vmem_limit_bytes=8 * 1024 * 1024),
    )(got, *operands)


def last_sums_kernel(whole_ref, sums_ref, send_ref):
    parts, rows, cols = whole_ref.shape[0], whole_ref.shape[1], send_ref.shape[1]
    for p in range(parts):
        value = whole_ref[p].astype(f32)
        sent = jnp.concatenate([sums_ref[p * rows : (p + 1) * rows, :], lanes_of([row_sum(value * value)])], 1)
        for k in range(rows // cols):
            send_ref[p * (rows // cols) + k] = sent[k * cols : (k + 1) * cols, :].astype(bf16)


def run_last_sums(n_sk, whole, sums):
    width, n = sums.shape
    vmem = pl.BlockSpec(memory_space=pltpu.VMEM)
    return pl.pallas_call(
        last_sums_kernel,
        out_shape=jax.ShapeDtypeStruct((n_sk, width // n_sk, n + SLOTS), bf16),
        in_specs=[vmem] * 2,
        out_specs=vmem,
        compiler_params=pltpu.CompilerParams(vmem_limit_bytes=8 * 1024 * 1024),
    )(whole, sums)


def last_u_kernel(share, got_ref, send_ref):
    total = summed(got_ref)
    n = total.shape[1] - SLOTS
    u = total[:, :n].astype(bf16).astype(f32)
    spread(send_ref, u, [row_sum(total[:, :n] * u) + share * row_sum(total[:, n:])])


def run_last_u(share, got):
    vmem = pl.BlockSpec(memory_space=pltpu.VMEM)
    return pl.pallas_call(
        functools.partial(last_u_kernel, share),
        out_shape=jax.ShapeDtypeStruct(got.shape, bf16),
        in_specs=[vmem],
        out_specs=vmem,
        compiler_params=pltpu.CompilerParams(vmem_limit_bytes=8 * 1024 * 1024),
    )(got)


def gathered(got_ref, halves, count):
    parts = []
    for h in range(halves):
        acc = got_ref[h, :, :count].astype(f32)
        for p in range(h + halves, got_ref.shape[0], halves):
            acc = acc + got_ref[p, :, :count].astype(f32)
        parts.append(acc)
    dots = got_ref[0, :, count:].astype(f32)
    for p in range(1, got_ref.shape[0]):
        dots = dots + got_ref[p, :, count:].astype(f32)
    at = lax.broadcasted_iota(jnp.int32, dots.shape, 1)
    sums = [row_sum(jnp.where((at >= 3 * k) & (at < 3 * k + 3), dots, 0.0)) for k in range(3)]
    return parts, sums


def coarse(parts, inverse):
    high_ref, low_ref = inverse
    rows, sides = parts[0].shape[0], []
    for part in parts:
        high = part.astype(bf16).astype(f32)
        both = jnp.concatenate([high, part - high], 0).astype(bf16)
        sides += [both[:, at : at + BLOCK] for at in range(0, part.shape[1], BLOCK)]
    blocks = range(len(sides))

    def times(ref, both, a, b):
        return dot(both, ref[place(a, b), :]) if a >= b else dot_turned(both, ref[place(b, a), :])

    solved = []
    for b in blocks:
        one = sum(times(high_ref, sides[a], a, b) for a in blocks)
        solved.append(one[:rows] + one[rows:])
    for b in blocks:
        solved[b] = solved[b] + sum(times(low_ref, sides[a], a, b) for a in blocks)[:rows]
    return jnp.concatenate(solved, 1)


def next_direction(parity_ref, parts, inverse, resid, scale, energy, factor):
    count = resid.shape[1]
    solved = coarse(parts, inverse)
    product = energy
    mine = solved[:, :count]
    for h, part in enumerate(parts):
        here = solved[:, h * count : (h + 1) * count]
        product = product + row_sum(part * here)
        if h:
            mine = jnp.where(parity_ref[0] == h, here, mine)
    return product, scale * resid + factor * mine


def first_kernel(
    factor, parity_ref, got_ref, high_ref, low_ref, resid_ref, scale_ref, dir_ref, send_ref, rho_ref, dots_ref
):
    count = resid_ref.shape[1]
    inverse = high_ref, low_ref
    parts, sums = gathered(got_ref, rho_ref.shape[1] // count, count)
    parts = [part * factor for part in parts]
    product, direction = next_direction(
        parity_ref, parts, inverse, resid_ref[...], scale_ref[...], sums[0], factor
    )
    dir_ref[...] = direction
    for p in range(send_ref.shape[0]):
        send_ref[p] = direction.astype(bf16)
    for h, part in enumerate(parts):
        rho_ref[:, h * count : (h + 1) * count] = part
    at = lax.broadcasted_iota(jnp.int32, dots_ref.shape, 1)
    dots_ref[...] = jnp.where(at == 0, sums[0], jnp.where(at == 1, product, 0.0))


def step_kernel(
    factor, parity_ref, got_ref, high_ref, low_ref, resid_ref, scale_ref, image_ref, old_ref, rho_ref, dots_ref, answer_ref,
    dir_ref, send_ref, new_rho_ref, new_dots_ref, new_resid_ref, new_answer_ref,
):
    count = resid_ref.shape[1]
    inverse = high_ref, low_ref
    parts, sums = gathered(got_ref, rho_ref.shape[1] // count, count)
    energy, product = lane(dots_ref[...], 0), lane(dots_ref[...], 1)
    alpha = product / sums[0]
    old = old_ref[...]
    new_answer_ref[...] = answer_ref[...] + alpha * old
    resid = resid_ref[...] - alpha * image_ref[...]
    new_resid_ref[...] = resid
    energy = energy - alpha * (2.0 * sums[1] - alpha * sums[2])
    parts = [
        rho_ref[:, h * count : (h + 1) * count] - alpha * (part * factor) for h, part in enumerate(parts)
    ]
    fresh, fine = next_direction(parity_ref, parts, inverse, resid, scale_ref[...], energy, factor)
    direction = fine + fresh / product * old
    dir_ref[...] = direction
    for p in range(send_ref.shape[0]):
        send_ref[p] = direction.astype(bf16)
    for h, part in enumerate(parts):
        new_rho_ref[:, h * count : (h + 1) * count] = part
    at = lax.broadcasted_iota(jnp.int32, dots_ref.shape, 1)
    new_dots_ref[...] = jnp.where(at == 0, energy, jnp.where(at == 1, fresh, 0.0))


def run_coarse(kernel, factor, n_dp, parity, *operands, more=0):
    rows, count = operands[3].shape
    vmem = pl.BlockSpec(memory_space=pltpu.VMEM)
    wide = jax.ShapeDtypeStruct((rows, count), f32)
    outs = [
        wide,
        jax.ShapeDtypeStruct((n_dp, rows, count), bf16),
        jax.ShapeDtypeStruct((rows, K), f32),
        jax.ShapeDtypeStruct((rows, SLOTS), f32),
    ] + [wide] * more
    return pl.pallas_call(
        functools.partial(kernel, factor),
        out_shape=outs,
        in_specs=[pl.BlockSpec(memory_space=pltpu.SMEM)] + [vmem] * len(operands),
        out_specs=[vmem] * len(outs),
        compiler_params=pltpu.CompilerParams(vmem_limit_bytes=50 * 1024 * 1024),
        cost_estimate=pl.CostEstimate(flops=10**8, bytes_accessed=5 * 2**20, transcendentals=0),
    )(parity, *operands)


def rounded(value):
    return lax.reduce_precision(value, 8, 7).astype(bf16)


def rounded(value):
    return lax.reduce_precision(value, 8, 7).astype(bf16)


def triple(value):
    high = lax.reduce_precision(value, 8, 7)
    mid = lax.reduce_precision(value - high, 8, 7)
    return jnp.stack([high, mid, value - high - mid], -1).astype(bf16)


def body(samples, projections, targets, feature_scale, coarse_factor):
    n_dp, n_sk = lax.axis_size(DP), lax.axis_size("sketch")
    count = projections.shape[2]
    width = targets.shape[1]
    mine = width // n_dp
    cols = width // n_sk
    factor = 1.0 / math.sqrt(F // K)
    halves = K // count
    n = samples.shape[0]
    scale = feature_scale[None, :]

    core = lax.axis_index("core").astype(jnp.int32).reshape(1)
    parity = (lax.axis_index("sketch") % halves).astype(jnp.int32).reshape(1)
    mine_proj = lax.all_to_all(repeat(projections, lax.axis_size("z")), "z", 0, 0)
    factor_high, factor_low, core, parity = coarse_factor_inverse(core, parity, coarse_factor)
    mine_proj, core = lax.optimization_barrier((mine_proj, core))
    other_proj = lax.ppermute(mine_proj, "core", [(0, 1), (1, 0)])
    feat, part = make_features(core, samples, mine_proj, other_proj, targets.T, n_dp)

    def scatter_dp(value):
        return lax.all_to_all(value, DP, 0, 0)

    def gather_sk(value):
        return lax.all_to_all(jnp.broadcast_to(value[None], (n_sk,) + value.shape), "sketch", 0, 0)

    def forward(send):
        whole = lax.all_to_all(send, DP, 0, 0)
        return whole, dot_turned(whole.reshape(width, count), feat)

    resid, sent = run_send(first_send_kernel, n_sk, scatter_dp(part), scale)
    inv_high, inv_low = coarse_inverse(factor_high, factor_low, resid)
    got = lax.all_to_all(sent, "sketch", 0, 0)
    direction, send, rho, dots = run_coarse(
        first_kernel, factor, n_dp, parity, got, inv_high, inv_low, resid, scale
    )
    answer = jnp.zeros_like(resid)
    for step in range(ITERS - 1):
        _, sums = forward(send)
        sums = lax.all_to_all(sums.astype(bf16).reshape(n_sk, cols, n), "sketch", 0, 0)
        u = rounded(jnp.sum(sums.astype(f32), 0))
        whole = gather_sk(u).reshape(width, n)
        parts = scatter_dp(dot(whole, feat).reshape(n_dp, mine, count))
        image, sent = run_send(step_send_kernel, n_sk, parts, scale, direction, resid)
        got = lax.all_to_all(sent, "sketch", 0, 0)
        direction, send, rho, dots, resid, answer = run_coarse(
            step_kernel, factor, n_dp, parity, got, inv_high, inv_low, resid, scale, image, direction, rho, dots, answer,
            more=2,
        )
    whole, sums = forward(send)
    got = lax.all_to_all(run_last_sums(n_sk, whole, sums), "sketch", 0, 0)
    sent = run_last_u(RIDGE / n_dp, got)
    got = lax.all_to_all(sent, "sketch", 0, 0).reshape(width, n + SLOTS)
    image = dot(got[:, :n], feat)
    sent = jnp.concatenate([image.astype(bf16), got[:, n:]], 1)
    got = lax.all_to_all(sent.reshape(n_dp, mine, count + SLOTS), DP, 0, 0).astype(f32)
    total = jnp.sum(got, 0)
    image = total[:, :count] + RIDGE * direction
    alpha = dots[:, 1:2] / row_sum(total[:, count:])
    out = jnp.stack([answer + alpha * direction, resid - alpha * image]).astype(bf16)
    got = lax.all_to_all(jnp.broadcast_to(out[None], (n_dp,) + out.shape), DP, 0, 0)
    answer, resid = outputs(got)
    return answer.T, resid.T


def solution(mesh):
    chips = mesh.shape["dp"] // 2
    mesh = jax.sharding.Mesh(mesh.devices.reshape(chips, 2, -1), ("z", "core", "sketch"))
    placed = (P(DP, None), P(None, DP, "sketch"), P(DP, None), P("sketch"), P())
    return jax.shard_map(
        body,
        mesh=mesh,
        in_specs=placed,
        out_specs=(P("sketch", None), P("sketch", None)),
        check_vma=False,
    )
```

```python
import functools
import math

import jax
import jax.numpy as jnp
from jax import lax
from jax.experimental import pallas as pl
from jax.experimental.pallas import tpu as pltpu
from jax.sharding import PartitionSpec as P

F = 16384
K = 1024
ITERS = 2
RIDGE = 0.5

f32 = jnp.float32
bf16 = jnp.bfloat16


def split(value):
    high = value.astype(bf16)
    return high, (value - high.astype(f32)).astype(bf16)


def dot(a, b):
    return lax.dot_general(a, b, (((1,), (0,)), ((), ())), preferred_element_type=f32)


def dot_turned(a, b):
    return lax.dot_general(a, b, (((1,), (1,)), ((), ())), preferred_element_type=f32)


def dot3(a, b):
    ah, al = split(a)
    bh, bl = split(b)
    return dot(ah, bh) + (dot(ah, bl) + dot(al, bh))


def dot2_left(a, exact):
    ah, al = split(a)
    return dot(ah, exact) + dot(al, exact)


def dot2_right(exact, b):
    bh, bl = split(b)
    return dot(exact, bh) + dot(exact, bl)


BLOCK = 256
DP = ("z", "core")


def inverse_kernel(core_ref, parity_ref, lower_hbm, high_ref, low_ref, made_core_ref, made_parity_ref, lower, inv, sems):
    n = lower.shape[0]
    blocks = n // BLOCK
    spans = [pl.ds(b * BLOCK, BLOCK) for b in range(blocks)]
    parts = [(span, span) for span in spans]
    size = BLOCK
    while size < n:
        parts += [(pl.ds(at + size, size), pl.ds(at, size)) for at in range(0, n, 2 * size)]
        size *= 2
    copies = [
        pltpu.make_async_copy(lower_hbm.at[part], lower.at[part], sems.at[k]) for k, part in enumerate(parts)
    ]
    for copy in copies:
        copy.start()
    made_core_ref[0], made_parity_ref[0] = core_ref[0], parity_ref[0]
    inv[...] = jnp.zeros_like(inv)
    rows = lax.broadcasted_iota(jnp.int32, (BLOCK, BLOCK), 0)
    cols = lax.broadcasted_iota(jnp.int32, (BLOCK, BLOCK), 1)

    def below(k):
        return ((rows >> k) == (cols >> k) + 1) & ((rows >> (k + 1)) == (cols >> (k + 1)))

    for copy, span in zip(copies, spans):
        copy.wait()
        block = lower[span, span].astype(f32)
        diag = jnp.where(rows == cols, block, 0.0)
        down = 1.0 / jnp.sum(diag, axis=1, keepdims=True)
        across = 1.0 / jnp.sum(diag, axis=0, keepdims=True)
        inv[span, span] = jnp.where(rows == cols, down, jnp.where(below(0), -(block * down) * across, 0.0))

    def level(k, carry):
        mask = below(k)
        for span in spans:
            x = inv[span, span]
            off = jnp.where(mask, lower[span, span].astype(f32), 0.0).astype(bf16)
            inv[span, span] = x - dot3(dot2_left(x, off), x)
        return carry

    lax.fori_loop(1, int(math.log2(BLOCK)), level, 0)
    for copy, (bottom, top) in list(zip(copies, parts))[blocks:]:
        copy.wait()
        a, b = inv[top, top], inv[bottom, bottom]
        inv[bottom, top] = -dot3(b, dot2_right(lower[bottom, top], a))
    for span in spans:
        high_ref[span, :], low_ref[span, :] = split(inv[span, :])


def coarse_factor_inverse(core, parity, lower):
    n = lower.shape[0]
    vmem = pl.BlockSpec(memory_space=pltpu.VMEM)
    return pl.pallas_call(
        inverse_kernel,
        out_shape=[jax.ShapeDtypeStruct((n, n), bf16)] * 2 + [jax.ShapeDtypeStruct((1,), jnp.int32)] * 2,
        in_specs=[pl.BlockSpec(memory_space=pltpu.SMEM)] * 2 + [pl.BlockSpec(memory_space=pl.ANY)],
        out_specs=[vmem] * 2 + [pl.BlockSpec(memory_space=pltpu.SMEM)] * 2,
        scratch_shapes=[
            pltpu.VMEM((n, n), bf16),
            pltpu.VMEM((n, n), f32),
            pltpu.SemaphoreType.DMA((2 * (n // BLOCK) - 1,)),
        ],
        compiler_params=pltpu.CompilerParams(vmem_limit_bytes=56 * 1024 * 1024),
        cost_estimate=pl.CostEstimate(flops=10**10, bytes_accessed=6 * 2**20, transcendentals=0),
    )(core, parity, lower)


def place(a, b):
    return pl.ds((a * (a + 1) // 2 + b) * BLOCK, BLOCK)


def product_kernel(xh_ref, xl_ref, order_hbm, high_ref, low_ref):
    del order_hbm
    spans = [slice(b, b + BLOCK) for b in range(0, xh_ref.shape[0], BLOCK)]
    parts = [[(xh_ref[row, col], xl_ref[row, col]) for col in spans[: r + 1]] for r, row in enumerate(spans)]
    turned = [[tuple(half.astype(f32).T.astype(bf16) for half in part) for part in row] for row in parts]
    for a in range(len(spans)):
        for b in range(a + 1):
            total = None
            for k in range(a, len(spans)):
                (ah, al), (bh, bl) = turned[k][a], parts[k][b]
                term = dot(ah, bh) + (dot(ah, bl) + dot(al, bh))
                total = term if total is None else total + term
            high_ref[place(a, b), :], low_ref[place(a, b), :] = split(total)


def coarse_inverse(xh, xl, order):
    n = xh.shape[0]
    blocks = n // BLOCK
    vmem = pl.BlockSpec(memory_space=pltpu.VMEM)
    return pl.pallas_call(
        product_kernel,
        out_shape=[jax.ShapeDtypeStruct((blocks * (blocks + 1) // 2 * BLOCK, BLOCK), bf16)] * 2,
        in_specs=[vmem, vmem, pl.BlockSpec(memory_space=pl.ANY)],
        out_specs=[vmem] * 2,
        compiler_params=pltpu.CompilerParams(vmem_limit_bytes=52 * 1024 * 1024),
        cost_estimate=pl.CostEstimate(flops=4 * 10**9, bytes_accessed=8 * 2**20, transcendentals=0),
    )(xh, xl, order)


def repeat_kernel(value_hbm, out_hbm, value, sems):
    get = pltpu.make_async_copy(value_hbm, value, sems.at[0])
    get.start()
    get.wait()
    puts = [pltpu.make_async_copy(value, out_hbm.at[p], sems.at[p + 1]) for p in range(out_hbm.shape[0])]
    for put in puts:
        put.start()
    for put in puts:
        put.wait()


def repeat(value, count):
    anywhere = pl.BlockSpec(memory_space=pl.ANY)
    return pl.pallas_call(
        repeat_kernel,
        out_shape=jax.ShapeDtypeStruct((count,) + value.shape, value.dtype),
        in_specs=[anywhere],
        out_specs=anywhere,
        scratch_shapes=[pltpu.VMEM(value.shape, value.dtype), pltpu.SemaphoreType.DMA((count + 1,))],
        compiler_params=pltpu.CompilerParams(vmem_limit_bytes=56 * 1024 * 1024),
    )(value)


def output_kernel(got_ref, answer_hbm, resid_hbm, value, sems):
    rows, puts = got_ref.shape[2], []
    for k, out in enumerate((answer_hbm, resid_hbm)):
        for p in range(got_ref.shape[0]):
            value[k, p * rows : (p + 1) * rows, :] = got_ref[p, k].astype(f32)
        puts.append(pltpu.make_async_copy(value.at[k], out, sems.at[k]))
        puts[k].start()
    for put in puts:
        put.wait()


def outputs(got):
    parts, _, rows, count = got.shape
    return pl.pallas_call(
        output_kernel,
        out_shape=[jax.ShapeDtypeStruct((parts * rows, count), f32)] * 2,
        in_specs=[pl.BlockSpec(memory_space=pltpu.VMEM)],
        out_specs=[pl.BlockSpec(memory_space=pl.ANY)] * 2,
        scratch_shapes=[pltpu.VMEM((2, parts * rows, count), f32), pltpu.SemaphoreType.DMA((2,))],
        compiler_params=pltpu.CompilerParams(vmem_limit_bytes=8 * 1024 * 1024),
    )(got)


def feature_kernel(core_ref, samples_ref, mine_ref, other_ref, targets_ref, feat_ref, part_ref, proj):
    core = core_ref[0]
    for j in range(proj.shape[0]):
        proj[j, :, core] = mine_ref[:, j]
        proj[j, :, 1 - core] = other_ref[:, j]
    samples, value = samples_ref[...], None
    for j in range(proj.shape[0]):
        panel = dot(samples, proj[j].reshape(samples.shape[1], proj.shape[-1]))
        value = panel if value is None else value * panel
    feat = (value * (1.0 / math.sqrt(F))).astype(bf16)
    feat_ref[...] = feat
    total = dot(targets_ref[...], feat)
    step = part_ref.shape[1]
    for p in range(part_ref.shape[0]):
        part_ref[p] = total[p * step : (p + 1) * step, :]


def make_features(core, samples, mine, other, targets_t, parts):
    n = samples.shape[0]
    chips, panels, rows, width = mine.shape
    vmem = pl.BlockSpec(memory_space=pltpu.VMEM)
    return pl.pallas_call(
        feature_kernel,
        out_shape=[
            jax.ShapeDtypeStruct((n, width), bf16),
            jax.ShapeDtypeStruct((parts, targets_t.shape[0] // parts, width), f32),
        ],
        in_specs=[pl.BlockSpec(memory_space=pltpu.SMEM)] + [vmem] * 4,
        out_specs=[vmem] * 2,
        scratch_shapes=[pltpu.VMEM((panels, chips, 2, rows, width), bf16)],
        compiler_params=pltpu.CompilerParams(vmem_limit_bytes=49 * 1024 * 1024),
        cost_estimate=pl.CostEstimate(flops=2 * 10**9, bytes_accessed=5 * 2**20, transcendentals=0),
    )(core, samples, mine, other, targets_t)


SLOTS = 128


def row_sum(value):
    return jnp.sum(value, axis=1, keepdims=True)


def lane(value, k):
    at = lax.broadcasted_iota(jnp.int32, value.shape, 1)
    return row_sum(jnp.where(at == k, value, 0.0))


def lanes_of(values):
    at = lax.broadcasted_iota(jnp.int32, (values[0].shape[0], SLOTS), 1)
    total = jnp.zeros(at.shape, f32)
    for k, value in enumerate(values):
        for piece in range(3):
            part = value.astype(bf16).astype(f32)
            total = jnp.where(at == 3 * k + piece, part, total)
            value = value - part
    return total


def summed(ref):
    total = ref[0].astype(f32)
    for p in range(1, ref.shape[0]):
        total = total + ref[p].astype(f32)
    return total


def spread(send_ref, value, dots):
    sent = jnp.concatenate([value, lanes_of(dots)], 1).astype(bf16)
    for p in range(send_ref.shape[0]):
        send_ref[p] = sent


def first_send_kernel(got_ref, scale_ref, value_ref, send_ref):
    value = summed(got_ref)
    value_ref[...] = value
    spread(send_ref, value, [row_sum(scale_ref[...] * value * value)])


def step_send_kernel(got_ref, scale_ref, direction_ref, resid_ref, value_ref, send_ref):
    direction = direction_ref[...]
    value = summed(got_ref) + RIDGE * direction
    value_ref[...] = value
    weighted = scale_ref[...] * value
    spread(
        send_ref, value, [row_sum(direction * value), row_sum(weighted * resid_ref[...]), row_sum(weighted * value)]
    )


def run_send(kernel, n_sk, got, *operands):
    _, rows, count = got.shape
    vmem = pl.BlockSpec(memory_space=pltpu.VMEM)
    return pl.pallas_call(
        kernel,
        out_shape=[
            jax.ShapeDtypeStruct((rows, count), f32),
            jax.ShapeDtypeStruct((n_sk, rows, count + SLOTS), bf16),
        ],
        in_specs=[vmem] * (1 + len(operands)),
        out_specs=[vmem] * 2,
        compiler_params=pltpu.CompilerParams(vmem_limit_bytes=8 * 1024 * 1024),
    )(got, *operands)


def last_step_kernel(got_ref, direction_ref, dots_ref, answer_ref, resid_ref, send_ref):
    count = direction_ref.shape[1]
    total, direction = summed(got_ref), direction_ref[...]
    image = total[:, :count] + RIDGE * direction
    alpha = lane(dots_ref[...], 1) / row_sum(total[:, count:])
    answer = (answer_ref[...] + alpha * direction).astype(bf16)
    resid = (resid_ref[...] - alpha * image).astype(bf16)
    for p in range(send_ref.shape[0]):
        send_ref[p, 0] = answer
        send_ref[p, 1] = resid


def run_last_step(got, *operands):
    vmem = pl.BlockSpec(memory_space=pltpu.VMEM)
    return pl.pallas_call(
        last_step_kernel,
        out_shape=jax.ShapeDtypeStruct((got.shape[0], 2) + operands[0].shape, bf16),
        in_specs=[vmem] * (1 + len(operands)),
        out_specs=vmem,
        compiler_params=pltpu.CompilerParams(vmem_limit_bytes=8 * 1024 * 1024),
    )(got, *operands)


def last_sums_kernel(whole_ref, sums_ref, send_ref):
    parts, rows, cols = whole_ref.shape[0], whole_ref.shape[1], send_ref.shape[1]
    for p in range(parts):
        value = whole_ref[p].astype(f32)
        sent = jnp.concatenate([sums_ref[p * rows : (p + 1) * rows, :], lanes_of([row_sum(value * value)])], 1)
        for k in range(rows // cols):
            send_ref[p * (rows // cols) + k] = sent[k * cols : (k + 1) * cols, :].astype(bf16)


def run_last_sums(n_sk, whole, sums):
    width, n = sums.shape
    vmem = pl.BlockSpec(memory_space=pltpu.VMEM)
    return pl.pallas_call(
        last_sums_kernel,
        out_shape=jax.ShapeDtypeStruct((n_sk, width // n_sk, n + SLOTS), bf16),
        in_specs=[vmem] * 2,
        out_specs=vmem,
        compiler_params=pltpu.CompilerParams(vmem_limit_bytes=8 * 1024 * 1024),
    )(whole, sums)


def last_u_kernel(share, got_ref, send_ref):
    total = summed(got_ref)
    n = total.shape[1] - SLOTS
    u = total[:, :n].astype(bf16).astype(f32)
    spread(send_ref, u, [row_sum(total[:, :n] * u) + share * row_sum(total[:, n:])])


def run_last_u(share, got):
    vmem = pl.BlockSpec(memory_space=pltpu.VMEM)
    return pl.pallas_call(
        functools.partial(last_u_kernel, share),
        out_shape=jax.ShapeDtypeStruct(got.shape, bf16),
        in_specs=[vmem],
        out_specs=vmem,
        compiler_params=pltpu.CompilerParams(vmem_limit_bytes=8 * 1024 * 1024),
    )(got)


def gathered(got_ref, halves, count):
    parts = []
    for h in range(halves):
        acc = got_ref[h, :, :count].astype(f32)
        for p in range(h + halves, got_ref.shape[0], halves):
            acc = acc + got_ref[p, :, :count].astype(f32)
        parts.append(acc)
    dots = got_ref[0, :, count:].astype(f32)
    for p in range(1, got_ref.shape[0]):
        dots = dots + got_ref[p, :, count:].astype(f32)
    at = lax.broadcasted_iota(jnp.int32, dots.shape, 1)
    sums = [row_sum(jnp.where((at >= 3 * k) & (at < 3 * k + 3), dots, 0.0)) for k in range(3)]
    return parts, sums


def coarse(parts, inverse):
    high_ref, low_ref = inverse
    rows, sides = parts[0].shape[0], []
    for part in parts:
        high = part.astype(bf16).astype(f32)
        both = jnp.concatenate([high, part - high], 0).astype(bf16)
        sides += [both[:, at : at + BLOCK] for at in range(0, part.shape[1], BLOCK)]
    blocks = range(len(sides))

    def times(ref, both, a, b):
        return dot(both, ref[place(a, b), :]) if a >= b else dot_turned(both, ref[place(b, a), :])

    solved = []
    for b in blocks:
        one = sum(times(high_ref, sides[a], a, b) for a in blocks)
        solved.append(one[:rows] + one[rows:])
    for b in blocks:
        solved[b] = solved[b] + sum(times(low_ref, sides[a], a, b) for a in blocks)[:rows]
    return jnp.concatenate(solved, 1)


def next_direction(parity_ref, parts, inverse, resid, scale, energy, factor):
    count = resid.shape[1]
    solved = coarse(parts, inverse)
    product = energy
    mine = solved[:, :count]
    for h, part in enumerate(parts):
        here = solved[:, h * count : (h + 1) * count]
        product = product + row_sum(part * here)
        if h:
            mine = jnp.where(parity_ref[0] == h, here, mine)
    return product, scale * resid + factor * mine


def first_kernel(
    factor, parity_ref, got_ref, high_ref, low_ref, resid_ref, scale_ref, dir_ref, send_ref, rho_ref, dots_ref
):
    count = resid_ref.shape[1]
    inverse = high_ref, low_ref
    parts, sums = gathered(got_ref, rho_ref.shape[1] // count, count)
    parts = [part * factor for part in parts]
    product, direction = next_direction(
        parity_ref, parts, inverse, resid_ref[...], scale_ref[...], sums[0], factor
    )
    dir_ref[...] = direction
    for p in range(send_ref.shape[0]):
        send_ref[p] = direction.astype(bf16)
    for h, part in enumerate(parts):
        rho_ref[:, h * count : (h + 1) * count] = part
    at = lax.broadcasted_iota(jnp.int32, dots_ref.shape, 1)
    dots_ref[...] = jnp.where(at == 0, sums[0], jnp.where(at == 1, product, 0.0))


def step_kernel(
    factor, parity_ref, got_ref, high_ref, low_ref, resid_ref, scale_ref, image_ref, old_ref, rho_ref, dots_ref, answer_ref,
    dir_ref, send_ref, new_rho_ref, new_dots_ref, new_resid_ref, new_answer_ref,
):
    count = resid_ref.shape[1]
    inverse = high_ref, low_ref
    parts, sums = gathered(got_ref, rho_ref.shape[1] // count, count)
    energy, product = lane(dots_ref[...], 0), lane(dots_ref[...], 1)
    alpha = product / sums[0]
    old = old_ref[...]
    new_answer_ref[...] = answer_ref[...] + alpha * old
    resid = resid_ref[...] - alpha * image_ref[...]
    new_resid_ref[...] = resid
    energy = energy - alpha * (2.0 * sums[1] - alpha * sums[2])
    parts = [
        rho_ref[:, h * count : (h + 1) * count] - alpha * (part * factor) for h, part in enumerate(parts)
    ]
    fresh, fine = next_direction(parity_ref, parts, inverse, resid, scale_ref[...], energy, factor)
    direction = fine + fresh / product * old
    dir_ref[...] = direction
    for p in range(send_ref.shape[0]):
        send_ref[p] = direction.astype(bf16)
    for h, part in enumerate(parts):
        new_rho_ref[:, h * count : (h + 1) * count] = part
    at = lax.broadcasted_iota(jnp.int32, dots_ref.shape, 1)
    new_dots_ref[...] = jnp.where(at == 0, energy, jnp.where(at == 1, fresh, 0.0))


def run_coarse(kernel, factor, n_dp, parity, *operands, more=0):
    rows, count = operands[3].shape
    vmem = pl.BlockSpec(memory_space=pltpu.VMEM)
    wide = jax.ShapeDtypeStruct((rows, count), f32)
    outs = [
        wide,
        jax.ShapeDtypeStruct((n_dp, rows, count), bf16),
        jax.ShapeDtypeStruct((rows, K), f32),
        jax.ShapeDtypeStruct((rows, SLOTS), f32),
    ] + [wide] * more
    return pl.pallas_call(
        functools.partial(kernel, factor),
        out_shape=outs,
        in_specs=[pl.BlockSpec(memory_space=pltpu.SMEM)] + [vmem] * len(operands),
        out_specs=[vmem] * len(outs),
        compiler_params=pltpu.CompilerParams(vmem_limit_bytes=50 * 1024 * 1024),
        cost_estimate=pl.CostEstimate(flops=10**8, bytes_accessed=5 * 2**20, transcendentals=0),
    )(parity, *operands)


def rounded(value):
    return lax.reduce_precision(value, 8, 7).astype(bf16)


def rounded(value):
    return lax.reduce_precision(value, 8, 7).astype(bf16)


def triple(value):
    high = lax.reduce_precision(value, 8, 7)
    mid = lax.reduce_precision(value - high, 8, 7)
    return jnp.stack([high, mid, value - high - mid], -1).astype(bf16)


def body(samples, projections, targets, feature_scale, coarse_factor):
    n_dp, n_sk = lax.axis_size(DP), lax.axis_size("sketch")
    count = projections.shape[2]
    width = targets.shape[1]
    mine = width // n_dp
    cols = width // n_sk
    factor = 1.0 / math.sqrt(F // K)
    halves = K // count
    n = samples.shape[0]
    scale = feature_scale[None, :]

    core = lax.axis_index("core").astype(jnp.int32).reshape(1)
    parity = (lax.axis_index("sketch") % halves).astype(jnp.int32).reshape(1)
    mine_proj = lax.all_to_all(repeat(projections, lax.axis_size("z")), "z", 0, 0)
    factor_high, factor_low, core, parity = coarse_factor_inverse(core, parity, coarse_factor)
    mine_proj, core = lax.optimization_barrier((mine_proj, core))
    other_proj = lax.ppermute(mine_proj, "core", [(0, 1), (1, 0)])
    feat, part = make_features(core, samples, mine_proj, other_proj, targets.T, n_dp)

    def scatter_dp(value):
        return lax.all_to_all(value, DP, 0, 0)

    def gather_sk(value):
        return lax.all_to_all(jnp.broadcast_to(value[None], (n_sk,) + value.shape), "sketch", 0, 0)

    def forward(send):
        whole = lax.all_to_all(send, DP, 0, 0)
        return whole, dot_turned(whole.reshape(width, count), feat)

    resid, sent = run_send(first_send_kernel, n_sk, scatter_dp(part), scale)
    inv_high, inv_low = coarse_inverse(factor_high, factor_low, resid)
    got = lax.all_to_all(sent, "sketch", 0, 0)
    direction, send, rho, dots = run_coarse(
        first_kernel, factor, n_dp, parity, got, inv_high, inv_low, resid, scale
    )
    answer = jnp.zeros_like(resid)
    for step in range(ITERS - 1):
        _, sums = forward(send)
        sums = lax.all_to_all(sums.astype(bf16).reshape(n_sk, cols, n), "sketch", 0, 0)
        u = rounded(jnp.sum(sums.astype(f32), 0))
        whole = gather_sk(u).reshape(width, n)
        parts = scatter_dp(dot(whole, feat).reshape(n_dp, mine, count))
        image, sent = run_send(step_send_kernel, n_sk, parts, scale, direction, resid)
        got = lax.all_to_all(sent, "sketch", 0, 0)
        direction, send, rho, dots, resid, answer = run_coarse(
            step_kernel, factor, n_dp, parity, got, inv_high, inv_low, resid, scale, image, direction, rho, dots, answer,
            more=2,
        )
    whole, sums = forward(send)
    got = lax.all_to_all(run_last_sums(n_sk, whole, sums), "sketch", 0, 0)
    sent = run_last_u(RIDGE / n_dp, got)
    got = lax.all_to_all(sent, "sketch", 0, 0).reshape(width, n + SLOTS)
    image = dot(got[:, :n], feat)
    sent = jnp.concatenate([image.astype(bf16), got[:, n:]], 1)
    got = lax.all_to_all(sent.reshape(n_dp, mine, count + SLOTS), DP, 0, 0)
    got = lax.all_to_all(run_last_step(got, direction, dots, answer, resid), DP, 0, 0)
    answer, resid = outputs(got)
    return answer.T, resid.T


def solution(mesh):
    chips = mesh.shape["dp"] // 2
    mesh = jax.sharding.Mesh(mesh.devices.reshape(chips, 2, -1), ("z", "core", "sketch"))
    placed = (P(DP, None), P(None, DP, "sketch"), P(DP, None), P("sketch"), P())
    return jax.shard_map(
        body,
        mesh=mesh,
        in_specs=placed,
        out_specs=(P("sketch", None), P("sketch", None)),
        check_vma=False,
    )
```
